32 devices in a mesh: dp: 8 (over y, x, core), fsdp: 4 (over z).
Axes of the slice: x: 2, y: 2, z: 4, core: 2. Of those that a mesh axis runs over, the one named last changes fastest.
Arguments:
- tokens: bfloat16 [8192, 2048], P(('dp', 'fsdp')), may hold values from -6 to 6
- text: bfloat16 [32, 128, 2048], P(('dp', 'fsdp')), may hold values from -6 to 6
- cotangent: bfloat16 [32, 128, 2048], P(('dp', 'fsdp')), may hold values from -6 to 6
- positions: int32 [32, 128], P(('dp', 'fsdp')), may hold values from 0 to 255, as said below
- text_lengths: int32 [32], P(('dp', 'fsdp')), may hold values from 1 to 128, as said below
- mask_embed: bfloat16 [2048], P(('dp', 'fsdp')), may hold values from -6 to 6
- gain_attn: bfloat16 [2048], P(('dp', 'fsdp')), may hold values from 0.099609375 to 1.8984375
- w_qkv: bfloat16 [2048, 6144], P(('dp', 'fsdp')), may hold values from -0.125 to 0.125
- w_attn_out: bfloat16 [2048, 2048], P(('dp', 'fsdp')), may hold values from -1 to 1
- gain_cross: bfloat16 [2048], P(('dp', 'fsdp')), may hold values from 0.099609375 to 1.8984375
- w_cross_q: bfloat16 [2048, 2048], P(('dp', 'fsdp')), may hold values from -0.125 to 0.125
- w_cross_kv: bfloat16 [2048, 4096], P(('dp', 'fsdp')), may hold values from -0.125 to 0.125
- w_cross_out: bfloat16 [2048, 2048], P(('dp', 'fsdp')), may hold values from -0.75 to 0.75
- gain_mlp: bfloat16 [2048], P(('dp', 'fsdp')), may hold values from 0.099609375 to 1.8984375
- w_up: bfloat16 [2048, 8192], P(('dp', 'fsdp')), may hold values from -0.125 to 0.125
- w_down: bfloat16 [8192, 2048], P(('dp', 'fsdp')), may hold values from -0.0625 to 0.0625
Outputs:
- output: bfloat16 [8192, 2048], P(('dp', 'fsdp'))
- grad_tokens: bfloat16 [8192, 2048], P(('dp', 'fsdp'))
- grad_text: bfloat16 [32, 128, 2048], P(('dp', 'fsdp'))
- grad_mask_embed: float32 [2048], P(('dp', 'fsdp'))
- grad_gain_attn: float32 [2048], P(('dp', 'fsdp'))
- grad_w_qkv: float32 [2048, 6144], P(('dp', 'fsdp'))
- grad_w_attn_out: float32 [2048, 2048], P(('dp', 'fsdp'))
- grad_gain_cross: float32 [2048], P(('dp', 'fsdp'))
- grad_w_cross_q: float32 [2048, 2048], P(('dp', 'fsdp'))
- grad_w_cross_kv: float32 [2048, 4096], P(('dp', 'fsdp'))
- grad_w_cross_out: float32 [2048, 2048], P(('dp', 'fsdp'))
- grad_gain_mlp: float32 [2048], P(('dp', 'fsdp'))
- grad_w_up: float32 [2048, 8192], P(('dp', 'fsdp'))
- grad_w_down: float32 [8192, 2048], P(('dp', 'fsdp'))
The draws below stay inside these ranges and needn't reach their ends.
Inputs may be any that keep to these rules, and one draw needn't show every extreme that they name: Each image's row holds 128 distinct positions. `text_lengths`: some image has all 128 text tokens valid.
All inputs are finite; a program needn't handle non-finite values.
Results may differ from the reference program's by a relative error of at most 0.02.
Values may be sent and summed in bfloat16 or wider, within the bound.
No kernel may reach another device: no remote copies, remote signals or barrier semaphores. Data moves between devices by JAX's collectives and lax.ppermute only.
A program may use at most 576 MiB of HBM per device.

```python
import math
import jax
import jax.numpy as jnp
from jax import lax

D = 2048
HEADS = 16
HDIM = 128
FF = 8192
SEQ = 256
TXT = 128
MASKED = 128
IMAGES = 32
TOKENS = 8192


def draw_positions(key, part):
    key = jax.random.fold_in(key, 11)
    subkeys = jax.random.split(key, IMAGES)

    def one_image(image_key):
        return jax.random.permutation(image_key, SEQ)[:MASKED]
    return jax.vmap(one_image)(subkeys).astype(jnp.int32)


def draw_text_lengths(key, part):
    key = jax.random.fold_in(key, 23)
    first_key, second_key = jax.random.split(key)
    lengths_drawn = jax.random.randint(first_key, (IMAGES,), 1, TXT + 1)
    chosen = jax.random.randint(second_key, (), 0, IMAGES)
    return lengths_drawn.at[chosen].set(TXT).astype(jnp.int32)


def steps_of(stream_key, shape, cuts, low, high):
    level, own = 1.0, jax.random.fold_in(stream_key, 6)
    for axis_at, shards_of in cuts:
        heights = jnp.exp(jax.random.uniform(jax.random.fold_in(own, axis_at), (shards_of,), jnp.float32, low / len(cuts), high / len(cuts)))
        level = level * jnp.repeat(heights, shape[axis_at] // shards_of).reshape([-1 if axis == axis_at else 1 for axis in range(len(shape))])
    return level


def bell_draw(stream_key, dims, scale, most, cuts=(), held_as=jnp.bfloat16):
    values = scale * jax.random.normal(stream_key, dims, jnp.float32)
    if cuts:
        values = values * steps_of(stream_key, dims, cuts, -0.22, 0.18)
    return jnp.clip(values, -most, most).astype(held_as)


def setup_inputs(seed: int = 0) -> dict:
    splits = jax.random.split(jax.random.key(seed), 17)
    tokens = bell_draw(splits[0], (TOKENS, D), 1.0, 6.0, ((0, 32),))
    text = bell_draw(splits[1], (IMAGES, TXT, D), 1.0, 6.0, ((0, 32),))
    cotangent = bell_draw(splits[2], (IMAGES, MASKED, D), 1.0, 6.0, ((0, 32),))
    positions = draw_positions(jax.random.fold_in(splits[16], 71), 0)
    text_lengths = draw_text_lengths(jax.random.fold_in(splits[16], 71), 0)
    mask_embed = bell_draw(splits[5], (D,), 1.0, 6.0, ((0, 32),))
    gain_attn = jnp.clip(1.0 + 0.18 * jax.random.normal(splits[6], (D,), jnp.float32), 0.099609375, 1.8984375).astype(jnp.bfloat16)
    w_qkv = bell_draw(splits[7], (D, 3 * D), D ** -0.5, 0.125, ((0, 32),))
    w_attn_out = bell_draw(splits[8], (D, D), (D // 64) ** -0.5, 1.0, ((0, 32),))
    gain_cross = jnp.clip(1.0 + 0.18 * jax.random.normal(splits[9], (D,), jnp.float32), 0.099609375, 1.8984375).astype(jnp.bfloat16)
    w_cross_q = bell_draw(splits[10], (D, D), D ** -0.5, 0.125, ((0, 32),))
    w_cross_kv = bell_draw(splits[11], (D, 2 * D), D ** -0.5, 0.125, ((0, 32),))
    w_cross_out = bell_draw(splits[12], (D, D), (D // 32) ** -0.5, 0.75, ((0, 32),))
    gain_mlp = jnp.clip(1.0 + 0.18 * jax.random.normal(splits[13], (D,), jnp.float32), 0.099609375, 1.8984375).astype(jnp.bfloat16)
    w_up = bell_draw(splits[14], (D, FF), D ** -0.5, 0.125, ((0, 32),))
    w_down = bell_draw(splits[15], (FF, D), FF ** -0.5, 0.0625, ((0, 32),))
    return {"tokens": tokens, "text": text, "cotangent": cotangent, "positions": positions, "text_lengths": text_lengths, "mask_embed": mask_embed, "gain_attn": gain_attn, "w_qkv": w_qkv, "w_attn_out": w_attn_out, "gain_cross": gain_cross, "w_cross_q": w_cross_q, "w_cross_kv": w_cross_kv, "w_cross_out": w_cross_out, "gain_mlp": gain_mlp, "w_up": w_up, "w_down": w_down}


PRECISE = lax.Precision.HIGHEST

@jax.custom_vjp
def low(v):
    return lax.optimization_barrier(v.astype(jnp.bfloat16)).astype(jnp.float32)

@jax.custom_vjp
def low_back(v):
    return v

def low_keep(v):
    return (low(v), None)

def low_pass(kept, grad):
    return (grad,)

def back_keep(v):
    return (v, None)

def back_low(kept, grad):
    return (low(grad),)
low.defvjp(low_keep, low_pass)
low_back.defvjp(back_keep, back_low)

def layer_norm(stream, gain_vec):
    centered = stream - lax.optimization_barrier(jnp.mean(stream, axis=-1, keepdims=True))
    return centered * lax.rsqrt(lax.optimization_barrier(jnp.mean(centered * centered, axis=-1, keepdims=True)) + 1e-05) * gain_vec

def project(left, right):
    return jnp.einsum('...d,de->...e', left, right, precision=PRECISE)

def split_heads(block):
    return block.reshape(block.shape[0], block.shape[1], HEADS, HDIM)

def attention(queries, key_heads, value_heads, text_valid):
    logits = low_back(jnp.einsum('bqhe,bkhe->bhqk', queries, key_heads, precision=PRECISE) * HDIM ** (-0.5))
    if text_valid is not None:
        logits = jnp.where(text_valid[:, None, None, :], logits, -1e+30)
    softmaxed = jax.nn.softmax(logits, axis=-1)
    mixture = jnp.einsum('bhqk,bkhe->bqhe', low(softmaxed), value_heads, precision=PRECISE)
    return mixture.reshape(mixture.shape[0], mixture.shape[1], D)

def group_forward(params, tokens_f, text_f, masked, text_valid):
    mask_embed, gain_attn, w_qkv, w_attn_out, gain_cross, w_cross_q, w_cross_kv, w_cross_out, gain_mlp, w_up, w_down = params
    start_rows = jnp.where(masked[..., None] > 0, mask_embed, tokens_f)
    entries = low(layer_norm(start_rows, gain_attn))
    packed = low(low_back(project(entries, w_qkv)))
    mixture = attention(split_heads(packed[..., :D]), split_heads(packed[..., D:2 * D]), split_heads(packed[..., 2 * D:]), None)
    mixture = low(low_back(mixture))
    after_attn = start_rows + low_back(project(mixture, w_attn_out))
    cross_entries = low(layer_norm(after_attn, gain_cross))
    cross_queries = low(low_back(project(cross_entries, w_cross_q)))
    text_pair = low(low_back(project(text_f, w_cross_kv)))
    cross_mix = attention(split_heads(cross_queries), split_heads(text_pair[..., :D]), split_heads(text_pair[..., D:]), text_valid)
    cross_mix = low(low_back(cross_mix))
    after_cross = after_attn + low_back(project(cross_mix, w_cross_out))
    mlp_entries = low(layer_norm(after_cross, gain_mlp))
    hidden_pre = low_back(project(mlp_entries, w_up))
    active = low(jax.nn.gelu(hidden_pre))
    return after_cross + low_back(project(active, w_down))

def reference(tokens, text, cotangent, positions, text_lengths, mask_embed, gain_attn, w_qkv, w_attn_out, gain_cross, w_cross_q, w_cross_kv, w_cross_out, gain_mlp, w_up, w_down):
    select = (positions[:, :, None] == jnp.arange(SEQ, dtype=jnp.int32)[None, None, :]).astype(jnp.float32)
    masked = lax.optimization_barrier(jnp.sum(select, axis=1))
    text_valid = jnp.arange(TXT, dtype=jnp.int32)[None, :] < text_lengths[:, None]
    params = tuple((weight_arr.astype(jnp.float32) for weight_arr in (mask_embed, gain_attn, w_qkv, w_attn_out, gain_cross, w_cross_q, w_cross_kv, w_cross_out, gain_mlp, w_up, w_down)))
    tokens_f = tokens.astype(jnp.float32).reshape(IMAGES, SEQ, D)
    text_f = text.astype(jnp.float32)
    group_size = math.gcd(IMAGES, 16)
    group_count = IMAGES // group_size
    masked_groups = masked.reshape(group_count, group_size, SEQ)
    valid_groups = text_valid.reshape(group_count, group_size, TXT)

    def run_all(params, tokens_f, text_f):

        def step_fn(carried, pieces):
            return (carried, jax.checkpoint(group_forward)(params, *pieces))
        scanned = (tokens_f.reshape(group_count, group_size, SEQ, D), text_f.reshape(group_count, group_size, TXT, D), masked_groups, valid_groups)
        carried, stacked = lax.scan(step_fn, jnp.zeros((), jnp.float32), scanned)
        return stacked.reshape(IMAGES, SEQ, D)
    result, backward = jax.vjp(run_all, params, tokens_f, text_f)
    image_index = jnp.arange(IMAGES, dtype=jnp.int32)[:, None]
    cot_full = jnp.zeros((IMAGES, SEQ, D), jnp.float32).at[image_index, positions.astype(jnp.int32)].set(cotangent.astype(jnp.float32))
    grad_params, grad_tokens, grad_text = backward(cot_full)
    return (result.reshape(TOKENS, D).astype(jnp.bfloat16), grad_tokens.reshape(TOKENS, D).astype(jnp.bfloat16), grad_text.astype(jnp.bfloat16), grad_params[0], grad_params[1], grad_params[2], grad_params[3], grad_params[4], grad_params[5], grad_params[6], grad_params[7], grad_params[8], grad_params[9], grad_params[10])
```

```python
import jax
import jax.numpy as jnp
from jax import lax
from jax.sharding import Mesh, PartitionSpec as P

HEADS = 16
HDIM = 128
PAD = 16
BF = jnp.bfloat16
F32 = jnp.float32


def dot(left, right):
    return jnp.dot(left, right, preferred_element_type=F32)


def dot_t(left, right):
    return lax.dot_general(left, right, (((1,), (1,)), ((), ())), preferred_element_type=F32)


def dot_sum(left, right):
    return lax.dot_general(left, right, (((0,), (0,)), ((), ())), preferred_element_type=F32)


def normed(rows):
    centered = rows - jnp.mean(rows, axis=-1, keepdims=True)
    scale = lax.rsqrt(jnp.mean(centered * centered, axis=-1, keepdims=True) + 1e-05)
    return centered * scale, scale


def norm_back(grad, field, scale):
    return scale * (
        grad
        - jnp.mean(grad, axis=-1, keepdims=True)
        - field * jnp.mean(grad * field, axis=-1, keepdims=True)
    )


def xor_order(stack, me, size):
    bit = 1
    while bit < size:
        split = stack.reshape((size // (2 * bit), 2, bit) + stack.shape[1:])
        stack = jnp.where((me & bit) != 0, split[:, ::-1], split).reshape(stack.shape)
        bit *= 2
    return stack


def bits_of(size):
    return [1 << k for k in range(size.bit_length() - 1)]


class Layer:
    def __init__(self, tp, planes):
        self.tp, self.planes = tp, planes
        self.t, self.c, self.z = (lax.axis_index(a) for a in ("tp", "core", "fsdp"))


    def hop(self, value, j):
        return lax.ppermute(value, "tp", [(i, i ^ j) for i in range(self.tp)])

    def other_core(self, value):
        return lax.ppermute(value, "core", [(0, 1), (1, 0)])

    def other_plane(self, value, k):
        return lax.ppermute(value, "fsdp", [(i, i ^ k) for i in range(self.planes)])

    def spread(self, value, bits):
        held = {0: value}
        for bit in bits:
            held.update({j | bit: self.hop(v, bit) for j, v in list(held.items())})
        return [held[j] for j in range(self.tp)]

    def gather_tp(self, halves):
        bits = bits_of(self.tp)
        left, right = self.spread(halves[0], bits), self.spread(halves[1], bits[::-1])
        return left, right

    def collect(self, parts, bits):
        held = dict(enumerate(parts))
        for bit in bits[::-1]:
            for j in [j for j in held if not j & bit]:
                came = self.hop(held[j | bit].astype(BF), bit)
                held[j] = held[j] + came.astype(F32)
                del held[j | bit]
        return held[0]

    def scatter_tp(self, partial):
        half = partial.shape[2] // 2
        bits = bits_of(self.tp)
        left = self.collect([partial[j, :, :half] for j in range(self.tp)], bits)
        right = self.collect([partial[j, :, half:] for j in range(self.tp)], bits[::-1])
        return jnp.concatenate([left, right], axis=1)

    def tp_direct(self, value):
        return jnp.stack([value] + [self.hop(value, j) for j in range(1, self.tp)])

    def tp_sum(self, value):
        total = value
        for j in range(1, self.tp):
            came = self.hop(value, j)
            total = total + jnp.stack([came[i ^ j] for i in range(self.tp)])
        return total

    def to_owner(self, stack):
        return jnp.stack([stack[0]] + [self.hop(stack[j], j) for j in range(1, self.tp)])

    def gather_cz(self, value):
        planes = jnp.stack([value] + [self.other_plane(value, k) for k in range(1, self.planes)])
        return jnp.concatenate([planes, self.other_core(planes)])


    def swap_halves(self, value):
        half = value.shape[-1] // 2
        turned = jnp.concatenate([value[..., half:], value[..., :half]], axis=-1)
        return jnp.where(self.c == 0, value, turned)

    def own_halves(self, value):
        split = value.reshape(value.shape[:-1] + (self.tp, 2, -1))
        first, second = split[..., 0, :], split[..., 1, :]
        shape = value.shape[:-1] + (value.shape[-1] // 2,)
        return (
            jnp.where(self.c == 0, first, second).reshape(shape),
            jnp.where(self.c == 0, second, first).reshape(shape),
        )

    def natural(self, value):
        split = value.reshape(value.shape[:-1] + (2, self.tp, -1))
        first, second = split[..., 0, :, :], split[..., 1, :, :]
        both = jnp.stack(
            [jnp.where(self.c == 0, first, second), jnp.where(self.c == 0, second, first)], axis=-2
        )
        return both.reshape(value.shape)


    def rings(self, block):
        lead, rows, n = block.shape
        held = jnp.zeros((2, lead, self.planes, rows, n), block.dtype)
        for k in range(self.planes):
            if k:
                block = lax.ppermute(
                    block, "fsdp", [(i, (i + 1) % self.planes) for i in range(self.planes)]
                )
            at = lax.rem(self.z + self.planes - k, self.planes)
            held = lax.dynamic_update_slice(held, block[None, :, None], (0, 0, at, 0, 0))
            held = lax.dynamic_update_slice(
                held, self.other_core(block)[None, :, None], (1, 0, at, 0, 0)
            )
        return held

    def shuffle(self, shard, blocks):
        rows = shard.shape[0]
        split = shard.reshape(rows, blocks, self.tp, -1).transpose(2, 0, 1, 3)
        return lax.all_to_all(split.reshape(self.tp, rows, -1), "tp", 0, 0, tiled=True)

    def by_columns(self, shuffled):
        return self.rings(shuffled).reshape(-1, shuffled.shape[2])

    def by_rows(self, shard):
        return self.rings(shard[None]).reshape(-1, shard.shape[1])


def attend(queries, key_heads, value_heads, bias):
    logits = jnp.einsum("bqhe,bkhe->bhqk", queries, key_heads, preferred_element_type=F32)
    probs = jax.nn.softmax(logits * HDIM ** (-0.5) + bias[:, None, None, :], axis=-1)
    mixture = jnp.einsum(
        "bhqk,bkhe->bqhe", probs.astype(BF), value_heads, preferred_element_type=F32
    )
    return probs, mixture.astype(BF)


def attend_back(queries, key_heads, value_heads, probs, grad_mix):
    grad_probs = jnp.einsum("bhe,bkhe->bhk", grad_mix, value_heads, preferred_element_type=F32)
    grad_scores = probs * (grad_probs - jnp.sum(grad_probs * probs, axis=-1, keepdims=True))
    grad_scores = grad_scores.astype(BF)
    grad_query = jnp.einsum("bhk,bkhe->bhe", grad_scores, key_heads, preferred_element_type=F32)
    return grad_scores, grad_query * HDIM ** (-0.5)


def head_blocks(rows, local):
    images = rows.shape[0]
    spread = rows.reshape(images, 1, local, HDIM) * jnp.eye(local, dtype=rows.dtype)[None, :, :, None]
    return spread.reshape(images * local, local * HDIM)


def shards(
    tp,
    planes,
    tokens,
    text,
    cotangent,
    positions,
    text_lengths,
    mask_embed,
    gain_attn,
    w_qkv,
    w_attn_out,
    gain_cross,
    w_cross_q,
    w_cross_kv,
    w_cross_out,
    gain_mlp,
    w_up,
    w_down,
):
    me = Layer(tp, planes)
    seq, width = tokens.shape
    masked_count = positions.shape[1]
    free = seq - masked_count
    txt = text.shape[1]
    local = HEADS // tp
    rows = free + PAD
    device = (me.t * 2 + me.c) * planes + me.z
    world = tp * 2 * planes
    own = width // world
    scale = HDIM ** (-0.5)

    qkv_rel = me.by_columns(me.shuffle(w_qkv, 3))
    out_rel = me.by_rows(w_attn_out)
    kv_rel = me.by_columns(me.shuffle(w_cross_kv, 2))
    cq_rel = me.by_columns(me.shuffle(w_cross_q, 1))
    cout_rel = me.by_rows(w_cross_out)
    up_rel = me.by_columns(me.shuffle(w_up, 1))
    down_rel = me.by_rows(w_down)

    vectors = jnp.stack([mask_embed, gain_attn, gain_cross, gain_mlp])
    vectors = me.tp_direct(me.gather_cz(vectors)).reshape(world, 4, own)
    vectors = xor_order(vectors, device, world)
    vectors = vectors.transpose(1, 0, 2).reshape(4, width).astype(F32)
    embed, gain_a, gain_c, gain_m = vectors[0], vectors[1], vectors[2], vectors[3]

    spots = lax.broadcasted_iota(jnp.int32, (masked_count, seq), 1)
    masked = jnp.sum((positions[0][:, None] == spots).astype(F32), axis=0)
    below = lax.broadcasted_iota(jnp.int32, (seq, seq), 0) <= lax.broadcasted_iota(
        jnp.int32, (seq, seq), 1
    )
    rank = dot((1.0 - masked).astype(BF)[None, :], below.astype(BF))[0]
    ranks = lax.broadcasted_iota(jnp.int32, (free, seq), 0).astype(F32) + 1.0
    pick = ((rank[None, :] == ranks) & (masked[None, :] == 0.0)).astype(BF)
    place = jnp.concatenate(
        [pick.T, masked[:, None].astype(BF), jnp.zeros((seq, PAD - 1), BF)], axis=1
    )
    start_free = dot(pick, tokens)
    start = jnp.concatenate([start_free, jnp.broadcast_to(embed[None], (PAD, width))])

    cot_sum = jnp.sum(cotangent[0].astype(F32), axis=0)
    cot_all = lax.all_gather(cot_sum[None], ("core", "fsdp"), axis=0, tiled=True)
    cot_group = me.tp_direct(cot_sum[None])[:, 0]
    cot_high = cot_group.astype(BF)

    cot_all = me.tp_direct(cot_all)
    cot_rows = cot_all.reshape(world, width)
    high = cot_rows.astype(BF)
    low = (cot_rows - high.astype(F32)).astype(BF)
    through = dot_t(jnp.concatenate([high, low]), w_down)
    through = through[:world] + through[world:]
    through = through.reshape(tp, 2 * planes, -1).transpose(1, 0, 2)
    through = lax.all_to_all(through, ("core", "fsdp"), 0, 0, tiled=True)
    grad_active = through.transpose(1, 0, 2).reshape(tp, -1)

    text_left, text_right = me.gather_tp(me.own_halves(text[0]))
    text_rows = jnp.concatenate(
        [jnp.concatenate(text_left), jnp.concatenate(text_right)], axis=1
    )
    open_text = lax.broadcasted_iota(jnp.int32, (1, txt), 1) < text_lengths[:, None]
    text_bias = jnp.where(me.tp_direct(open_text.astype(F32))[:, 0] > 0, 0.0, -1e30)

    field_a, scale_a = normed(start)
    entries = (field_a * gain_a[None]).astype(BF)
    ent_left, ent_right = me.own_halves(entries)
    got_left, got_right = me.gather_tp((ent_left[:free], ent_right[:free]))
    ent_rows = jnp.concatenate(
        [
            jnp.concatenate(got_left + [ent_left[free:]]),
            jnp.concatenate(got_right + [ent_right[free:]]),
        ],
        axis=1,
    )
    packed = dot(ent_rows, qkv_rel).astype(BF)
    packed_free = packed[: tp * free].reshape(tp, free, 3, local, HDIM)
    packed_masked = packed[tp * free :].reshape(1, PAD, 3, local, HDIM)
    packed = jnp.concatenate(
        [packed_free, jnp.broadcast_to(packed_masked, (tp,) + packed_masked.shape[1:])], axis=1
    )
    queries, key_heads, value_heads = packed[:, :, 0], packed[:, :, 1], packed[:, :, 2]
    spot = lax.broadcasted_iota(jnp.int32, (1, rows), 1)
    key_bias = jnp.where(
        spot < free, 0.0, jnp.where(spot == free, jnp.log(float(masked_count)), -1e30)
    )
    probs, mixture = attend(queries, key_heads, value_heads, key_bias)
    mixture = mixture.reshape(tp, rows, local * HDIM)
    added = dot(me.swap_halves(mixture).reshape(tp * rows, -1), out_rel)
    after_attn = start + me.scatter_tp(added.reshape(tp, rows, width))

    field_c, scale_c = normed(after_attn)
    cross_entries = (field_c * gain_c[None]).astype(BF)
    got_left, got_right = me.gather_tp(me.own_halves(cross_entries))
    cross_rows = jnp.concatenate([jnp.concatenate(got_left), jnp.concatenate(got_right)], axis=1)
    cross_queries = dot(cross_rows, cq_rel).astype(BF).reshape(tp, rows, local, HDIM)
    pair = dot(text_rows, kv_rel).astype(BF).reshape(tp, txt, 2, local, HDIM)
    text_keys, text_values = pair[:, :, 0], pair[:, :, 1]
    cross_probs, cross_mix = attend(cross_queries, text_keys, text_values, text_bias)
    cross_mix = cross_mix.reshape(tp, rows, local * HDIM)
    added = dot(me.swap_halves(cross_mix).reshape(tp * rows, -1), cout_rel)
    after_cross = after_attn + me.scatter_tp(added.reshape(tp, rows, width))

    field_m, scale_m = normed(after_cross)
    mlp_entries = (field_m * gain_m[None]).astype(BF)
    got_left, got_right = me.gather_tp(me.own_halves(mlp_entries))
    mlp_rows = jnp.concatenate([jnp.concatenate(got_left), jnp.concatenate(got_right)], axis=1)
    hidden = dot(mlp_rows, up_rel)
    active = jax.nn.gelu(hidden).astype(BF)
    added = dot(me.swap_halves(active), down_rel)
    output = after_cross + me.scatter_tp(added.reshape(tp, rows, width))
    output = dot(place, output.astype(BF)).astype(BF)

    field_c1, scale_c1 = normed(me.tp_direct(after_attn[free]))
    field_m1, scale_m1 = normed(me.tp_direct(after_cross[free]))

    hidden_one = hidden.reshape(tp, rows, -1)[:, free]
    active_one, gelu_back = jax.vjp(jax.nn.gelu, hidden_one)
    active_one = active_one.astype(BF)
    grad_pre = gelu_back(grad_active)[0].astype(BF)
    grad_entry = me.natural(me.tp_sum(dot_t(grad_pre, up_rel)))
    grad_gain_m = grad_entry[0] * field_m1[0]
    grad_mid = cot_group + norm_back(grad_entry * gain_m[None], field_m1, scale_m1)
    low_mid = grad_mid.astype(BF)

    grad_cmix = me.swap_halves(dot_t(low_mid, cout_rel)).astype(BF)
    query_one = cross_queries[:, free]
    cross_probs_one = cross_probs[:, :, free]
    grad_scores, grad_cq = attend_back(
        query_one, text_keys, text_values, cross_probs_one, grad_cmix.reshape(tp, local, HDIM)
    )
    grad_cq = grad_cq.reshape(tp, -1).astype(BF)
    query_one = query_one.reshape(tp, -1)
    grad_entry = me.natural(me.tp_sum(dot_t(grad_cq, cq_rel)))
    grad_gain_c = grad_entry[0] * field_c1[0]
    grad_attn = grad_mid + norm_back(grad_entry * gain_c[None], field_c1, scale_c1)
    low_attn = grad_attn.astype(BF)

    heads_back = jnp.concatenate(
        [
            jnp.pad(head_blocks(query_one, local), ((0, 0), (0, local * HDIM))),
            jnp.pad(head_blocks(grad_cmix, local), ((0, 0), (local * HDIM, 0))),
        ]
    )
    rows_back = dot_t(heads_back, kv_rel).reshape(2, tp, local, width)
    rows_back = jnp.stack([rows_back[0] * scale, rows_back[1]], axis=1).astype(BF)
    weighs = jnp.stack([grad_scores, cross_probs_one.astype(BF)], axis=1)
    sent = jnp.concatenate([rows_back, weighs], axis=-1).reshape(tp, 2 * local, width + txt)
    sent = me.to_owner(sent)
    weighs = sent[:, :, width:].reshape(tp * 2 * local, txt)
    rows_back = me.natural(sent[:, :, :width].reshape(tp * 2 * local, width))
    grad_text = dot_sum(weighs, rows_back).astype(BF)
    weighs = xor_order(sent[:, :, width:], me.t, tp).reshape(tp * 2 * local, txt)
    left_text = dot(weighs, text[0]).astype(BF)
    lefts = jnp.concatenate(
        [left_text, cross_entries[free : free + 1], mlp_entries[free : free + 1]]
    )
    lefts = lefts.reshape(-1, world, own).transpose(1, 0, 2)
    lefts = lax.all_to_all(lefts, ("tp", "core", "fsdp"), 0, 0, tiled=True)

    grad_amix = me.swap_halves(dot_t(low_attn, out_rel)).astype(BF)
    attn_scores, grad_q = attend_back(
        queries[:, free],
        key_heads,
        value_heads,
        probs[:, :, free],
        grad_amix.reshape(tp, local, HDIM),
    )
    grad_q = grad_q.reshape(tp, -1).astype(BF)
    span = local * HDIM
    query_zero = queries[0, free].reshape(1, -1)
    heads_back = jnp.concatenate(
        [
            jnp.pad(head_blocks(grad_amix, local), ((0, 0), (2 * span, 0))),
            jnp.pad(head_blocks(query_zero, local), ((0, 0), (span, span))),
            jnp.pad(grad_q, ((0, 0), (0, 2 * span))),
        ]
    )
    rows_back = dot_t(heads_back, qkv_rel)
    value_rows = rows_back[: tp * local].reshape(tp, local, width)
    key_rows = rows_back[tp * local : tp * local + local] * scale
    query_rows = rows_back[tp * local + local :].reshape(tp, 1, width)
    rows_back = jnp.concatenate(
        [jnp.broadcast_to(key_rows[None], (tp, local, width)), value_rows, query_rows], axis=1
    ).astype(BF)
    weighs = jnp.concatenate([attn_scores, probs[:, :, free].astype(BF)], axis=1)
    only = (lax.broadcasted_iota(jnp.int32, (tp, 1, rows), 2) == free).astype(BF)
    weighs = jnp.concatenate([weighs, only], axis=1)
    sent = me.to_owner(jnp.concatenate([rows_back, weighs], axis=-1))
    count = 2 * local + 1
    weighs = sent[:, :, width:].reshape(tp * count, rows)
    rows_back = me.natural(sent[:, :, :width].reshape(tp * count, width))
    grad_entry = dot_sum(weighs, rows_back)
    weighs = xor_order(sent[:, : 2 * local, width:], me.t, tp).reshape(tp * 2 * local, rows)
    left_attn = dot(weighs, entries)
    grad_gain_a = jnp.sum(grad_entry * field_a, axis=0)
    grad_start = norm_back(grad_entry * gain_a[None], field_a, scale_a)
    grad_embed = grad_attn[0] + grad_start[free]
    grad_tokens = dot(place[:, :free], grad_start[:free].astype(BF)).astype(BF)
    summed = jnp.stack([grad_embed, grad_gain_a, grad_gain_c, grad_gain_m])
    lefts2 = jnp.concatenate([left_attn, summed]).astype(BF)
    lefts2 = lefts2.reshape(-1, world, own).transpose(1, 0, 2)
    lefts2 = lax.all_to_all(lefts2, ("tp", "core", "fsdp"), 0, 0, tiled=True)

    mixed_one = mixture[:, free]
    cross_one = cross_mix[:, free]
    by_group = me.gather_cz(
        jnp.concatenate([mixed_one, cross_one, active_one, cot_high, low_mid, low_attn], axis=1)
    )
    by_group = by_group.reshape(world, -1)
    ff = active_one.shape[1]
    cuts = [span, 2 * span, 2 * span + ff, 2 * span + ff + width, 2 * span + ff + 2 * width]
    mixed_all, cross_all, active_all, cot_f, mid_f, attn_f = jnp.split(by_group, cuts, axis=1)
    corner = me.c * planes + me.z

    def mine(stack):
        size = stack.shape[1] // (2 * planes)
        return lax.dynamic_slice_in_dim(stack, corner * size, size, axis=1)

    grad_w_out = dot_sum(mine(mixed_all), attn_f)
    grad_w_cout = dot_sum(mine(cross_all), mid_f)
    grad_w_down = dot_sum(mine(active_all), cot_f)

    by_column = me.gather_cz(
        jnp.concatenate([grad_pre, grad_cq, query_one, grad_cmix, grad_amix, grad_q], axis=1)
    )
    query_wide = me.tp_direct(query_zero)
    pieces = []
    for j in range(tp):
        came = me.hop(by_column, j) if j else by_column
        came = jnp.stack([came[:, i ^ j] for i in range(tp)], axis=1)
        pieces.append(came.reshape(world, -1))
    by_column = xor_order(jnp.stack(pieces), me.t, tp)
    query_wide = xor_order(query_wide, me.t, tp).reshape(HEADS, HDIM)

    def columns(start_at, size):
        return by_column[:, :, start_at : start_at + size]

    def flat(part):
        return part.transpose(1, 0, 2).reshape(world, -1)

    pre_f = flat(columns(0, ff))
    cq_f = flat(columns(ff, span))
    query_f = flat(columns(ff + span, span)).reshape(world, HEADS, HDIM)
    cmix_f = flat(columns(ff + 2 * span, span)).reshape(world, HEADS, HDIM)
    amix_f = flat(columns(ff + 3 * span, span)).reshape(world, HEADS, HDIM)
    q_f = flat(columns(ff + 4 * span, span))

    def image_order(stack):
        ordered = xor_order(stack, device, world)
        ordered = ordered.reshape((tp, 2 * planes) + stack.shape[1:])
        return ordered.swapaxes(0, 1).reshape(stack.shape)

    lefts = image_order(lefts)
    text_left = lefts[:, : 2 * HEADS].reshape(world, tp, 2, local, own)
    text_left = text_left.transpose(2, 0, 1, 3, 4).reshape(2, world, HEADS, own)
    grad_w_cq = dot_sum(lefts[:, 2 * HEADS], cq_f)
    grad_w_up = dot_sum(lefts[:, 2 * HEADS + 1], pre_f)

    def by_head(left, right):
        outer = jnp.einsum("ihr,ihe->hre", left, right, preferred_element_type=F32)
        return outer.transpose(1, 0, 2).reshape(own, width)

    grad_w_kv = jnp.concatenate(
        [by_head(text_left[0], query_f) * scale, by_head(text_left[1], cmix_f)], axis=1
    )
    attn_left = image_order(lefts2[:, : 2 * HEADS]).reshape(world, tp, 2, local, own)
    attn_left = attn_left.transpose(2, 0, 1, 3, 4).reshape(2, world, HEADS, own)
    key_left = jnp.sum(attn_left[0].astype(F32), axis=0)
    entry_own = lax.dynamic_slice_in_dim(entries[free], device * own, own).astype(F32)
    query_sum = jnp.sum(q_f.astype(F32), axis=0)
    grad_k = key_left[:, :, None] * query_wide.astype(F32)[:, None, :] * scale
    grad_w_qkv = jnp.concatenate(
        [
            entry_own[:, None] * query_sum[None, :],
            grad_k.transpose(1, 0, 2).reshape(own, width),
            by_head(attn_left[1], amix_f),
        ],
        axis=1,
    )
    summed = jnp.sum(lefts2[:, 2 * HEADS :].astype(F32), axis=0)
    return (
        output,
        grad_tokens,
        grad_text[None],
        summed[0],
        summed[1],
        grad_w_qkv,
        grad_w_out,
        summed[2],
        grad_w_cq,
        grad_w_kv,
        grad_w_cout,
        summed[3],
        grad_w_up,
        grad_w_down,
    )


def solution(mesh):
    tp, planes = mesh.shape["dp"] // 2, mesh.shape["fsdp"]
    fine = Mesh(mesh.devices.reshape(tp, 2, planes), ("tp", "core", "fsdp"))
    every = ("tp", "core", "fsdp")
    one, two, three = P(every), P(every, None), P(every, None, None)

    def layer(*arguments):
        return shards(tp, planes, *arguments)

    return jax.shard_map(
        layer,
        mesh=fine,
        in_specs=(two, three, three, two, one, one, one, two, two, one, two, two, two, one, two, two),
        out_specs=(two, two, three, one, one, two, two, one, two, two, two, one, two, two),
        check_vma=False,
    )
```

```python
import jax
import jax.numpy as jnp
from jax import lax
from jax.sharding import Mesh, PartitionSpec as P

HEADS = 16
HDIM = 128
PAD = 16
BF = jnp.bfloat16
F32 = jnp.float32


def dot(left, right):
    return jnp.dot(left, right, preferred_element_type=F32)


def dot_t(left, right):
    return lax.dot_general(left, right, (((1,), (1,)), ((), ())), preferred_element_type=F32)


def dot_sum(left, right):
    return lax.dot_general(left, right, (((0,), (0,)), ((), ())), preferred_element_type=F32)


def normed(rows):
    centered = rows - jnp.mean(rows, axis=-1, keepdims=True)
    scale = lax.rsqrt(jnp.mean(centered * centered, axis=-1, keepdims=True) + 1e-05)
    return centered * scale, scale


def norm_back(grad, field, scale):
    return scale * (
        grad
        - jnp.mean(grad, axis=-1, keepdims=True)
        - field * jnp.mean(grad * field, axis=-1, keepdims=True)
    )


def xor_order(stack, me, size):
    bit = 1
    while bit < size:
        split = stack.reshape((size // (2 * bit), 2, bit) + stack.shape[1:])
        turned = jnp.concatenate([split[:, 1:], split[:, :1]], axis=1)
        stack = jnp.where((me & bit) != 0, turned, split).reshape(stack.shape)
        bit *= 2
    return stack


def bits_of(size):
    return [1 << k for k in range(size.bit_length() - 1)]


class Layer:
    def __init__(self, tp, planes):
        self.tp, self.planes = tp, planes
        self.t, self.c, self.z = (lax.axis_index(a) for a in ("tp", "core", "fsdp"))


    def hop(self, value, j):
        return lax.ppermute(value, "tp", [(i, i ^ j) for i in range(self.tp)])

    def other_core(self, value):
        return lax.ppermute(value, "core", [(0, 1), (1, 0)])

    def other_plane(self, value, k):
        return lax.ppermute(value, "fsdp", [(i, i ^ k) for i in range(self.planes)])

    def spread(self, value):
        return [value] + [self.hop(value, j) for j in range(1, self.tp)]

    def collect(self, partial):
        total = partial[0]
        low = partial.astype(BF)
        for j in range(1, self.tp):
            total = total + self.hop(low[j], j).astype(F32)
        return total

    def tp_direct(self, value):
        return jnp.stack([value] + [self.hop(value, j) for j in range(1, self.tp)])

    def tp_sum(self, value):
        total = value
        for j in range(1, self.tp):
            came = self.hop(value, j)
            total = total + jnp.stack([came[i ^ j] for i in range(self.tp)])
        return total

    def to_owner(self, stack):
        return jnp.stack([stack[0]] + [self.hop(stack[j], j) for j in range(1, self.tp)])

    def gather_cz(self, value):
        planes = jnp.stack([value] + [self.other_plane(value, k) for k in range(1, self.planes)])
        return jnp.concatenate([planes, self.other_core(planes)])


    def shuffle(self, shard, blocks):
        rows = shard.shape[0]
        split = shard.reshape(rows, blocks, self.tp, -1).transpose(2, 0, 1, 3)
        return lax.all_to_all(split.reshape(self.tp, rows, -1), "tp", 0, 0, tiled=True)

    def by_columns(self, shuffled):
        whole = lax.all_gather(shuffled, ("core", "fsdp"), axis=1, tiled=True)
        return whole.reshape(-1, shuffled.shape[2])

    def by_rows(self, shard):
        return lax.all_gather(shard, ("core", "fsdp"), axis=0, tiled=True)


def attend(queries, key_heads, value_heads, bias):
    logits = jnp.einsum("bqhe,bkhe->bhqk", queries, key_heads, preferred_element_type=F32)
    probs = jax.nn.softmax(logits * HDIM ** (-0.5) + bias[:, None, None, :], axis=-1)
    mixture = jnp.einsum(
        "bhqk,bkhe->bqhe", probs.astype(BF), value_heads, preferred_element_type=F32
    )
    return probs, mixture.astype(BF)


def attend_back(queries, key_heads, value_heads, probs, grad_mix):
    grad_probs = jnp.einsum("bhe,bkhe->bhk", grad_mix, value_heads, preferred_element_type=F32)
    grad_scores = probs * (grad_probs - jnp.sum(grad_probs * probs, axis=-1, keepdims=True))
    grad_scores = grad_scores.astype(BF)
    grad_query = jnp.einsum("bhk,bkhe->bhe", grad_scores, key_heads, preferred_element_type=F32)
    return grad_scores, grad_query * HDIM ** (-0.5)


def head_blocks(rows, local):
    images = rows.shape[0]
    spread = rows.reshape(images, 1, local, HDIM) * jnp.eye(local, dtype=rows.dtype)[None, :, :, None]
    return spread.reshape(images * local, local * HDIM)


def shards(
    tp,
    planes,
    tokens,
    text,
    cotangent,
    positions,
    text_lengths,
    mask_embed,
    gain_attn,
    w_qkv,
    w_attn_out,
    gain_cross,
    w_cross_q,
    w_cross_kv,
    w_cross_out,
    gain_mlp,
    w_up,
    w_down,
):
    me = Layer(tp, planes)
    seq, width = tokens.shape
    masked_count = positions.shape[1]
    free = seq - masked_count
    txt = text.shape[1]
    local = HEADS // tp
    rows = free + PAD
    device = (me.t * 2 + me.c) * planes + me.z
    world = tp * 2 * planes
    own = width // world
    scale = HDIM ** (-0.5)

    qkv = me.by_columns(me.shuffle(w_qkv, 3))
    out_w = me.by_rows(w_attn_out)
    kv = me.by_columns(me.shuffle(w_cross_kv, 2))
    cq = me.by_columns(me.shuffle(w_cross_q, 1))
    cout = me.by_rows(w_cross_out)
    up = me.by_columns(me.shuffle(w_up, 1))
    down = me.by_rows(w_down)

    vectors = jnp.stack([mask_embed, gain_attn, gain_cross, gain_mlp])
    vectors = me.tp_direct(me.gather_cz(vectors)).reshape(world, 4, own)
    vectors = xor_order(vectors, device, world)
    vectors = vectors.transpose(1, 0, 2).reshape(4, width).astype(F32)
    embed, gain_a, gain_c, gain_m = vectors[0], vectors[1], vectors[2], vectors[3]

    spots = lax.broadcasted_iota(jnp.int32, (masked_count, seq), 1)
    masked = jnp.sum((positions[0][:, None] == spots).astype(F32), axis=0)
    below = lax.broadcasted_iota(jnp.int32, (seq, seq), 0) <= lax.broadcasted_iota(
        jnp.int32, (seq, seq), 1
    )
    rank = dot((1.0 - masked).astype(BF)[None, :], below.astype(BF))[0]
    ranks = lax.broadcasted_iota(jnp.int32, (free, seq), 0).astype(F32) + 1.0
    pick = ((rank[None, :] == ranks) & (masked[None, :] == 0.0)).astype(BF)
    place = jnp.concatenate(
        [pick.T, masked[:, None].astype(BF), jnp.zeros((seq, PAD - 1), BF)], axis=1
    )
    start_free = dot(pick, tokens)
    start = jnp.concatenate([start_free, jnp.broadcast_to(embed[None], (PAD, width))])

    cot_sum = jnp.sum(cotangent[0].astype(F32), axis=0)
    cot_all = xor_order(me.gather_cz(cot_sum), me.c * planes + me.z, 2 * planes)
    cot_group = me.tp_direct(cot_sum[None])[:, 0]
    cot_high = cot_group.astype(BF)

    cot_all = me.tp_direct(cot_all)
    cot_rows = cot_all.reshape(world, width)
    high = cot_rows.astype(BF)
    low = (cot_rows - high.astype(F32)).astype(BF)
    through = dot_t(jnp.concatenate([high, low]), w_down)
    through = through[:world] + through[world:]
    through = through.reshape(tp, 2 * planes, -1).transpose(1, 0, 2)
    through = lax.all_to_all(through, ("core", "fsdp"), 0, 0, tiled=True)
    grad_active = through.transpose(1, 0, 2).reshape(tp, -1)

    text_rows = jnp.concatenate(me.spread(text[0]))
    open_text = lax.broadcasted_iota(jnp.int32, (1, txt), 1) < text_lengths[:, None]
    text_bias = jnp.where(me.tp_direct(open_text.astype(F32))[:, 0] > 0, 0.0, -1e30)

    field_a, scale_a = normed(start)
    entries = (field_a * gain_a[None]).astype(BF)
    ent_rows = jnp.concatenate(me.spread(entries[:free]) + [entries[free:]])
    packed = dot(ent_rows, qkv).astype(BF)
    packed_free = packed[: tp * free].reshape(tp, free, 3, local, HDIM)
    packed_masked = packed[tp * free :].reshape(1, PAD, 3, local, HDIM)
    packed = jnp.concatenate(
        [packed_free, jnp.broadcast_to(packed_masked, (tp,) + packed_masked.shape[1:])], axis=1
    )
    queries, key_heads, value_heads = packed[:, :, 0], packed[:, :, 1], packed[:, :, 2]
    spot = lax.broadcasted_iota(jnp.int32, (1, rows), 1)
    key_bias = jnp.where(
        spot < free, 0.0, jnp.where(spot == free, jnp.log(float(masked_count)), -1e30)
    )
    probs, mixture = attend(queries, key_heads, value_heads, key_bias)
    mixture = mixture.reshape(tp, rows, local * HDIM)
    added = dot(mixture.reshape(tp * rows, -1), out_w)
    after_attn = start + me.collect(added.reshape(tp, rows, width))

    field_c, scale_c = normed(after_attn)
    cross_entries = (field_c * gain_c[None]).astype(BF)
    cross_rows = jnp.concatenate(me.spread(cross_entries))
    cross_queries = dot(cross_rows, cq).astype(BF).reshape(tp, rows, local, HDIM)
    pair = dot(text_rows, kv).astype(BF).reshape(tp, txt, 2, local, HDIM)
    text_keys, text_values = pair[:, :, 0], pair[:, :, 1]
    cross_probs, cross_mix = attend(cross_queries, text_keys, text_values, text_bias)
    cross_mix = cross_mix.reshape(tp, rows, local * HDIM)
    added = dot(cross_mix.reshape(tp * rows, -1), cout)
    after_cross = after_attn + me.collect(added.reshape(tp, rows, width))

    field_m, scale_m = normed(after_cross)
    mlp_entries = (field_m * gain_m[None]).astype(BF)
    mlp_rows = jnp.concatenate(me.spread(mlp_entries))
    hidden = dot(mlp_rows, up)
    active = jax.nn.gelu(hidden).astype(BF)
    added = dot(active, down)
    output = after_cross + me.collect(added.reshape(tp, rows, width))
    output = dot(place, output.astype(BF)).astype(BF)

    field_c1, scale_c1 = normed(me.tp_direct(after_attn[free]))
    field_m1, scale_m1 = normed(me.tp_direct(after_cross[free]))

    hidden_one = hidden.reshape(tp, rows, -1)[:, free]
    active_one, gelu_back = jax.vjp(jax.nn.gelu, hidden_one)
    active_one = active_one.astype(BF)
    grad_pre = gelu_back(grad_active)[0].astype(BF)
    grad_entry = me.tp_sum(dot_t(grad_pre, up))
    grad_gain_m = grad_entry[0] * field_m1[0]
    grad_mid = cot_group + norm_back(grad_entry * gain_m[None], field_m1, scale_m1)
    low_mid = grad_mid.astype(BF)

    grad_cmix = dot_t(low_mid, cout).astype(BF)
    query_one = cross_queries[:, free]
    cross_probs_one = cross_probs[:, :, free]
    grad_scores, grad_cq = attend_back(
        query_one, text_keys, text_values, cross_probs_one, grad_cmix.reshape(tp, local, HDIM)
    )
    grad_cq = grad_cq.reshape(tp, -1).astype(BF)
    query_one = query_one.reshape(tp, -1)
    grad_entry = me.tp_sum(dot_t(grad_cq, cq))
    grad_gain_c = grad_entry[0] * field_c1[0]
    grad_attn = grad_mid + norm_back(grad_entry * gain_c[None], field_c1, scale_c1)
    low_attn = grad_attn.astype(BF)

    heads_back = jnp.concatenate(
        [
            jnp.pad(head_blocks(query_one, local), ((0, 0), (0, local * HDIM))),
            jnp.pad(head_blocks(grad_cmix, local), ((0, 0), (local * HDIM, 0))),
        ]
    )
    rows_back = dot_t(heads_back, kv).reshape(2, tp, local, width)
    rows_back = jnp.stack([rows_back[0] * scale, rows_back[1]], axis=1).astype(BF)
    weighs = jnp.stack([grad_scores, cross_probs_one.astype(BF)], axis=1)
    sent = jnp.concatenate([rows_back, weighs], axis=-1).reshape(tp, 2 * local, width + txt)
    sent = me.to_owner(sent)
    weighs = sent[:, :, width:].reshape(tp * 2 * local, txt)
    rows_back = sent[:, :, :width].reshape(tp * 2 * local, width)
    grad_text = dot_sum(weighs, rows_back).astype(BF)
    weighs = xor_order(sent[:, :, width:], me.t, tp).reshape(tp * 2 * local, txt)
    left_text = dot(weighs, text[0]).astype(BF)
    lefts = jnp.concatenate(
        [left_text, cross_entries[free : free + 1], mlp_entries[free : free + 1]]
    )
    lefts = lefts.reshape(-1, world, own).transpose(1, 0, 2)
    lefts = lax.all_to_all(lefts, ("tp", "core", "fsdp"), 0, 0, tiled=True)

    grad_amix = dot_t(low_attn, out_w).astype(BF)
    attn_scores, grad_q = attend_back(
        queries[:, free],
        key_heads,
        value_heads,
        probs[:, :, free],
        grad_amix.reshape(tp, local, HDIM),
    )
    grad_q = grad_q.reshape(tp, -1).astype(BF)
    span = local * HDIM
    query_zero = queries[0, free].reshape(1, -1)
    heads_back = jnp.concatenate(
        [
            jnp.pad(head_blocks(grad_amix, local), ((0, 0), (2 * span, 0))),
            jnp.pad(head_blocks(query_zero, local), ((0, 0), (span, span))),
            jnp.pad(grad_q, ((0, 0), (0, 2 * span))),
        ]
    )
    rows_back = dot_t(heads_back, qkv)
    value_rows = rows_back[: tp * local].reshape(tp, local, width)
    key_rows = rows_back[tp * local : tp * local + local] * scale
    query_rows = rows_back[tp * local + local :].reshape(tp, 1, width)
    rows_back = jnp.concatenate(
        [jnp.broadcast_to(key_rows[None], (tp, local, width)), value_rows, query_rows], axis=1
    ).astype(BF)
    weighs = jnp.concatenate([attn_scores, probs[:, :, free].astype(BF)], axis=1)
    only = (lax.broadcasted_iota(jnp.int32, (tp, 1, rows), 2) == free).astype(BF)
    weighs = jnp.concatenate([weighs, only], axis=1)
    sent = me.to_owner(jnp.concatenate([rows_back, weighs], axis=-1))
    count = 2 * local + 1
    weighs = sent[:, :, width:].reshape(tp * count, rows)
    rows_back = sent[:, :, :width].reshape(tp * count, width)
    grad_entry = dot_sum(weighs, rows_back)
    weighs = xor_order(sent[:, : 2 * local, width:], me.t, tp).reshape(tp * 2 * local, rows)
    left_attn = dot(weighs, entries)
    grad_gain_a = jnp.sum(grad_entry * field_a, axis=0)
    grad_start = norm_back(grad_entry * gain_a[None], field_a, scale_a)
    grad_embed = grad_attn[0] + grad_start[free]
    grad_tokens = dot(place[:, :free], grad_start[:free].astype(BF)).astype(BF)
    summed = jnp.stack([grad_embed, grad_gain_a, grad_gain_c, grad_gain_m])
    lefts2 = jnp.concatenate([left_attn, summed]).astype(BF)
    lefts2 = lefts2.reshape(-1, world, own).transpose(1, 0, 2)
    lefts2 = lax.all_to_all(lefts2, ("tp", "core", "fsdp"), 0, 0, tiled=True)

    mixed_one = mixture[:, free]
    cross_one = cross_mix[:, free]
    by_group = me.gather_cz(
        jnp.concatenate([mixed_one, cross_one, active_one, cot_high, low_mid, low_attn], axis=1)
    )
    by_group = by_group.reshape(world, -1)
    ff = active_one.shape[1]
    cuts = [span, 2 * span, 2 * span + ff, 2 * span + ff + width, 2 * span + ff + 2 * width]
    mixed_all, cross_all, active_all, cot_f, mid_f, attn_f = jnp.split(by_group, cuts, axis=1)
    corner = me.c * planes + me.z

    def mine(stack):
        size = stack.shape[1] // (2 * planes)
        return lax.dynamic_slice_in_dim(stack, corner * size, size, axis=1)

    grad_w_out = dot_sum(mine(mixed_all), attn_f)
    grad_w_cout = dot_sum(mine(cross_all), mid_f)
    grad_w_down = dot_sum(mine(active_all), cot_f)

    by_column = me.gather_cz(
        jnp.concatenate([grad_pre, grad_cq, query_one, grad_cmix, grad_amix, grad_q], axis=1)
    )
    query_wide = me.tp_direct(query_zero)
    pieces = []
    for j in range(tp):
        came = me.hop(by_column, j) if j else by_column
        came = jnp.stack([came[:, i ^ j] for i in range(tp)], axis=1)
        pieces.append(came.reshape(world, -1))
    by_column = xor_order(jnp.stack(pieces), me.t, tp)
    query_wide = xor_order(query_wide, me.t, tp).reshape(HEADS, HDIM)

    def columns(start_at, size):
        return by_column[:, :, start_at : start_at + size]

    def flat(part):
        return part.transpose(1, 0, 2).reshape(world, -1)

    pre_f = flat(columns(0, ff))
    cq_f = flat(columns(ff, span))
    query_f = flat(columns(ff + span, span)).reshape(world, HEADS, HDIM)
    cmix_f = flat(columns(ff + 2 * span, span)).reshape(world, HEADS, HDIM)
    amix_f = flat(columns(ff + 3 * span, span)).reshape(world, HEADS, HDIM)
    q_f = flat(columns(ff + 4 * span, span))

    def image_order(stack):
        ordered = xor_order(stack, device, world)
        ordered = ordered.reshape((tp, 2 * planes) + stack.shape[1:])
        return ordered.swapaxes(0, 1).reshape(stack.shape)

    lefts = image_order(lefts)
    text_left = lefts[:, : 2 * HEADS].reshape(world, tp, 2, local, own)
    text_left = text_left.transpose(2, 0, 1, 3, 4).reshape(2, world, HEADS, own)
    grad_w_cq = dot_sum(lefts[:, 2 * HEADS], cq_f)
    grad_w_up = dot_sum(lefts[:, 2 * HEADS + 1], pre_f)

    def by_head(left, right):
        outer = jnp.einsum("ihr,ihe->hre", left, right, preferred_element_type=F32)
        return outer.transpose(1, 0, 2).reshape(own, width)

    grad_w_kv = jnp.concatenate(
        [by_head(text_left[0], query_f) * scale, by_head(text_left[1], cmix_f)], axis=1
    )
    attn_left = image_order(lefts2[:, : 2 * HEADS]).reshape(world, tp, 2, local, own)
    attn_left = attn_left.transpose(2, 0, 1, 3, 4).reshape(2, world, HEADS, own)
    key_left = jnp.sum(attn_left[0].astype(F32), axis=0)
    entry_own = lax.dynamic_slice_in_dim(entries[free], device * own, own).astype(F32)
    query_sum = jnp.sum(q_f.astype(F32), axis=0)
    grad_k = key_left[:, :, None] * query_wide.astype(F32)[:, None, :] * scale
    grad_w_qkv = jnp.concatenate(
        [
            entry_own[:, None] * query_sum[None, :],
            grad_k.transpose(1, 0, 2).reshape(own, width),
            by_head(attn_left[1], amix_f),
        ],
        axis=1,
    )
    summed = jnp.sum(lefts2[:, 2 * HEADS :].astype(F32), axis=0)
    return (
        output,
        grad_tokens,
        grad_text[None],
        summed[0],
        summed[1],
        grad_w_qkv,
        grad_w_out,
        summed[2],
        grad_w_cq,
        grad_w_kv,
        grad_w_cout,
        summed[3],
        grad_w_up,
        grad_w_down,
    )


def solution(mesh):
    tp, planes = mesh.shape["dp"] // 2, mesh.shape["fsdp"]
    fine = Mesh(mesh.devices.reshape(tp, 2, planes), ("tp", "core", "fsdp"))
    every = ("tp", "core", "fsdp")
    one, two, three = P(every), P(every, None), P(every, None, None)

    def layer(*arguments):
        return shards(tp, planes, *arguments)

    return jax.shard_map(
        layer,
        mesh=fine,
        in_specs=(two, three, three, two, one, one, one, two, two, one, two, two, two, one, two, two),
        out_specs=(two, two, three, one, one, two, two, one, two, two, two, one, two, two),
        check_vma=False,
    )
```

```python
import functools

import jax
import jax.numpy as jnp
from jax import lax
from jax.experimental import pallas as pl
from jax.experimental.pallas import tpu as pltpu
from jax.sharding import Mesh, PartitionSpec as P

HEADS = 16
HDIM = 128
TILE = 128
PAD = 16
BF = jnp.bfloat16
F32 = jnp.float32
VMEM_BYTES = 48 << 20


def dot(left, right):
    return jnp.dot(left, right, preferred_element_type=F32)


def dot_t(left, right):
    return lax.dot_general(left, right, (((1,), (1,)), ((), ())), preferred_element_type=F32)


def dot_sum(left, right):
    return lax.dot_general(left, right, (((0,), (0,)), ((), ())), preferred_element_type=F32)


def normed(rows):
    centered = rows - jnp.mean(rows, axis=-1, keepdims=True)
    scale = lax.rsqrt(jnp.mean(centered * centered, axis=-1, keepdims=True) + 1e-05)
    return centered * scale, scale


def norm_back(grad, field, scale):
    return scale * (
        grad
        - jnp.mean(grad, axis=-1, keepdims=True)
        - field * jnp.mean(grad * field, axis=-1, keepdims=True)
    )


def xor_order(stack, me, size):
    bit = 1
    while bit < size:
        split = stack.reshape((size // (2 * bit), 2, bit) + stack.shape[1:])
        turned = jnp.concatenate([split[:, 1:], split[:, :1]], axis=1)
        stack = jnp.where((me & bit) != 0, turned, split).reshape(stack.shape)
        bit *= 2
    return stack


def bits_of(size):
    return [1 << k for k in range(size.bit_length() - 1)]


class Layer:
    def __init__(self, tp, planes):
        self.tp, self.planes = tp, planes
        self.t, self.c, self.z = (lax.axis_index(a) for a in ("tp", "core", "fsdp"))


    def hop(self, value, j):
        return lax.ppermute(value, "tp", [(i, i ^ j) for i in range(self.tp)])

    def other_core(self, value):
        return lax.ppermute(value, "core", [(0, 1), (1, 0)])

    def other_plane(self, value, k):
        return lax.ppermute(value, "fsdp", [(i, i ^ k) for i in range(self.planes)])

    def spread(self, value):
        return [value] + [self.hop(value, j) for j in range(1, self.tp)]

    def collect(self, parts):
        return [parts[0]] + [self.hop(parts[j], j) for j in range(1, self.tp)]

    def tp_direct(self, value):
        return jnp.stack([value] + [self.hop(value, j) for j in range(1, self.tp)])

    def tp_parts(self, value):
        return [value] + [self.hop(value, j) for j in range(1, self.tp)]

    def to_owner(self, stack):
        return [stack[0]] + [self.hop(stack[j], j) for j in range(1, self.tp)]

    def to_rows(self, value):
        return lax.all_to_all(value, ("tp", "core", "fsdp"), 0, 0, tiled=True)

    def gather_cz(self, value):
        planes = jnp.stack([value] + [self.other_plane(value, k) for k in range(1, self.planes)])
        return jnp.concatenate([planes, self.other_core(planes)])


    def shuffle(self, shards):
        split = [
            shard.reshape(shard.shape[0], kinds, self.tp, -1).transpose(2, 0, 1, 3)
            for shard, kinds in shards
        ]
        split = [part.reshape(part.shape[:2] + (-1,)) for part in split]
        sent = lax.all_to_all(jnp.concatenate(split, axis=2), "tp", 0, 0, tiled=True)
        cuts = [sum(part.shape[2] for part in split[: k + 1]) for k in range(len(split) - 1)]
        return jnp.split(sent, cuts, axis=2)

    def gather_blocks(self, shard):
        return lax.all_gather(shard, ("core", "fsdp"), axis=0)


def block(weights, t, columns):
    part = weights[:, t, :, columns]
    return part.reshape(part.shape[0] * part.shape[1], part.shape[2])


def project(rows, weights, columns):
    tp = weights.shape[1]
    step = rows.shape[1] // tp
    total = dot(rows[:, :step], block(weights, 0, columns))
    for t in range(1, tp):
        total = total + dot(rows[:, t * step : (t + 1) * step], block(weights, t, columns))
    return total


def start_copies(pairs, sems):
    copies = [pltpu.make_async_copy(a, b, sems.at[k]) for k, (a, b) in enumerate(pairs)]
    for copy in copies:
        copy.start()
    return copies


def softmax_head(queries, keys, bias, free, extra):
    scale = HDIM ** (-0.5)
    logits = dot_t(queries, keys[:free]) * scale
    if bias is not None:
        logits = logits + bias
    top = jnp.max(logits, axis=-1, keepdims=True)
    if not extra:
        weighs = jnp.exp(logits - top)
        return weighs / jnp.sum(weighs, axis=-1, keepdims=True), None
    one = dot_t(queries, keys[free:])[:, :1] * scale
    top = jnp.maximum(top, one)
    weighs, one = jnp.exp(logits - top), jnp.exp(one - top) * extra
    total = jnp.sum(weighs, axis=-1, keepdims=True) + one
    return weighs / total, one / total


def self_kernel(tp, local, count, *refs):
    entries, masked_entries, gathered, outs = refs[:tp], refs[tp], refs[tp + 1], refs[tp + 2]
    partial = refs[tp + 3 : 2 * tp + 3]
    packed, mix_out, probs_out, weight, out_weight, held, mixed, sems = refs[2 * tp + 3 :]
    free, rows, span = entries[0].shape[0], packed.shape[1], local * HDIM
    pairs = [(ref, held.at[i * free : (i + 1) * free]) for i, ref in enumerate(entries)]
    pairs += [(masked_entries, held.at[tp * free :]), (gathered, weight)]
    pairs += [(outs.at[:, : out_weight.shape[1]], out_weight)]
    copies = start_copies(pairs, sems)
    for copy in copies[:-1]:
        copy.wait()
    for k in range(3):
        cols = slice(k * span, (k + 1) * span)
        found = project(held[...], weight, cols).astype(BF)
        for i in range(tp):
            packed[i, :free, cols] = found[i * free : (i + 1) * free]
            packed[i, free:, cols] = found[tp * free :]
    probs_out[...] = jnp.zeros_like(probs_out)
    for i in range(tp):
        for h in range(local):
            cols = [slice(k * span + h * HDIM, k * span + (h + 1) * HDIM) for k in range(3)]
            queries, keys, values = (packed[i, :, c] for c in cols)
            probs, one = softmax_head(queries, keys, None, free, float(count))
            probs_out[i, h : h + 1, :free] = probs[free : free + 1]
            probs_out[i, h : h + 1, free:] = jnp.broadcast_to(one[free : free + 1], (1, TILE))
            mixture = dot(probs.astype(BF), values[:free])
            mixture = mixture + one.astype(BF).astype(F32) * values[free : free + 1].astype(F32)
            mixed[i * rows : (i + 1) * rows, cols[0]] = mixture.astype(BF)
        mix_out[i] = mixed[i * rows + free : (i + 1) * rows]
    copies[-1].wait()
    write_out(tp, mixed, out_weight, partial)


def write_out(tp, mixed, out_weight, partial):
    rows, width = partial[0].shape
    for start in range(0, width, 512):
        cols = slice(start, start + 512)
        part = out_weight[:, :, cols].reshape(-1, 512)
        added = dot(mixed[...], part).astype(BF)
        for i in range(tp):
            partial[i][:, cols] = added[i * rows : (i + 1) * rows]


def cross_kernel(tp, local, *refs):
    entries, text = refs[:tp], refs[tp : 2 * tp]
    bias, gathered, outs = refs[2 * tp : 2 * tp + 3]
    partial = refs[2 * tp + 3 : 3 * tp + 3]
    pair, query_out, mix_out, probs_out = refs[3 * tp + 3 : 3 * tp + 7]
    weight, out_weight, held, held_text, queries, mixed, sems = refs[3 * tp + 7 :]
    rows, txt, span = entries[0].shape[0], text[0].shape[0], local * HDIM
    free = rows - PAD
    pairs = [(ref, held_text.at[i * txt : (i + 1) * txt]) for i, ref in enumerate(text)]
    pairs += [(ref, held.at[i * rows : (i + 1) * rows]) for i, ref in enumerate(entries)]
    pairs += [(gathered, weight), (outs.at[:, out_weight.shape[1] :], out_weight)]
    copies = start_copies(pairs, sems)
    for copy in copies[:-1]:
        copy.wait()
    for k in range(2):
        cols = slice(k * span, (k + 1) * span)
        found = project(held_text[...], weight, cols).astype(BF)
        for i in range(tp):
            pair[i, :, cols] = found[i * txt : (i + 1) * txt]
    queries[...] = project(held[...], weight, slice(2 * span, 3 * span)).astype(BF)
    probs_out[...] = jnp.zeros_like(probs_out)
    for i in range(tp):
        query_out[i] = queries[i * rows + free : (i + 1) * rows]
        for h in range(local):
            cols = slice(h * HDIM, (h + 1) * HDIM)
            keys = pair[i, :, cols]
            values = pair[i, :, span + h * HDIM : span + (h + 1) * HDIM]
            some = queries[i * rows : (i + 1) * rows, cols]
            probs, _ = softmax_head(some, keys, bias[i : i + 1], txt, 0)
            probs_out[i, h : h + 1] = probs[free : free + 1]
            mixed[i * rows : (i + 1) * rows, cols] = dot(probs.astype(BF), values).astype(BF)
        mix_out[i] = mixed[i * rows + free : (i + 1) * rows]
    copies[-1].wait()
    write_out(tp, mixed, out_weight, partial)


def gelu_parts(value):
    slope = 0.7978845608
    bent = jnp.tanh(slope * (value + 0.044715 * value * value * value))
    half = 0.5 * (1.0 + bent)
    steep = slope * (1.0 + 3.0 * 0.044715 * value * value)
    return value * half, half + 0.5 * value * (1.0 - bent * bent) * steep


def up_kernel(entries, weight, active):
    active[...] = gelu_parts(project(entries[...], weight, slice(None)))[0].astype(BF)


def mlp_back_kernel(
    entries, grad_active, gathered, active, grad_pre, grad_entry, weight, sem,
):
    tp, step = weight.shape[1], entries.shape[1] // weight.shape[1]
    copies = [
        pltpu.make_async_copy(gathered.at[:, t], weight.at[:, t], sem.at[t]) for t in range(tp)
    ]
    for copy in copies:
        copy.start()
    hidden = jnp.zeros(active.shape, F32)
    for t, copy in enumerate(copies):
        copy.wait()
        hidden = hidden + dot(
            entries[:, t * step : (t + 1) * step], block(weight, t, slice(None))
        )
    value, steep = gelu_parts(hidden)
    active[...] = value.astype(BF)
    grad_pre[...] = (steep * grad_active[...]).astype(BF)
    for t in range(tp):
        back = dot_t(grad_pre[...], block(weight, t, slice(None)))
        grad_entry[:, t * step : (t + 1) * step] = back[:tp]


def summed(parts, i):
    total = parts[0][i : i + 1]
    for j in range(1, len(parts)):
        total = total + parts[j][i ^ j : (i ^ j) + 1]
    return total


def head_mask(span):
    heads = lax.broadcasted_iota(jnp.int32, (8, span), 0)
    return lax.broadcasted_iota(jnp.int32, (8, span), 1) // HDIM == heads


def row_back(parts, rows, gain, base, i, out, gain_row):
    grad = summed(parts, i)
    field, scale = normed(rows[i : i + 1])
    out[i : i + 1] = base[i : i + 1] + norm_back(grad * gain[...], field, scale)
    if i == 0:
        gain_row[...] = grad * field


def cross_back_kernel(
    tp, base, rows, gain, pair, probs, kvq, outs, *refs,
):
    parts = refs[:tp]
    grad_mid, grad_cmix, scores, grad_cq, grad_entry, gain_row = refs[tp : tp + 6]
    weight, out_weight, held, sems = refs[tp + 6 :]
    span, own = weight.shape[3], out_weight.shape[1]
    copies = [
        pltpu.make_async_copy(outs.at[:, own:], out_weight, sems.at[0]),
        pltpu.make_async_copy(kvq.at[:, :, :, 2 * span :], weight, sems.at[1]),
    ]
    for copy in copies:
        copy.start()
    held[...] = jnp.zeros_like(held)
    for i in range(tp):
        row_back(parts, rows, gain, base, i, held, gain_row)
    grad_mid[...] = held[:tp]
    copies[0].wait()
    mixed = dot_t(held[...].astype(BF), out_weight[...].reshape(span, -1)).astype(BF).astype(F32)
    grad_cmix[...] = mixed[:tp]
    mask = head_mask(span)
    held[...] = jnp.zeros_like(held)
    for i in range(tp):
        spread = jnp.where(mask, mixed[i : i + 1], 0.0).astype(BF)
        grad_probs = dot_t(spread, pair[i, :, span:])
        weighs = probs[i]
        grad = weighs * (grad_probs - jnp.sum(grad_probs * weighs, axis=-1, keepdims=True))
        grad = grad.astype(BF)
        scores[i] = grad.astype(F32)
        back = jnp.where(mask, dot(grad, pair[i, :, :span]), 0.0)
        held[i : i + 1, :span] = jnp.sum(back, axis=0, keepdims=True) * HDIM ** (-0.5)
    grad_cq[...] = held[:tp, :span]
    queries = held[:, :span].astype(BF)
    copies[1].wait()
    step = grad_entry.shape[1] // tp
    for t in range(tp):
        back = dot_t(queries, block(weight, t, slice(None)))
        grad_entry[:, t * step : (t + 1) * step] = back[:tp]


def self_back_kernel(
    tp, base, rows, gain, packed, probs, masked_entries, qkv, outs, *refs,
):
    parts, entries, refs = refs[:tp], refs[tp : 2 * tp], refs[tp:]
    grad_attn, grad_amix, grad_q, gain_row, left, sent = refs[tp : tp + 6]
    weight, out_weight, held, spreads, sems = refs[tp + 6 :]
    own, width = out_weight.shape[1:]
    span, free = weight.shape[3] // 3, entries[0].shape[0]
    copies = [
        pltpu.make_async_copy(outs.at[:, :own], out_weight, sems.at[0]),
        pltpu.make_async_copy(qkv, weight, sems.at[1]),
    ]
    for copy in copies:
        copy.start()
    held[...] = jnp.zeros_like(held)
    for i in range(tp):
        row_back(parts, rows, gain, base, i, held, gain_row)
    grad_attn[...] = held[:tp]
    copies[0].wait()
    mixed = dot_t(held[...].astype(BF), out_weight[...].reshape(span, -1)).astype(BF).astype(F32)
    grad_amix[...] = mixed[:tp]
    mask = head_mask(span)
    held[...] = jnp.zeros_like(held)
    first = lax.broadcasted_iota(jnp.int32, (PAD, TILE), 1) == 0
    only = first & (lax.broadcasted_iota(jnp.int32, (PAD, TILE), 0) == 0)
    masked_row = masked_entries[:1].astype(F32)
    for i in range(tp):
        spread = jnp.where(mask, mixed[i : i + 1], 0.0)
        spreads[8 * i : 8 * i + 8] = spread
        spread = spread.astype(BF)
        values = packed[i, :, 2 * span :]
        grad_probs, grad_one = dot_t(spread, values[:free]), dot_t(spread, values[free:])[:, :1]
        weighs, one = probs[i, :, :free], probs[i, :, free : free + 1]
        mean = jnp.sum(grad_probs * weighs, axis=-1, keepdims=True) + grad_one * one
        grad = (weighs * (grad_probs - mean)).astype(BF)
        grad_one = (one * (grad_one - mean)).astype(BF).astype(F32)
        keys = packed[i, :, span : 2 * span]
        back = dot(grad, keys[:free]) + grad_one * keys[free : free + 1].astype(F32)
        back = jnp.sum(jnp.where(mask, back, 0.0), axis=0, keepdims=True)
        held[i : i + 1, :span] = back * HDIM ** (-0.5)
        both = jnp.concatenate([grad.astype(F32), weighs], axis=0).astype(BF)
        both_one = jnp.concatenate([grad_one, one], axis=0).astype(BF).astype(F32)
        left[i] = (dot(both, entries[i][...]) + both_one * masked_row).astype(BF)
        sent[i, :PAD, width : width + free] = both
        sent[i, :PAD, width + free :] = jnp.where(first, both_one, 0.0).astype(BF)
        sent[i, PAD:, width : width + free] = jnp.zeros((PAD, free), BF)
        sent[i, PAD:, width + free :] = jnp.where(only, 1.0, 0.0).astype(BF)
    grad_q[...] = held[:tp, :span]
    queries = held[:, :span].astype(BF)
    zero_query = packed[0, free:, :span].astype(F32)[:1]
    key_spread = jnp.where(mask, zero_query, 0.0).astype(BF)
    value_spread = spreads[...].astype(BF)
    step = width // tp
    copies[1].wait()
    empty = jnp.zeros((PAD - 1, step), F32)
    for t in range(tp):
        cols = slice(t * step, (t + 1) * step)
        keys = dot_t(key_spread, block(weight, t, slice(span, 2 * span))) * HDIM ** (-0.5)
        values = dot_t(value_spread, block(weight, t, slice(2 * span, 3 * span)))
        query_rows = dot_t(queries, block(weight, t, slice(0, span)))
        for i in range(tp):
            both = jnp.concatenate([keys, values[8 * i : 8 * i + 8]], axis=0)
            sent[i, :PAD, cols] = both.astype(BF)
            last = jnp.concatenate([query_rows[i : i + 1], empty], axis=0)
            sent[i, PAD:, cols] = last.astype(BF)


def tokens_back_kernel(tp, rows, gain, base, place, *refs):
    came, (tokens, small) = refs[:tp], refs[tp:]
    width, free = rows.shape[1], place.shape[1]
    grad, grad_one = 0.0, 0.0
    for part in came:
        back = part[:, :width]
        grad = grad + dot_sum(part[:, width : width + free], back)
        grad_one = grad_one + dot_sum(part[:, width + free :], back)[:1]
    field, scale = normed(rows[:free])
    start = norm_back(grad * gain[...], field, scale)
    tokens[...] = dot(place[...], start.astype(BF)).astype(BF)
    one_field, one_scale = normed(rows[free : free + 1])
    start = norm_back(grad_one * gain[...], one_field, one_scale)
    small[0:1] = base[0:1] + start
    small[1:2] = jnp.sum(grad * field, axis=0, keepdims=True) + grad_one * one_field


def aligned(right, corner, tp):
    count = right.shape[0]
    out = lax.broadcasted_iota(jnp.int32, (count, count), 0)
    into = lax.broadcasted_iota(jnp.int32, (count, count), 1)
    same = (out // tp == (corner ^ (into // tp))) & (out % tp == into % tp)
    return dot(same.astype(BF), right).astype(BF)


def cross_columns_kernel(
    local, place, text_left, one_left, right, grad_kv, grad_cq, grad_up,
):
    tp, span = right.shape[0], local * HDIM
    ff = right.shape[2] - 3 * span
    for j in range(tp):
        at = place[0] ^ j
        rows = aligned(right[j], place[1], tp)
        columns = pl.ds(pl.multiple_of(at * span, span), span)
        grad_cq[:, columns] = dot_sum(one_left[at, 0], rows[:, ff : ff + span])
        wide = pl.ds(pl.multiple_of(at * ff, ff), ff)
        grad_up[:, wide] = dot_sum(one_left[at, 1], rows[:, :ff])
        for h in range(local):
            for kind in range(2):
                start = ff + (1 + kind) * span + h * HDIM
                outer = dot_sum(text_left[at, kind, h], rows[:, start : start + HDIM])
                if kind == 0:
                    outer = outer * HDIM ** (-0.5)
                begin = kind * tp * span + at * span + h * HDIM
                grad_kv[:, pl.ds(pl.multiple_of(begin, HDIM), HDIM)] = outer


def self_columns_kernel(local, place, left, entry, right, grad_qkv):
    tp, span = right.shape[0], local * HDIM
    ones = jnp.ones((right.shape[1], HDIM), BF)
    for j in range(tp):
        at = place[0] ^ j
        rows = aligned(right[j, :, :span], place[1], tp)
        total = jnp.sum(right[j, :, span : 2 * span].astype(F32), axis=0, keepdims=True)
        queries = right[j, :, 2 * span :].astype(F32)[:1] * HDIM ** (-0.5)
        grad_qkv[:, pl.ds(pl.multiple_of(at * span, span), span)] = entry[...] * total
        for h in range(local):
            cols = slice(h * HDIM, (h + 1) * HDIM)
            keys = dot_sum(left[at, 0, h], ones) * queries[:, cols]
            begin = tp * span + at * span + h * HDIM
            grad_qkv[:, pl.ds(pl.multiple_of(begin, HDIM), HDIM)] = keys
            begin = 2 * tp * span + at * span + h * HDIM
            values = dot_sum(left[at, 1, h], rows[:, cols])
            grad_qkv[:, pl.ds(pl.multiple_of(begin, HDIM), HDIM)] = values


def whole_spec():
    return pl.BlockSpec(memory_space=pl.ANY)


def in_vmem(kernel, name, operands, out_shape, scratch_shapes=(), held=()):
    spaces = dict(held)
    return pl.pallas_call(
        kernel,
        in_specs=[
            pl.BlockSpec(memory_space=spaces.get(k, pltpu.VMEM)) for k in range(len(operands))
        ],
        out_specs=[pl.BlockSpec(memory_space=pltpu.VMEM)] * len(out_shape),
        out_shape=[jax.ShapeDtypeStruct(shape, dtype) for shape, dtype in out_shape],
        scratch_shapes=scratch_shapes,
        compiler_params=pltpu.CompilerParams(vmem_limit_bytes=VMEM_BYTES),
        name=name,
    )(*operands)


def self_forward(local, count, entries, masked_entries, gathered, outs):
    tp, (free, width) = len(entries), entries[0].shape
    span, rows = local * HDIM, free + PAD
    found = in_vmem(
        functools.partial(self_kernel, tp, local, count),
        "self_attention",
        [*entries, masked_entries, gathered, outs],
        [((rows, width), BF)] * tp
        + [((tp, rows, 3 * span), BF), ((tp, PAD, span), BF), ((tp, 8, free + TILE), F32)],
        [
            pltpu.VMEM(gathered.shape, BF),
            pltpu.VMEM((outs.shape[0], outs.shape[1] // 2, width), BF),
            pltpu.VMEM((tp * free + PAD, width), BF),
            pltpu.VMEM((tp * rows, span), BF),
            pltpu.SemaphoreType.DMA((tp + 3,)),
        ],
        [(k, pl.ANY) for k in range(tp + 3)],
    )
    return found[:tp], *found[tp:]


def cross_forward(local, entries, text, bias, gathered, outs):
    tp, (rows, width) = len(entries), entries[0].shape
    txt, span = text[0].shape[0], local * HDIM
    found = in_vmem(
        functools.partial(cross_kernel, tp, local),
        "cross_attention",
        [*entries, *text, bias, gathered, outs],
        [((rows, width), BF)] * tp
        + [
            ((tp, txt, 2 * span), BF),
            ((tp, PAD, span), BF),
            ((tp, PAD, span), BF),
            ((tp, 8, txt), F32),
        ],
        [
            pltpu.VMEM(gathered.shape, BF),
            pltpu.VMEM((outs.shape[0], outs.shape[1] // 2, width), BF),
            pltpu.VMEM((tp * rows, width), BF),
            pltpu.VMEM((tp * txt, width), BF),
            pltpu.VMEM((tp * rows, span), BF),
            pltpu.VMEM((tp * rows, span), BF),
            pltpu.SemaphoreType.DMA((2 * tp + 2,)),
        ],
        [(k, pl.ANY) for k in range(2 * tp + 3) if k != 2 * tp],
    )
    return found[:tp], *found[tp:]


def down_kernel(tp, active, weight, *partial):
    rows = partial[0].shape[0]
    part = weight[...]
    added = dot(active[...], part.reshape(-1, part.shape[2])).astype(BF)
    for i in range(tp):
        partial[i][...] = added[i * rows : (i + 1) * rows]


def mlp_down(tp, active, gathered):
    blocks, own, width = gathered.shape
    rows, step = active.shape[0] // tp, 512
    return pl.pallas_call(
        functools.partial(down_kernel, tp),
        grid=(width // step,),
        in_specs=[
            pl.BlockSpec(active.shape, lambda i: (0, 0)),
            pl.BlockSpec((blocks, own, step), lambda i: (0, 0, i)),
        ],
        out_specs=[pl.BlockSpec((rows, step), lambda i: (0, i))] * tp,
        out_shape=[jax.ShapeDtypeStruct((rows, width), BF)] * tp,
        compiler_params=pltpu.CompilerParams(vmem_limit_bytes=VMEM_BYTES),
        name="mlp_down",
    )(active, gathered)


def mlp_up(entries, gathered):
    rows, width = entries.shape
    blocks, tp, own, ff = gathered.shape
    step = min(ff, 512)
    return pl.pallas_call(
        up_kernel,
        grid=(ff // step,),
        in_specs=[
            pl.BlockSpec((rows, width), lambda i: (0, 0)),
            pl.BlockSpec((blocks, tp, own, step), lambda i: (0, 0, 0, i)),
        ],
        out_specs=pl.BlockSpec((rows, step), lambda i: (0, i)),
        out_shape=jax.ShapeDtypeStruct((rows, ff), BF),
        compiler_params=pltpu.CompilerParams(vmem_limit_bytes=VMEM_BYTES),
        name="mlp_up",
    )(entries, gathered)


def mlp_back(entries, grad_active, gathered):
    rows, width = entries.shape
    tp, ff = gathered.shape[1], gathered.shape[3]
    return pl.pallas_call(
        mlp_back_kernel,
        in_specs=[
            pl.BlockSpec(memory_space=pltpu.VMEM),
            pl.BlockSpec(memory_space=pltpu.VMEM),
            whole_spec(),
        ],
        out_specs=[pl.BlockSpec(memory_space=pltpu.VMEM)] * 3,
        out_shape=[
            jax.ShapeDtypeStruct((rows, ff), BF),
            jax.ShapeDtypeStruct((rows, ff), BF),
            jax.ShapeDtypeStruct((tp, width), F32),
        ],
        scratch_shapes=[pltpu.VMEM(gathered.shape, BF), pltpu.SemaphoreType.DMA((tp,))],
        compiler_params=pltpu.CompilerParams(vmem_limit_bytes=VMEM_BYTES),
        name="mlp_back",
    )(entries, grad_active, gathered)


def cross_back(base, rows, gain, pair, probs, kvq, outs, parts):
    tp, width = base.shape
    blocks, _, own, columns = kvq.shape
    span = columns // 3
    return in_vmem(
        functools.partial(cross_back_kernel, tp),
        "cross_back",
        [base, rows, gain[None], pair, probs, kvq, outs, *parts],
        [
            ((tp, width), F32),
            ((tp, span), F32),
            (probs.shape, F32),
            ((tp, span), F32),
            ((tp, width), F32),
            ((1, width), F32),
        ],
        [
            pltpu.VMEM((blocks, tp, own, span), BF),
            pltpu.VMEM((blocks, own, width), BF),
            pltpu.VMEM((8, width), F32),
            pltpu.SemaphoreType.DMA((2,)),
        ],
        ((5, pl.ANY), (6, pl.ANY)),
    )


def self_back(base, rows, gain, packed, probs, entries, masked_entries, qkv, outs, parts):
    tp, width = base.shape
    blocks, _, own, columns = qkv.shape
    span, free = columns // 3, entries[0].shape[0]
    return in_vmem(
        functools.partial(self_back_kernel, tp),
        "self_back",
        [base, rows, gain[None], packed, probs, masked_entries, qkv, outs, *parts, *entries],
        [
            ((tp, width), F32),
            ((tp, span), F32),
            ((tp, span), F32),
            ((1, width), F32),
            ((tp, PAD, width), BF),
            ((tp, 2 * PAD, width + free + TILE), BF),
        ],
        [
            pltpu.VMEM(qkv.shape, BF),
            pltpu.VMEM((blocks, own, width), BF),
            pltpu.VMEM((8, width), F32),
            pltpu.VMEM((8 * tp, span), F32),
            pltpu.SemaphoreType.DMA((2,)),
        ],
        ((6, pl.ANY), (7, pl.ANY)),
    )


def join_kernel(free, base, gain, *refs):
    parts, (total, entries) = refs[:-2], refs[-2:]
    value = base[...]
    for part in parts:
        value = value + part[...].astype(F32)
    total[...] = value
    found = normed(value)[0] * gain[...]
    entries[...] = found.astype(BF)

    @pl.when(pl.program_id(0) == pl.num_programs(0) - 1)
    def _():
        at = value.shape[0] - PAD
        row = value[at : at + 1]
        spot = lax.broadcasted_iota(jnp.int32, (PAD, value.shape[1]), 0)
        last = found[at:]
        for k in range(3):
            part = row.astype(BF).astype(F32)
            last = jnp.where(spot == k + 1, part, last)
            row = row - part
        entries[at:] = last.astype(BF)


def join(base, parts, gain):
    rows, width = base.shape
    step = PAD * 3 if rows % (PAD * 3) == 0 else PAD
    block = pl.BlockSpec((step, width), lambda i: (i, 0))
    return pl.pallas_call(
        functools.partial(join_kernel, rows - PAD),
        grid=(rows // step,),
        in_specs=[block, pl.BlockSpec((1, width), lambda i: (0, 0))] + [block] * len(parts),
        out_specs=[block, block],
        out_shape=[
            jax.ShapeDtypeStruct((rows, width), F32),
            jax.ShapeDtypeStruct((rows, width), BF),
        ],
        compiler_params=pltpu.CompilerParams(vmem_limit_bytes=VMEM_BYTES),
        name="join",
    )(base, gain[None], *parts)


def masked_rows(entries, free):
    last = jnp.stack([value[free:] for value in entries])
    return last[:, 0], jnp.sum(last[:, 1:4].astype(F32), axis=1)


def head_blocks(rows, local):
    images = rows.shape[0]
    spread = rows.reshape(images, 1, local, HDIM) * jnp.eye(local, dtype=rows.dtype)[None, :, :, None]
    return spread.reshape(images * local, local * HDIM)


def shards(
    tp,
    planes,
    tokens,
    text,
    cotangent,
    positions,
    text_lengths,
    mask_embed,
    gain_attn,
    w_qkv,
    w_attn_out,
    gain_cross,
    w_cross_q,
    w_cross_kv,
    w_cross_out,
    gain_mlp,
    w_up,
    w_down,
):
    me = Layer(tp, planes)
    seq, width = tokens.shape
    masked_count = positions.shape[1]
    free = seq - masked_count
    txt = text.shape[1]
    local = HEADS // tp
    rows = free + PAD
    device = (me.t * 2 + me.c) * planes + me.z
    world = tp * 2 * planes
    own = width // world

    def after(value, earlier):
        return lax.optimization_barrier((value, earlier))[0]

    span = local * HDIM

    outs = me.gather_blocks(jnp.concatenate([w_attn_out, w_cross_out]))
    (qkv_sent,) = me.shuffle([(w_qkv, 3)])
    text_rows = me.spread(text[0])

    def natural(value):
        split = value.reshape(value.shape[:-1] + (2 * planes, tp, own))
        return split.swapaxes(-3, -2).reshape(value.shape)

    cot_sum = jnp.sum(cotangent[0].astype(F32), axis=0)
    vectors = jnp.concatenate([mask_embed, gain_attn, gain_cross, gain_mlp]).astype(F32)
    fill = TILE - vectors.shape[0] % TILE
    length = jnp.broadcast_to(text_lengths.astype(F32), (fill,))
    gathered = me.tp_direct(me.gather_cz(jnp.concatenate([cot_sum, vectors, length])))
    pair_query = jnp.concatenate([w_cross_kv, w_cross_q], axis=1)
    others = after((pair_query, w_up), (gathered, qkv_sent))
    kvq_sent, up_sent = lax.optimization_barrier(me.shuffle(list(zip(others, (3, 1)))))
    vectors = gathered[:, :, width : width + 4 * own].reshape(world, 4, own)
    vectors = xor_order(vectors, device, world).transpose(1, 0, 2).reshape(4, width)
    embed, gain_a, gain_c, gain_m = vectors[0], vectors[1], vectors[2], vectors[3]
    lengths = gathered[:, 0, width + 4 * own :][:, :1]
    text_bias = jnp.where(
        lax.broadcasted_iota(jnp.int32, (tp, txt), 1).astype(F32) < lengths, 0.0, -1e30
    )
    cot_group = gathered[:, 0, :width]

    spots = lax.broadcasted_iota(jnp.int32, (masked_count, seq), 1)
    masked = jnp.sum((positions[0][:, None] == spots).astype(F32), axis=0)
    below = lax.broadcasted_iota(jnp.int32, (seq, seq), 0) <= lax.broadcasted_iota(
        jnp.int32, (seq, seq), 1
    )
    rank = dot((1.0 - masked).astype(BF)[None, :], below.astype(BF))[0]
    ranks = lax.broadcasted_iota(jnp.int32, (free, seq), 0).astype(F32) + 1.0
    pick = ((rank[None, :] == ranks) & (masked[None, :] == 0.0)).astype(BF)
    place = jnp.concatenate(
        [pick.T, masked[:, None].astype(BF), jnp.zeros((seq, PAD - 1), BF)], axis=1
    )
    start_free = dot(pick, tokens)
    start = jnp.concatenate([start_free, jnp.broadcast_to(embed[None], (PAD, width))])

    cot_rows = gathered[:, :, :width].reshape(world, width)
    high = cot_rows.astype(BF)
    low = (cot_rows - high.astype(F32)).astype(BF)
    through = dot_t(jnp.concatenate([high, low]), w_down)
    through = through[:world] + through[world:]
    through = through.reshape(tp, 2 * planes, -1).transpose(1, 0, 2)
    through = xor_order(through, me.c * planes + me.z, 2 * planes)
    through = lax.all_to_all(through, ("core", "fsdp"), 0, 0, tiled=True)
    grad_active = through.transpose(1, 0, 2).reshape(tp, -1)

    field_a, scale_a = normed(start)
    entries = (field_a * gain_a[None]).astype(BF)
    qkv = me.gather_blocks(after(qkv_sent, (outs, entries, text_rows)))
    entries_all = me.spread(entries[:free])
    kvq = me.gather_blocks(after(kvq_sent, (qkv, entries_all)))
    partial, packed, mixed_one, probs_one = self_forward(
        local, masked_count, entries_all, entries[free:], qkv, outs
    )
    after_attn, cross_entries = join(after(start, (grad_active, place)), me.collect(partial), gain_c)

    cross_all = me.spread(cross_entries)
    up = me.gather_blocks(after(up_sent, (kvq, after_attn)))
    partial, pair, query_one, cross_one, cross_probs_one = cross_forward(
        local, cross_all, text_rows, text_bias, kvq, outs
    )
    after_cross, mlp_entries = join(after_attn, me.collect(partial), gain_m)

    mlp_all = me.spread(mlp_entries)
    down = me.gather_blocks(after(w_down, (up, after_cross)))

    mlp_one, cross_stream = masked_rows(mlp_all, free)
    cross_entry, attn_stream = masked_rows(cross_all, free)
    active_one, grad_pre, grad_entry = mlp_back(
        jnp.pad(mlp_one, ((0, PAD - tp), (0, 0))),
        jnp.pad(grad_active, ((0, PAD - tp), (0, 0))),
        up,
    )
    grad_mid, grad_cmix, scores, grad_cq, grad_entry, grad_gain_m = cross_back(
        cot_group, cross_stream, gain_m, pair, cross_probs_one, kvq, outs, me.tp_parts(grad_entry)
    )
    grad_attn, grad_amix, grad_q, grad_gain_c, left, sent = self_back(
        grad_mid,
        attn_stream,
        gain_c,
        packed,
        probs_one,
        entries_all,
        entries[free:],
        qkv,
        outs,
        me.tp_parts(grad_entry),
    )

    came = me.to_owner(sent)

    query_one = after(query_one, grad_attn)[:, 0]
    heads_back = jnp.concatenate(
        [
            jnp.pad(head_blocks(query_one, local), ((0, 0), (0, span))),
            jnp.pad(head_blocks(grad_cmix.astype(BF), local), ((0, 0), (span, 0))),
        ]
    )
    kv_rows = after(kvq, grad_attn).reshape(width, -1)[:, : 2 * span]
    rows_back = natural(dot_t(heads_back, kv_rows)).reshape(2, tp, local, width)
    rows_back = jnp.stack([rows_back[0] * HDIM ** (-0.5), rows_back[1]], axis=1).astype(BF)
    weighs = jnp.stack([scores[:, :local], cross_probs_one[:, :local]], axis=1).astype(BF)
    text_sent = jnp.concatenate([rows_back, weighs], axis=-1)
    text_sent = jnp.stack(me.to_owner(text_sent.reshape(tp, 2 * local, width + txt)))
    grad_text = dot_sum(
        text_sent[:, :, width:].reshape(-1, txt), text_sent[:, :, :width].reshape(-1, width)
    ).astype(BF)

    corner = me.c * planes + me.z
    ff = grad_pre.shape[1]

    def gather_factors(columns, others):
        parts = [part.astype(BF) for part in columns + others]
        whole = me.gather_cz(jnp.concatenate(parts, axis=1)).reshape(world, -1)
        cuts = [sum(part.shape[1] for part in parts[: k + 1]) for k in range(len(parts) - 1)]
        cut = cuts[len(columns) - 1]
        right = whole[:, :cut]
        right = jnp.stack([right] + [me.hop(right, j) for j in range(1, tp)])
        return right, jnp.split(whole[:, cut:], [c - cut for c in cuts[len(columns) :]], axis=1)

    def mine(stack):
        size = stack.shape[1] // (2 * planes)
        return lax.dynamic_slice_in_dim(stack, corner * size, size, axis=1)

    early_right, (mixed_f, cross_f, active_f, cot_f, mid_f) = gather_factors(
        [after(grad_pre, grad_attn)[:tp], grad_cq, query_one, grad_cmix],
        [mixed_one[:, 0], cross_one[:, 0], active_one[:tp], cot_group, grad_mid],
    )
    grad_w_cout = dot_sum(mine(cross_f), mid_f)
    grad_w_down = dot_sum(mine(active_f), cot_f)

    active = mlp_up(jnp.concatenate(after(tuple(mlp_all), grad_mid)), up)
    partial = mlp_down(tp, after(active, (grad_attn, grad_text, early_right, grad_w_cout, grad_w_down)), down)
    output = sum(part.astype(F32) for part in me.collect(partial))
    output = dot(place, (after_cross + output).astype(BF)).astype(BF)

    grad_tokens, small = in_vmem(
        functools.partial(tokens_back_kernel, tp),
        "tokens_back",
        [start, gain_a[None], grad_attn, pick.T, *after(tuple(came), partial)],
        [((seq, width), BF), ((2, width), F32)],
    )
    small = jnp.concatenate([small, grad_gain_c, grad_gain_m]).astype(BF)
    small = me.to_rows(small.reshape(4, world, own).transpose(1, 0, 2))
    small = jnp.sum(small.astype(F32), axis=0)

    text_left = jnp.einsum(
        "ihk,ikd->ihd",
        weighs.reshape(tp, 2 * local, txt),
        jnp.stack(text_rows),
        preferred_element_type=F32,
    ).astype(BF)
    count = 4 * local + 2
    lefts = jnp.concatenate(
        [
            left[:, :local],
            left[:, 8 : 8 + local],
            text_left,
            cross_entry[:, None],
            mlp_one[:, None],
        ],
        axis=1,
    )
    lefts = me.to_rows(lefts.reshape(tp * count, world, own).transpose(1, 0, 2))
    lefts = lefts.reshape(tp, 2 * planes, tp, count, own).transpose(0, 3, 1, 2, 4)
    lefts = lefts.reshape(tp, count, world, own)
    attn_left = lefts[:, : 2 * local].reshape(tp, 2, local, world, own)
    text_left = lefts[:, 2 * local : 4 * local].reshape(tp, 2, local, world, own)
    place_at = jnp.stack([me.t, corner]).astype(jnp.int32)
    held = ((0, pltpu.SMEM),)
    grad_w_kv, grad_w_cq, grad_w_up = in_vmem(
        functools.partial(cross_columns_kernel, local),
        "cross_columns",
        [place_at, text_left, lefts[:, 4 * local :], early_right],
        [((own, 2 * width), F32), ((own, width), F32), ((own, tp * ff), F32)],
        held=held,
    )
    query_zero = jnp.broadcast_to(packed[0, free : free + 1, :span], (tp, span))
    late_right, (attn_f,) = gather_factors(
        [after(grad_amix, partial), grad_q, query_zero], [grad_attn]
    )
    entry_own = lax.dynamic_slice_in_dim(entries[free], device * own, own).astype(F32)
    (grad_w_qkv,) = in_vmem(
        functools.partial(self_columns_kernel, local),
        "self_columns",
        [place_at, attn_left, entry_own[:, None], late_right],
        [((own, 3 * width), F32)],
        held=held,
    )
    grad_w_out = dot_sum(mine(mixed_f), attn_f)
    return (
        output,
        grad_tokens,
        grad_text[None],
        small[0],
        small[1],
        grad_w_qkv,
        grad_w_out,
        small[2],
        grad_w_cq,
        grad_w_kv,
        grad_w_cout,
        small[3],
        grad_w_up,
        grad_w_down,
    )


def solution(mesh):
    tp, planes = mesh.shape["dp"] // 2, mesh.shape["fsdp"]
    fine = Mesh(mesh.devices.reshape(tp, 2, planes), ("tp", "core", "fsdp"))
    every = ("tp", "core", "fsdp")
    one, two, three = P(every), P(every, None), P(every, None, None)

    def layer(*arguments):
        return shards(tp, planes, *arguments)

    return jax.shard_map(
        layer,
        mesh=fine,
        in_specs=(two, three, three, two, one, one, one, two, two, one, two, two, two, one, two, two),
        out_specs=(two, two, three, one, one, two, two, one, two, two, two, one, two, two),
        check_vma=False,
    )
```

```python
import functools

import jax
import jax.numpy as jnp
from jax import lax
from jax.experimental import pallas as pl
from jax.experimental.pallas import tpu as pltpu
from jax.sharding import Mesh, PartitionSpec as P

HEADS = 16
HDIM = 128
TILE = 128
PAD = 16
BF = jnp.bfloat16
F32 = jnp.float32
VMEM_BYTES = 60 << 20


def dot(left, right):
    return jnp.dot(left, right, preferred_element_type=F32)


def dot_t(left, right):
    return lax.dot_general(left, right, (((1,), (1,)), ((), ())), preferred_element_type=F32)


def dot_sum(left, right):
    return lax.dot_general(left, right, (((0,), (0,)), ((), ())), preferred_element_type=F32)


def normed(rows):
    centered = rows - jnp.mean(rows, axis=-1, keepdims=True)
    scale = lax.rsqrt(jnp.mean(centered * centered, axis=-1, keepdims=True) + 1e-05)
    return centered * scale, scale


def norm_back(grad, field, scale):
    return scale * (
        grad
        - jnp.mean(grad, axis=-1, keepdims=True)
        - field * jnp.mean(grad * field, axis=-1, keepdims=True)
    )


def xor_order(stack, me, size):
    bit = 1
    while bit < size:
        split = stack.reshape((size // (2 * bit), 2, bit) + stack.shape[1:])
        turned = jnp.concatenate([split[:, 1:], split[:, :1]], axis=1)
        stack = jnp.where((me & bit) != 0, turned, split).reshape(stack.shape)
        bit *= 2
    return stack


def bits_of(size):
    return [1 << k for k in range(size.bit_length() - 1)]


class Layer:
    def __init__(self, tp, planes):
        self.tp, self.planes = tp, planes
        self.t, self.c, self.z = (lax.axis_index(a) for a in ("tp", "core", "fsdp"))


    def hop(self, value, j):
        return lax.ppermute(value, "tp", [(i, i ^ j) for i in range(self.tp)])

    def other_core(self, value):
        return lax.ppermute(value, "core", [(0, 1), (1, 0)])

    def other_plane(self, value, k):
        return lax.ppermute(value, "fsdp", [(i, i ^ k) for i in range(self.planes)])

    def spread(self, value):
        return [value] + [self.hop(value, j) for j in range(1, self.tp)]

    def collect(self, parts):
        return [parts[0]] + [self.hop(parts[j], j) for j in range(1, self.tp)]

    def tp_direct(self, value):
        return jnp.stack([value] + [self.hop(value, j) for j in range(1, self.tp)])

    def tp_parts(self, value):
        return [value] + [self.hop(value, j) for j in range(1, self.tp)]

    def to_owner(self, stack):
        return [stack[0]] + [self.hop(stack[j], j) for j in range(1, self.tp)]

    def to_rows(self, value):
        return lax.all_to_all(value, ("tp", "core", "fsdp"), 0, 0, tiled=True)

    def gather_cz(self, value):
        planes = jnp.stack([value] + [self.other_plane(value, k) for k in range(1, self.planes)])
        return jnp.concatenate([planes, self.other_core(planes)])


    def shuffle(self, shards):
        return lax.all_to_all(column_blocks(self.tp, shards), "tp", 0, 0, tiled=True)

    def gather_blocks(self, shard):
        return lax.all_gather(shard, ("core", "fsdp"), axis=0)


def blocks_kernel(moves, *refs):
    for source, begin, t, at, size in moves:
        refs[-1][t, :, at : at + size] = refs[source][:, begin : begin + size]


def column_blocks(tp, shards):
    moves, at = [], 0
    for source, (shard, kinds) in enumerate(shards):
        size = shard.shape[1] // (kinds * tp)
        for kind in range(kinds):
            moves += [(source, (kind * tp + t) * size, t, at, size) for t in range(tp)]
            at += size
    rows = shards[0][0].shape[0]
    return in_vmem(
        functools.partial(blocks_kernel, moves),
        "column_blocks",
        [shard for shard, _ in shards],
        [((tp, rows, at), BF)],
    )[0]


def block(weights, t, columns):
    part = weights[:, t, :, columns]
    return part.reshape(part.shape[0] * part.shape[1], part.shape[2])


def project(rows, weights, columns):
    tp = weights.shape[1]
    step = rows.shape[1] // tp
    total = dot(rows[:, :step], block(weights, 0, columns))
    for t in range(1, tp):
        total = total + dot(rows[:, t * step : (t + 1) * step], block(weights, t, columns))
    return total


def start_copies(pairs, sems):
    copies = [pltpu.make_async_copy(a, b, sems.at[k]) for k, (a, b) in enumerate(pairs)]
    for copy in copies:
        copy.start()
    return copies


def softmax_head(queries, keys, bias, free, extra):
    scale = HDIM ** (-0.5)
    logits = dot_t(queries, keys[:free]) * scale
    if bias is not None:
        logits = logits + bias
    top = jnp.max(logits, axis=-1, keepdims=True)
    if not extra:
        weighs = jnp.exp(logits - top)
        return weighs / jnp.sum(weighs, axis=-1, keepdims=True), None
    one = dot_t(queries, keys[free:])[:, :1] * scale
    top = jnp.maximum(top, one)
    weighs, one = jnp.exp(logits - top), jnp.exp(one - top) * extra
    total = jnp.sum(weighs, axis=-1, keepdims=True) + one
    return weighs / total, one / total


def self_kernel(tp, local, count, *refs):
    entries, masked_entries, gathered = refs[:tp], refs[tp], refs[tp + 1]
    partial = refs[tp + 2 : 2 * tp + 2]
    packed, mix_out, probs_out, weight, held, mixed, sems = refs[2 * tp + 2 :]
    free, rows, span = entries[0].shape[0], packed.shape[1], local * HDIM
    pairs = [(ref, held.at[i * free : (i + 1) * free]) for i, ref in enumerate(entries)]
    pairs += [(masked_entries, held.at[tp * free :]), (gathered, weight)]
    for copy in start_copies(pairs, sems):
        copy.wait()
    for k in range(3):
        cols = slice(k * span, (k + 1) * span)
        found = project(held[...], weight, cols).astype(BF)
        for i in range(tp):
            packed[i, :free, cols] = found[i * free : (i + 1) * free]
            packed[i, free:, cols] = found[tp * free :]
    probs_out[...] = jnp.zeros_like(probs_out)
    for i in range(tp):
        for h in range(local):
            cols = [slice(k * span + h * HDIM, k * span + (h + 1) * HDIM) for k in range(3)]
            queries, keys, values = (packed[i, :, c] for c in cols)
            probs, one = softmax_head(queries, keys, None, free, float(count))
            probs_out[i, h : h + 1, :free] = probs[free : free + 1]
            probs_out[i, h : h + 1, free:] = jnp.broadcast_to(one[free : free + 1], (1, TILE))
            mixture = dot(probs.astype(BF), values[:free])
            mixture = mixture + one.astype(BF).astype(F32) * values[free : free + 1].astype(F32)
            mixed[i * rows : (i + 1) * rows, cols[0]] = mixture.astype(BF)
        mix_out[i] = mixed[i * rows + free : (i + 1) * rows]
    write_out(tp, mixed, weight, partial)


def write_out(tp, mixed, weight, partial):
    rows, width = partial[0].shape
    span = width // tp
    for t in range(tp):
        added = dot(mixed[...], block(weight, t, slice(3 * span, 4 * span))).astype(BF)
        for i in range(tp):
            partial[i][:, t * span : (t + 1) * span] = added[i * rows : (i + 1) * rows]


def masked_row(last, i, one_entry, one_row):
    last = last.astype(F32)
    one_entry[i : i + 1] = last[:1]
    one_row[i : i + 1] = last[1:2] + last[2:3] + last[3:4]


def cross_kernel(tp, local, *refs):
    entries, text = refs[:tp], refs[tp : 2 * tp]
    bias, gathered = refs[2 * tp : 2 * tp + 2]
    partial = refs[2 * tp + 2 : 3 * tp + 2]
    pair, query_out, mix_out, probs_out, one_entry, one_row = refs[3 * tp + 2 : 3 * tp + 8]
    weight, held, held_text, queries, mixed, sems = refs[3 * tp + 8 :]
    rows, txt, span = entries[0].shape[0], text[0].shape[0], local * HDIM
    free = rows - PAD
    pairs = [(ref, held_text.at[i * txt : (i + 1) * txt]) for i, ref in enumerate(text)]
    pairs += [(ref, held.at[i * rows : (i + 1) * rows]) for i, ref in enumerate(entries)]
    pairs += [(gathered, weight)]
    for copy in start_copies(pairs, sems):
        copy.wait()
    for k in range(2):
        cols = slice(k * span, (k + 1) * span)
        found = project(held_text[...], weight, cols).astype(BF)
        for i in range(tp):
            pair[i, :, cols] = found[i * txt : (i + 1) * txt]
    queries[...] = project(held[...], weight, slice(2 * span, 3 * span)).astype(BF)
    probs_out[...] = jnp.zeros_like(probs_out)
    for i in range(tp):
        masked_row(held[i * rows + free : (i + 1) * rows], i, one_entry, one_row)
        query_out[i] = queries[i * rows + free : (i + 1) * rows]
        for h in range(local):
            cols = slice(h * HDIM, (h + 1) * HDIM)
            keys = pair[i, :, cols]
            values = pair[i, :, span + h * HDIM : span + (h + 1) * HDIM]
            some = queries[i * rows : (i + 1) * rows, cols]
            probs, _ = softmax_head(some, keys, bias[i : i + 1], txt, 0)
            probs_out[i, h : h + 1] = probs[free : free + 1]
            mixed[i * rows : (i + 1) * rows, cols] = dot(probs.astype(BF), values).astype(BF)
        mix_out[i] = mixed[i * rows + free : (i + 1) * rows]
    write_out(tp, mixed, weight, partial)


def gelu_parts(value):
    slope = 0.7978845608
    bent = jnp.tanh(slope * (value + 0.044715 * value * value * value))
    half = 0.5 * (1.0 + bent)
    steep = slope * (1.0 + 3.0 * 0.044715 * value * value)
    return value * half, half + 0.5 * value * (1.0 - bent * bent) * steep


def up_kernel(entries, weight, active):
    active[...] = gelu_parts(project(entries[...], weight, slice(None)))[0].astype(BF)


def mlp_back_kernel(tp, *refs):
    entries_all, grad_active, gathered = refs[:tp], refs[tp], refs[tp + 1]
    active, grad_pre, grad_entry, one_entry, one_row, weight, last, entries, sem = refs[tp + 2 :]
    step, free = entries.shape[1] // tp, entries_all[0].shape[0] - PAD
    ends = [
        pltpu.make_async_copy(ref.at[free:], last.at[i], sem.at[tp + i])
        for i, ref in enumerate(entries_all)
    ]
    for copy in ends:
        copy.start()
    copies = [
        pltpu.make_async_copy(gathered.at[:, t], weight.at[:, t], sem.at[t]) for t in range(tp)
    ]
    for copy in copies:
        copy.start()
    for i, copy in enumerate(ends):
        copy.wait()
        masked_row(last[i], i, one_entry, one_row)
    entries[...] = jnp.zeros_like(entries)
    entries[:tp] = one_entry[...]
    hidden = jnp.zeros(active.shape, F32)
    for t, copy in enumerate(copies):
        copy.wait()
        rows = entries[:, t * step : (t + 1) * step].astype(BF)
        hidden = hidden + dot(rows, block(weight, t, slice(None)))
    value, steep = gelu_parts(hidden)
    active[...] = value.astype(BF)
    grad_pre[...] = (steep * grad_active[...]).astype(BF)
    for t in range(tp):
        back = dot_t(grad_pre[...], block(weight, t, slice(None)))
        grad_entry[:, t * step : (t + 1) * step] = back[:tp]


def summed(parts, i):
    total = parts[0][i : i + 1]
    for j in range(1, len(parts)):
        total = total + parts[j][i ^ j : (i ^ j) + 1]
    return total


def out_back(rows, weights, columns):
    tp = weights.shape[1]
    step = rows.shape[1] // tp
    total = dot_t(rows[:, :step], block(weights, 0, columns))
    for t in range(1, tp):
        total = total + dot_t(rows[:, t * step : (t + 1) * step], block(weights, t, columns))
    return total.astype(BF).astype(F32)


def head_mask(span):
    heads = lax.broadcasted_iota(jnp.int32, (8, span), 0)
    return lax.broadcasted_iota(jnp.int32, (8, span), 1) // HDIM == heads


def row_back(parts, rows, gain, base, i, out, gain_row):
    grad = summed(parts, i)
    field, scale = normed(rows[i : i + 1])
    out[i : i + 1] = base[i : i + 1] + norm_back(grad * gain[...], field, scale)
    if i == 0:
        gain_row[...] = grad * field


def cross_back_kernel(
    tp, base, rows, gain, pair, probs, gathered, *refs,
):
    parts = refs[:tp]
    grad_mid, grad_cmix, scores, grad_cq, grad_entry, gain_row = refs[tp : tp + 6]
    weight, held, sems = refs[tp + 6 :]
    span = weight.shape[3] // 2
    copies = [
        pltpu.make_async_copy(gathered.at[:, :, :, 2 * span :], weight, sems.at[0]),
    ]
    for copy in copies:
        copy.start()
    held[...] = jnp.zeros_like(held)
    for i in range(tp):
        row_back(parts, rows, gain, base, i, held, gain_row)
    grad_mid[...] = held[:tp]
    copies[0].wait()
    mixed = out_back(held[...].astype(BF), weight, slice(span, 2 * span))
    grad_cmix[...] = mixed[:tp]
    mask = head_mask(span)
    held[...] = jnp.zeros_like(held)
    for i in range(tp):
        spread = jnp.where(mask, mixed[i : i + 1], 0.0).astype(BF)
        grad_probs = dot_t(spread, pair[i, :, span:])
        weighs = probs[i]
        grad = weighs * (grad_probs - jnp.sum(grad_probs * weighs, axis=-1, keepdims=True))
        grad = grad.astype(BF)
        scores[i] = grad.astype(F32)
        back = jnp.where(mask, dot(grad, pair[i, :, :span]), 0.0)
        held[i : i + 1, :span] = jnp.sum(back, axis=0, keepdims=True) * HDIM ** (-0.5)
    grad_cq[...] = held[:tp, :span]
    queries = held[:, :span].astype(BF)
    step = grad_entry.shape[1] // tp
    for t in range(tp):
        back = dot_t(queries, block(weight, t, slice(0, span)))
        grad_entry[:, t * step : (t + 1) * step] = back[:tp]


def spread_heads(rows, i, spreads, mask):
    spreads[8 * i : 8 * i + 8] = jnp.where(mask, rows, 0.0)


def text_back_kernel(tp, local, *refs):
    scores, probs, query_one, grad_cmix, kvq = refs[:5]
    cross_one_row, mlp_one, grad_pre, grad_cq, mixed, cross, active, base, grad_mid = refs[5:14]
    text = refs[14 : 14 + tp]
    sent = refs[14 + tp : 14 + 2 * tp]
    lefts, factors, weight, held, keys, values, sems = refs[14 + 2 * tp :]
    span, width, txt = grad_cmix.shape[1], lefts.shape[1], scores.shape[2]
    copy = pltpu.make_async_copy(kvq.at[:, :, :, : 2 * span], weight, sems.at[0])
    copy.start()
    mask = head_mask(span)
    ff = grad_pre.shape[1]
    places, at = [], 0
    for size in (ff, span, span, span, span, span, ff, width, width):
        places.append(slice(at, at + size))
        at += size
    for i in range(tp):
        spread_heads(query_one[i].astype(F32)[:1], i, keys, mask)
        spread_heads(grad_cmix[i : i + 1], i, values, mask)
        both = jnp.concatenate([scores[i], probs[i]], axis=0).astype(BF)
        found = dot(both, text[i][...])
        for kind in range(2):
            begin = (2 * i + kind) * local
            lefts[begin : begin + local] = found[8 * kind : 8 * kind + local]
        sent[i][:, width:] = both
        for k, rows in ((2, query_one), (4, mixed), (5, cross)):
            held[i : i + 1, places[k]] = rows[i].astype(F32)[:1]
    held[:tp, places[0]] = grad_pre[...].astype(F32)[:tp]
    held[:tp, places[1]] = grad_cq[...]
    held[:tp, places[3]] = grad_cmix[...]
    held[:tp, places[6]] = active[...].astype(F32)[:tp]
    held[:tp, places[7]] = base[...]
    held[:tp, places[8]] = grad_mid[...]
    factors[...] = held[:tp].astype(BF)
    begin = 2 * tp * local
    lefts[begin : begin + tp] = cross_one_row[...]
    lefts[begin + tp :] = mlp_one[...]
    copy.wait()
    step = width // tp
    key_spread, value_spread = keys[...].astype(BF), values[...].astype(BF)
    for t in range(tp):
        cols = slice(t * step, (t + 1) * step)
        key_rows = dot_t(key_spread, block(weight, t, slice(0, span))) * HDIM ** (-0.5)
        value_rows = dot_t(value_spread, block(weight, t, slice(span, 2 * span)))
        for i in range(tp):
            eight = slice(8 * i, 8 * i + 8)
            both = jnp.concatenate([key_rows[eight], value_rows[eight]], axis=0)
            sent[i][:, cols] = both.astype(BF)


def self_back_kernel(
    tp, local, base, rows, gain, packed, probs, masked_entries, text_lefts, gathered, *refs,
):
    parts, entries, refs = refs[:tp], refs[tp : 2 * tp], refs[tp:]
    sent = refs[tp : 2 * tp]
    grad_attn, gain_row, payload, factors = refs[2 * tp : 2 * tp + 4]
    weight, held, spreads, lefts, sems = refs[2 * tp + 4 :]
    width = lefts.shape[1]
    span, free = weight.shape[3] // 4, entries[0].shape[0]
    copies = [pltpu.make_async_copy(gathered, weight, sems.at[0])]
    for copy in copies:
        copy.start()
    held[...] = jnp.zeros_like(held)
    for i in range(tp):
        row_back(parts, rows, gain, base, i, held, gain_row)
    grad_attn[...] = held[:tp]
    copies[0].wait()
    mixed = out_back(held[...].astype(BF), weight, slice(3 * span, 4 * span))
    factors[:, :span] = mixed[:tp].astype(BF)
    factors[:, 3 * span :] = grad_attn[...].astype(BF)
    mask = head_mask(span)
    held[...] = jnp.zeros_like(held)
    first = lax.broadcasted_iota(jnp.int32, (PAD, TILE), 1) == 0
    only = first & (lax.broadcasted_iota(jnp.int32, (PAD, TILE), 0) == 0)
    masked_row = masked_entries[:1].astype(F32)
    for i in range(tp):
        spread = jnp.where(mask, mixed[i : i + 1], 0.0)
        spreads[8 * i : 8 * i + 8] = spread
        spread = spread.astype(BF)
        values = packed[i, :, 2 * span :]
        grad_probs, grad_one = dot_t(spread, values[:free]), dot_t(spread, values[free:])[:, :1]
        weighs, one = probs[i, :, :free], probs[i, :, free : free + 1]
        mean = jnp.sum(grad_probs * weighs, axis=-1, keepdims=True) + grad_one * one
        grad = (weighs * (grad_probs - mean)).astype(BF)
        grad_one = (one * (grad_one - mean)).astype(BF).astype(F32)
        keys = packed[i, :, span : 2 * span]
        back = dot(grad, keys[:free]) + grad_one * keys[free : free + 1].astype(F32)
        back = jnp.sum(jnp.where(mask, back, 0.0), axis=0, keepdims=True)
        held[i : i + 1, :span] = back * HDIM ** (-0.5)
        both = jnp.concatenate([grad.astype(F32), weighs], axis=0).astype(BF)
        both_one = jnp.concatenate([grad_one, one], axis=0).astype(BF).astype(F32)
        found = dot(both, entries[i][...]) + both_one * masked_row
        for kind in range(2):
            begin = (2 * i + kind) * local
            lefts[begin : begin + local] = found[8 * kind : 8 * kind + local]
        sent[i][:PAD, width : width + free] = both
        sent[i][:PAD, width + free :] = jnp.where(first, both_one, 0.0).astype(BF)
        sent[i][PAD:, width : width + free] = jnp.zeros((PAD, free), BF)
        sent[i][PAD:, width + free :] = jnp.where(only, 1.0, 0.0).astype(BF)
    lefts[2 * tp * local :] = text_lefts[...]
    own_width = payload.shape[2]
    for d in range(payload.shape[0]):
        payload[d] = lefts[:, d * own_width : (d + 1) * own_width].astype(BF)
    factors[:, span : 2 * span] = held[:tp, :span].astype(BF)
    queries = held[:, :span].astype(BF)
    zero_query = packed[0, free:, :span].astype(F32)[:1]
    factors[:, 2 * span : 3 * span] = jnp.broadcast_to(zero_query, (tp, span)).astype(BF)
    key_spread = jnp.where(mask, zero_query, 0.0).astype(BF)
    value_spread = spreads[...].astype(BF)
    step = width // tp
    empty = jnp.zeros((PAD - 1, step), F32)
    for t in range(tp):
        cols = slice(t * step, (t + 1) * step)
        keys = dot_t(key_spread, block(weight, t, slice(span, 2 * span))) * HDIM ** (-0.5)
        values = dot_t(value_spread, block(weight, t, slice(2 * span, 3 * span)))
        query_rows = dot_t(queries, block(weight, t, slice(0, span)))
        for i in range(tp):
            both = jnp.concatenate([keys, values[8 * i : 8 * i + 8]], axis=0)
            sent[i][:PAD, cols] = both.astype(BF)
            last = jnp.concatenate([query_rows[i : i + 1], empty], axis=0)
            sent[i][PAD:, cols] = last.astype(BF)


def tokens_back_kernel(tp, rows, gain, base, place, gain_c, gain_m, *refs):
    came, came_text, (tokens, text, payload, small) = refs[:tp], refs[tp : 2 * tp], refs[2 * tp :]
    width, free = rows.shape[1], place.shape[1]
    grad, grad_one, grad_text = 0.0, 0.0, 0.0
    for part, text_part in zip(came, came_text):
        back = part[:, :width]
        grad = grad + dot_sum(part[:, width : width + free], back)
        grad_one = grad_one + dot_sum(part[:, width + free :], back)[:1]
        grad_text = grad_text + dot_sum(text_part[:, width:], text_part[:, :width])
    text[...] = grad_text.astype(BF)
    field, scale = normed(rows[:free])
    start = norm_back(grad * gain[...], field, scale)
    tokens[...] = dot(place[...], start.astype(BF)).astype(BF)
    one_field, one_scale = normed(rows[free : free + 1])
    start = norm_back(grad_one * gain[...], one_field, one_scale)
    small[...] = jnp.zeros_like(small)
    small[0:1] = base[0:1] + start
    small[1:2] = jnp.sum(grad * field, axis=0, keepdims=True) + grad_one * one_field
    small[2:3] = gain_c[...]
    small[3:4] = gain_m[...]
    own = payload.shape[2]
    for d in range(payload.shape[0]):
        payload[d] = small[:, d * own : (d + 1) * own]


def stack_kernel(*refs):
    for k, ref in enumerate(refs[:-1]):
        refs[-1][k] = ref[...]


def unpack_kernel(planes, others, right, group, held):
    count, tp = planes.shape[:2]
    for k in range(count):
        held[k * tp : (k + 1) * tp] = planes[k].astype(F32)
        held[(count + k) * tp : (count + k + 1) * tp] = others[k].astype(F32)
    right[...] = held[:, : right.shape[1]].astype(BF)
    group[...] = held[:, right.shape[1] :].astype(BF)


def aligned(right, corner, tp):
    count = right.shape[0]
    out = lax.broadcasted_iota(jnp.int32, (count, count), 0)
    into = lax.broadcasted_iota(jnp.int32, (count, count), 1)
    same = (out // tp == (corner ^ (into // tp))) & (out % tp == into % tp)
    return dot(same.astype(BF), right).astype(BF)


def cross_columns_kernel(local, place, text_left, one_left, *refs):
    right, (grad_kv, grad_cq, grad_up) = refs[:-3], refs[-3:]
    tp, span = len(right), local * HDIM
    ff = right[0].shape[1] - 3 * span
    for j in range(tp):
        at = place[0] ^ j
        rows = aligned(right[j][...], place[1], tp)
        columns = pl.ds(pl.multiple_of(at * span, span), span)
        grad_cq[:, columns] = dot_sum(one_left[at, 0], rows[:, ff : ff + span])
        wide = pl.ds(pl.multiple_of(at * ff, ff), ff)
        grad_up[:, wide] = dot_sum(one_left[at, 1], rows[:, :ff])
        for h in range(local):
            for kind in range(2):
                start = ff + (1 + kind) * span + h * HDIM
                outer = dot_sum(text_left[at, kind, h], rows[:, start : start + HDIM])
                if kind == 0:
                    outer = outer * HDIM ** (-0.5)
                begin = kind * tp * span + at * span + h * HDIM
                grad_kv[:, pl.ds(pl.multiple_of(begin, HDIM), HDIM)] = outer


def self_columns_kernel(local, place, left, entry, *refs):
    right, grad_qkv = refs[:-1], refs[-1]
    tp, span = len(right), local * HDIM
    ones = jnp.ones((right[0].shape[0], HDIM), BF)
    for j in range(tp):
        at = place[0] ^ j
        rows = aligned(right[j][:, :span], place[1], tp)
        total = jnp.sum(right[j][:, span : 2 * span].astype(F32), axis=0, keepdims=True)
        queries = right[j][:, 2 * span :].astype(F32)[:1] * HDIM ** (-0.5)
        grad_qkv[:, pl.ds(pl.multiple_of(at * span, span), span)] = entry[...] * total
        for h in range(local):
            cols = slice(h * HDIM, (h + 1) * HDIM)
            keys = dot_sum(left[at, 0, h], ones) * queries[:, cols]
            begin = tp * span + at * span + h * HDIM
            grad_qkv[:, pl.ds(pl.multiple_of(begin, HDIM), HDIM)] = keys
            begin = 2 * tp * span + at * span + h * HDIM
            values = dot_sum(left[at, 1, h], rows[:, cols])
            grad_qkv[:, pl.ds(pl.multiple_of(begin, HDIM), HDIM)] = values


def whole_spec():
    return pl.BlockSpec(memory_space=pl.ANY)


def in_vmem(kernel, name, operands, out_shape, scratch_shapes=(), held=()):
    spaces = dict(held)
    return pl.pallas_call(
        kernel,
        in_specs=[
            pl.BlockSpec(memory_space=spaces.get(k, pltpu.VMEM)) for k in range(len(operands))
        ],
        out_specs=[pl.BlockSpec(memory_space=pltpu.VMEM)] * len(out_shape),
        out_shape=[jax.ShapeDtypeStruct(shape, dtype) for shape, dtype in out_shape],
        scratch_shapes=scratch_shapes,
        compiler_params=pltpu.CompilerParams(vmem_limit_bytes=VMEM_BYTES),
        name=name,
    )(*operands)


def self_forward(local, count, entries, masked_entries, gathered):
    tp, (free, width) = len(entries), entries[0].shape
    span, rows = local * HDIM, free + PAD
    found = in_vmem(
        functools.partial(self_kernel, tp, local, count),
        "self_attention",
        [*entries, masked_entries, gathered],
        [((rows, width), BF)] * tp
        + [((tp, rows, 3 * span), BF), ((tp, PAD, span), BF), ((tp, 8, free + TILE), F32)],
        [
            pltpu.VMEM(gathered.shape, BF),
            pltpu.VMEM((tp * free + PAD, width), BF),
            pltpu.VMEM((tp * rows, span), BF),
            pltpu.SemaphoreType.DMA((tp + 2,)),
        ],
        [(k, pl.ANY) for k in range(tp + 2)],
    )
    return found[:tp], *found[tp:]


def cross_forward(local, entries, text, bias, gathered):
    tp, (rows, width) = len(entries), entries[0].shape
    txt, span = text[0].shape[0], local * HDIM
    found = in_vmem(
        functools.partial(cross_kernel, tp, local),
        "cross_attention",
        [*entries, *text, bias, gathered],
        [((rows, width), BF)] * tp
        + [
            ((tp, txt, 2 * span), BF),
            ((tp, PAD, span), BF),
            ((tp, PAD, span), BF),
            ((tp, 8, txt), F32),
            ((tp, width), F32),
            ((tp, width), F32),
        ],
        [
            pltpu.VMEM(gathered.shape, BF),
            pltpu.VMEM((tp * rows, width), BF),
            pltpu.VMEM((tp * txt, width), BF),
            pltpu.VMEM((tp * rows, span), BF),
            pltpu.VMEM((tp * rows, span), BF),
            pltpu.SemaphoreType.DMA((2 * tp + 1,)),
        ],
        [(k, pl.ANY) for k in range(2 * tp + 2) if k != 2 * tp],
    )
    return found[:tp], *found[tp:]


def down_kernel(tp, active, weight, *partial):
    rows = partial[0].shape[0]
    part = weight[...]
    added = dot(active[...], part.reshape(-1, part.shape[2])).astype(BF)
    for i in range(tp):
        partial[i][...] = added[i * rows : (i + 1) * rows]


def mlp_down(tp, active, gathered):
    blocks, own, width = gathered.shape
    rows, step = active.shape[0] // tp, 512
    return pl.pallas_call(
        functools.partial(down_kernel, tp),
        grid=(width // step,),
        in_specs=[
            pl.BlockSpec(active.shape, lambda i: (0, 0)),
            pl.BlockSpec((blocks, own, step), lambda i: (0, 0, i)),
        ],
        out_specs=[pl.BlockSpec((rows, step), lambda i: (0, i))] * tp,
        out_shape=[jax.ShapeDtypeStruct((rows, width), BF)] * tp,
        compiler_params=pltpu.CompilerParams(vmem_limit_bytes=VMEM_BYTES),
        name="mlp_down",
    )(active, gathered)


def mlp_up(entries, gathered):
    rows, width = entries.shape
    blocks, tp, own, ff = gathered.shape
    step = min(ff, 512)
    return pl.pallas_call(
        up_kernel,
        grid=(ff // step,),
        in_specs=[
            pl.BlockSpec((rows, width), lambda i: (0, 0)),
            pl.BlockSpec((blocks, tp, own, step), lambda i: (0, 0, 0, i)),
        ],
        out_specs=pl.BlockSpec((rows, step), lambda i: (0, i)),
        out_shape=jax.ShapeDtypeStruct((rows, ff), BF),
        compiler_params=pltpu.CompilerParams(vmem_limit_bytes=VMEM_BYTES),
        name="mlp_up",
    )(entries, gathered)


def mlp_back(entries, grad_active, gathered):
    tp, width = len(entries), entries[0].shape[1]
    ff = gathered.shape[3]
    return in_vmem(
        functools.partial(mlp_back_kernel, tp),
        "mlp_back",
        [*entries, grad_active, gathered],
        [
            ((PAD, ff), BF),
            ((PAD, ff), BF),
            ((tp, width), F32),
            ((tp, width), F32),
            ((tp, width), F32),
        ],
        [
            pltpu.VMEM(gathered.shape, BF),
            pltpu.VMEM((tp, PAD, width), BF),
            pltpu.VMEM((PAD, width), F32),
            pltpu.SemaphoreType.DMA((2 * tp,)),
        ],
        [(k, pl.ANY) for k in range(tp + 2) if k != tp],
    )


def cross_back(base, rows, gain, pair, probs, gathered, parts):
    tp, width = base.shape
    blocks, _, own, columns = gathered.shape
    span = columns // 4
    return in_vmem(
        functools.partial(cross_back_kernel, tp),
        "cross_back",
        [base, rows, gain[None], pair, probs, gathered, *parts],
        [
            ((tp, width), F32),
            ((tp, span), F32),
            (probs.shape, F32),
            ((tp, span), F32),
            ((tp, width), F32),
            ((1, width), F32),
        ],
        [
            pltpu.VMEM((blocks, tp, own, 2 * span), BF),
            pltpu.VMEM((8, width), F32),
            pltpu.SemaphoreType.DMA((1,)),
        ],
        ((5, pl.ANY),),
    )


def text_back(local, scores, probs, query_one, grad_cmix, kvq, rest, text):
    tp, span = grad_cmix.shape
    blocks, _, own, _ = kvq.shape
    (txt, width), ff = text[0].shape, rest[2].shape[1]
    found = in_vmem(
        functools.partial(text_back_kernel, tp, local),
        "text_back",
        [scores, probs, query_one, grad_cmix, kvq, *rest, *text],
        [((PAD, width + txt), BF)] * tp
        + [((2 * tp * (local + 1), width), F32), ((tp, 2 * ff + 5 * span + 2 * width), BF)],
        [
            pltpu.VMEM((blocks, tp, own, 2 * span), BF),
            pltpu.VMEM((8, 2 * ff + 5 * span + 2 * width), F32),
            pltpu.VMEM((8 * tp, span), F32),
            pltpu.VMEM((8 * tp, span), F32),
            pltpu.SemaphoreType.DMA((1,)),
        ],
        ((4, pl.ANY),),
    )
    return found[:tp], *found[tp:]


def self_back(local, world, base, rows, gain, packed, probs, masked_entries, text_lefts, gathered, parts, entries):
    tp, width = base.shape
    _, _, own, columns = gathered.shape
    span, free = columns // 4, entries[0].shape[0]
    count = 2 * tp * (2 * local + 1)
    found = in_vmem(
        functools.partial(self_back_kernel, tp, local),
        "self_back",
        [base, rows, gain[None], packed, probs, masked_entries, text_lefts, gathered, *parts, *entries],
        [((2 * PAD, width + free + TILE), BF)] * tp
        + [
            ((tp, width), F32),
            ((1, width), F32),
            ((world, count, own), BF),
            ((tp, 3 * span + width), BF),
        ],
        [
            pltpu.VMEM(gathered.shape, BF),
            pltpu.VMEM((8, width), F32),
            pltpu.VMEM((8 * tp, span), F32),
            pltpu.VMEM((count, width), F32),
            pltpu.SemaphoreType.DMA((1,)),
        ],
        ((7, pl.ANY),),
    )
    return found[:tp], *found[tp:]


def stacked(pieces):
    shape = (len(pieces),) + pieces[0].shape
    return in_vmem(stack_kernel, "stack", pieces, [(shape, BF)])[0]


def unpack(planes, others, cut):
    count, tp, wide = planes.shape
    rows = 2 * count * tp
    return in_vmem(
        unpack_kernel,
        "unpack",
        [planes, others],
        [((rows, cut), BF), ((rows, wide - cut), BF)],
        [pltpu.VMEM((rows, wide), F32)],
    )


def join_kernel(free, base, gain, *refs):
    parts, (total, entries) = refs[:-2], refs[-2:]
    value = base[...]
    for part in parts:
        value = value + part[...].astype(F32)
    total[...] = value
    found = normed(value)[0] * gain[...]
    entries[...] = found.astype(BF)

    @pl.when(pl.program_id(0) == pl.num_programs(0) - 1)
    def _():
        at = value.shape[0] - PAD
        row = value[at : at + 1]
        spot = lax.broadcasted_iota(jnp.int32, (PAD, value.shape[1]), 0)
        last = found[at:]
        for k in range(3):
            part = row.astype(BF).astype(F32)
            last = jnp.where(spot == k + 1, part, last)
            row = row - part
        entries[at:] = last.astype(BF)


def join(base, parts, gain):
    rows, width = base.shape
    step = PAD * 3 if rows % (PAD * 3) == 0 else PAD
    block = pl.BlockSpec((step, width), lambda i: (i, 0))
    return pl.pallas_call(
        functools.partial(join_kernel, rows - PAD),
        grid=(rows // step,),
        in_specs=[block, pl.BlockSpec((1, width), lambda i: (0, 0))] + [block] * len(parts),
        out_specs=[block, block],
        out_shape=[
            jax.ShapeDtypeStruct((rows, width), F32),
            jax.ShapeDtypeStruct((rows, width), BF),
        ],
        compiler_params=pltpu.CompilerParams(vmem_limit_bytes=VMEM_BYTES),
        name="join",
    )(base, gain[None], *parts)


def shards(
    tp,
    planes,
    tokens,
    text,
    cotangent,
    positions,
    text_lengths,
    mask_embed,
    gain_attn,
    w_qkv,
    w_attn_out,
    gain_cross,
    w_cross_q,
    w_cross_kv,
    w_cross_out,
    gain_mlp,
    w_up,
    w_down,
):
    me = Layer(tp, planes)
    seq, width = tokens.shape
    masked_count = positions.shape[1]
    free = seq - masked_count
    txt = text.shape[1]
    local = HEADS // tp
    rows = free + PAD
    device = (me.t * 2 + me.c) * planes + me.z
    world = tp * 2 * planes
    own = width // world

    def after(value, earlier):
        return lax.optimization_barrier((value, earlier))[0]

    span = local * HDIM

    qkv_sent = me.shuffle([(w_qkv, 3)])
    attn_w = jnp.concatenate([qkv_sent, column_blocks(tp, [(w_attn_out, 1)])], axis=2)
    attn_w = me.gather_blocks(attn_w)

    def natural(value):
        split = value.reshape(value.shape[:-1] + (2 * planes, tp, own))
        return split.swapaxes(-3, -2).reshape(value.shape)

    cot_sum = jnp.sum(cotangent[0].astype(F32), axis=0)
    vectors = jnp.concatenate([mask_embed, gain_attn, gain_cross, gain_mlp]).astype(F32)
    fill = TILE - vectors.shape[0] % TILE
    length = jnp.broadcast_to(text_lengths.astype(F32), (fill,))
    gathered = me.tp_direct(me.gather_cz(jnp.concatenate([cot_sum, vectors, length])))
    others = after((w_cross_kv, w_cross_q, w_cross_out), (gathered, qkv_sent))
    kvq_sent = me.shuffle([(others[0], 2), (others[1], 1)])
    cross_sent = jnp.concatenate([kvq_sent, column_blocks(tp, [(others[2], 1)])], axis=2)
    vectors = gathered[:, :, width : width + 4 * own].reshape(world, 4, own)
    vectors = xor_order(vectors, device, world).transpose(1, 0, 2).reshape(4, width)
    embed, gain_a, gain_c, gain_m = vectors[0], vectors[1], vectors[2], vectors[3]
    lengths = gathered[:, 0, width + 4 * own :][:, :1]
    text_bias = jnp.where(
        lax.broadcasted_iota(jnp.int32, (tp, txt), 1).astype(F32) < lengths, 0.0, -1e30
    )
    cot_group = gathered[:, 0, :width]

    spots = lax.broadcasted_iota(jnp.int32, (masked_count, seq), 1)
    masked = jnp.sum((positions[0][:, None] == spots).astype(F32), axis=0)
    below = lax.broadcasted_iota(jnp.int32, (seq, seq), 0) <= lax.broadcasted_iota(
        jnp.int32, (seq, seq), 1
    )
    rank = dot((1.0 - masked).astype(BF)[None, :], below.astype(BF))[0]
    ranks = lax.broadcasted_iota(jnp.int32, (free, seq), 0).astype(F32) + 1.0
    pick = ((rank[None, :] == ranks) & (masked[None, :] == 0.0)).astype(BF)
    place = jnp.concatenate(
        [pick.T, masked[:, None].astype(BF), jnp.zeros((seq, PAD - 1), BF)], axis=1
    )
    start_free = dot(pick, tokens)
    start = jnp.concatenate([start_free, jnp.broadcast_to(embed[None], (PAD, width))])

    cot_rows = gathered[:, :, :width].reshape(world, width)
    high = cot_rows.astype(BF)
    low = (cot_rows - high.astype(F32)).astype(BF)
    through = dot_t(jnp.concatenate([high, low]), w_down)
    through = through[:world] + through[world:]
    through = through.reshape(tp, 2 * planes, -1).transpose(1, 0, 2)
    through = xor_order(through, me.c * planes + me.z, 2 * planes)
    through = lax.all_to_all(after(through, kvq_sent), ("core", "fsdp"), 0, 0, tiled=True)
    grad_active = through.transpose(1, 0, 2).reshape(tp, -1)

    field_a, scale_a = normed(start)
    entries = (field_a * gain_a[None]).astype(BF)
    entries_all = me.spread(entries[:free])
    text_rows = me.spread(after(text[0], entries_all))
    up_sent = me.shuffle([(after(w_up, (entries_all, kvq_sent)), 1)])
    cross_w = me.gather_blocks(after(cross_sent, (attn_w, entries_all, up_sent)))
    partial, packed, mixed_one, probs_one = self_forward(
        local, masked_count, entries_all, entries[free:], attn_w
    )
    after_attn, cross_entries = join(after(start, (grad_active, place)), me.collect(after(tuple(partial), text_rows)), gain_c)

    cross_all = me.spread(cross_entries)
    up = me.gather_blocks(after(up_sent, (cross_w, cross_all)))
    partial, pair, query_one, cross_one, cross_probs_one, cross_entry, attn_stream = cross_forward(
        local, cross_all, text_rows, text_bias, cross_w
    )
    after_cross, mlp_entries = join(after_attn, me.collect(partial), gain_m)

    mlp_all = me.spread(mlp_entries)
    down = me.gather_blocks(after(w_down, (up, mlp_all)))

    active_one, grad_pre, grad_entry, mlp_one, cross_stream = mlp_back(
        mlp_all, jnp.pad(grad_active, ((0, PAD - tp), (0, 0))), up
    )
    grad_mid, grad_cmix, scores, grad_cq, grad_entry, grad_gain_m = cross_back(
        cot_group, cross_stream, gain_m, pair, cross_probs_one, cross_w, me.tp_parts(grad_entry)
    )
    text_sent, text_lefts, early_factors = text_back(
        local,
        scores,
        cross_probs_one,
        query_one,
        grad_cmix,
        cross_w,
        [
            cross_entry,
            mlp_one,
            grad_pre,
            grad_cq,
            mixed_one,
            cross_one,
            active_one,
            cot_group,
            grad_mid,
        ],
        text_rows,
    )
    sent, grad_attn, grad_gain_c, payload, late_factors = self_back(
        local,
        world,
        grad_mid,
        attn_stream,
        gain_c,
        packed,
        probs_one,
        entries[free:],
        text_lefts,
        attn_w,
        me.tp_parts(grad_entry),
        entries_all,
    )
    came = me.to_owner(sent)
    came_text = me.to_owner(text_sent)

    corner = me.c * planes + me.z
    ff = grad_pre.shape[1]

    def gather_factors(factors, cut):
        planes_of = stacked([factors] + [me.other_plane(factors, k) for k in range(1, planes)])
        right, group = unpack(planes_of, me.other_core(planes_of), cut)
        return [right] + [me.hop(right, j) for j in range(1, tp)], group

    def mine(stack):
        size = stack.shape[1] // (2 * planes)
        return lax.dynamic_slice_in_dim(stack, corner * size, size, axis=1)

    early_right, group = gather_factors(early_factors, ff + 3 * span)
    cuts = [span, 2 * span, 2 * span + ff, 2 * span + ff + width]
    mixed_f, cross_f, active_f, cot_f, mid_f = jnp.split(group, cuts, axis=1)
    grad_w_cout = dot_sum(mine(cross_f), mid_f)
    grad_w_down = dot_sum(mine(active_f), cot_f)

    late_right, attn_f = gather_factors(late_factors, 3 * span)
    lefts = me.to_rows(payload)

    active = mlp_up(jnp.concatenate(after(tuple(mlp_all), grad_attn)), up)
    partial = mlp_down(tp, after(active, (early_right, late_right, lefts)), down)
    output = sum(part.astype(F32) for part in me.collect(partial))
    output = dot(place, (after_cross + output).astype(BF)).astype(BF)

    grad_tokens, grad_text, small = in_vmem(
        functools.partial(tokens_back_kernel, tp),
        "tokens_back",
        [start, gain_a[None], grad_attn, pick.T, grad_gain_c, grad_gain_m, *after(tuple(came), partial), *came_text],
        [((seq, width), BF), ((txt, width), BF), ((world, 8, own), F32)],
        [pltpu.VMEM((8, width), F32)],
    )
    small = jnp.sum(me.to_rows(small), axis=0)

    heads = 2 * tp * local
    lefts = after(lefts, partial)
    attn_left, text_left = (
        lefts[:, k * heads : (k + 1) * heads]
        .reshape(tp, 2 * planes, tp, 2, local, own)
        .transpose(0, 3, 4, 1, 2, 5)
        .reshape(tp, 2, local, world, own)
        for k in range(2)
    )
    one_left = lefts[:, 2 * heads :].reshape(tp, 2 * planes, 2, tp, own)
    one_left = one_left.transpose(0, 2, 1, 3, 4).reshape(tp, 2, world, own)
    place_at = jnp.stack([me.t, corner]).astype(jnp.int32)
    held = ((0, pltpu.SMEM),)
    grad_w_kv, grad_w_cq, grad_w_up = in_vmem(
        functools.partial(cross_columns_kernel, local),
        "cross_columns",
        [place_at, text_left, one_left, *early_right],
        [((own, 2 * width), F32), ((own, width), F32), ((own, tp * ff), F32)],
        held=held,
    )
    entry_own = lax.dynamic_slice_in_dim(entries[free], device * own, own).astype(F32)
    (grad_w_qkv,) = in_vmem(
        functools.partial(self_columns_kernel, local),
        "self_columns",
        [place_at, attn_left, entry_own[:, None], *late_right],
        [((own, 3 * width), F32)],
        held=held,
    )
    grad_w_out = dot_sum(mine(mixed_f), attn_f)
    return (
        output,
        grad_tokens,
        grad_text[None],
        small[0],
        small[1],
        grad_w_qkv,
        grad_w_out,
        small[2],
        grad_w_cq,
        grad_w_kv,
        grad_w_cout,
        small[3],
        grad_w_up,
        grad_w_down,
    )


def solution(mesh):
    tp, planes = mesh.shape["dp"] // 2, mesh.shape["fsdp"]
    fine = Mesh(mesh.devices.reshape(tp, 2, planes), ("tp", "core", "fsdp"))
    every = ("tp", "core", "fsdp")
    one, two, three = P(every), P(every, None), P(every, None, None)

    def layer(*arguments):
        return shards(tp, planes, *arguments)

    return jax.shard_map(
        layer,
        mesh=fine,
        in_specs=(two, three, three, two, one, one, one, two, two, one, two, two, two, one, two, two),
        out_specs=(two, two, three, one, one, two, two, one, two, two, two, one, two, two),
        check_vma=False,
    )
```

```python
import functools

import jax
import jax.numpy as jnp
from jax import lax
from jax.experimental import pallas as pl
from jax.experimental.pallas import tpu as pltpu
from jax.sharding import Mesh, PartitionSpec as P

HEADS = 16
HDIM = 128
TILE = 128
PAD = 16
BF = jnp.bfloat16
F32 = jnp.float32
VMEM_BYTES = 60 << 20
COST = pl.CostEstimate(flops=1, bytes_accessed=1, transcendentals=0)


def dot(left, right):
    return jnp.dot(left, right, preferred_element_type=F32)


def dot_t(left, right):
    return lax.dot_general(left, right, (((1,), (1,)), ((), ())), preferred_element_type=F32)


def dot_sum(left, right):
    return lax.dot_general(left, right, (((0,), (0,)), ((), ())), preferred_element_type=F32)


def normed(rows):
    centered = rows - jnp.mean(rows, axis=-1, keepdims=True)
    scale = lax.rsqrt(jnp.mean(centered * centered, axis=-1, keepdims=True) + 1e-05)
    return centered * scale, scale


def norm_back(grad, field, scale):
    return scale * (
        grad
        - jnp.mean(grad, axis=-1, keepdims=True)
        - field * jnp.mean(grad * field, axis=-1, keepdims=True)
    )


def xor_order(stack, me, size):
    bit = 1
    while bit < size:
        split = stack.reshape((size // (2 * bit), 2, bit) + stack.shape[1:])
        turned = jnp.concatenate([split[:, 1:], split[:, :1]], axis=1)
        stack = jnp.where((me & bit) != 0, turned, split).reshape(stack.shape)
        bit *= 2
    return stack


def bits_of(size):
    return [1 << k for k in range(size.bit_length() - 1)]


class Layer:
    def __init__(self, tp, planes):
        self.tp, self.planes = tp, planes
        self.t, self.c, self.z = (lax.axis_index(a) for a in ("tp", "core", "fsdp"))


    def hop(self, value, j):
        return lax.ppermute(value, "tp", [(i, i ^ j) for i in range(self.tp)])

    def other_core(self, value):
        return lax.ppermute(value, "core", [(0, 1), (1, 0)])

    def other_plane(self, value, k):
        return lax.ppermute(value, "fsdp", [(i, i ^ k) for i in range(self.planes)])

    def spread(self, value):
        return [value] + [self.hop(value, j) for j in range(1, self.tp)]

    def collect(self, parts):
        return [parts[0]] + [self.hop(parts[j], j) for j in range(1, self.tp)]

    def tp_direct(self, value):
        return jnp.stack([value] + [self.hop(value, j) for j in range(1, self.tp)])

    def tp_parts(self, value):
        return [value] + [self.hop(value, j) for j in range(1, self.tp)]

    def to_owner(self, stack):
        return [stack[0]] + [self.hop(stack[j], j) for j in range(1, self.tp)]

    def to_rows(self, value):
        return lax.all_to_all(value, ("tp", "core", "fsdp"), 0, 0, tiled=True)

    def gather_cz(self, value):
        planes = jnp.stack([value] + [self.other_plane(value, k) for k in range(1, self.planes)])
        return jnp.concatenate([planes, self.other_core(planes)])


    def shuffle(self, shards):
        return lax.all_to_all(column_blocks(self.tp, shards), "tp", 0, 0, tiled=True)

    def gather_blocks(self, shard):
        return lax.all_gather(shard, ("core", "fsdp"), axis=0)


def blocks_kernel(moves, *refs):
    for source, begin, t, at, size in moves:
        refs[-1][t, :, at : at + size] = refs[source][:, begin : begin + size]


def column_blocks(tp, shards):
    moves, at = [], 0
    for source, (shard, kinds) in enumerate(shards):
        size = shard.shape[1] // (kinds * tp)
        for kind in range(kinds):
            moves += [(source, (kind * tp + t) * size, t, at, size) for t in range(tp)]
            at += size
    rows = shards[0][0].shape[0]
    return in_vmem(
        functools.partial(blocks_kernel, moves),
        "column_blocks",
        [shard for shard, _ in shards],
        [((tp, rows, at), BF)],
    )[0]


def block(weights, t, columns):
    part = weights[:, t, :, columns]
    return part.reshape(part.shape[0] * part.shape[1], part.shape[2])


def project(rows, weights, columns):
    tp = weights.shape[1]
    step = rows.shape[1] // tp
    total = dot(rows[:, :step], block(weights, 0, columns))
    for t in range(1, tp):
        total = total + dot(rows[:, t * step : (t + 1) * step], block(weights, t, columns))
    return total


def start_copies(pairs, sems):
    copies = [pltpu.make_async_copy(a, b, sems.at[k]) for k, (a, b) in enumerate(pairs)]
    for copy in copies:
        copy.start()
    return copies


def softmax_head(queries, keys, bias, free, extra):
    scale = HDIM ** (-0.5)
    logits = dot_t(queries, keys[:free]) * scale
    if bias is not None:
        logits = logits + bias
    top = jnp.max(logits, axis=-1, keepdims=True)
    if not extra:
        weighs = jnp.exp(logits - top)
        return weighs / jnp.sum(weighs, axis=-1, keepdims=True), None
    one = dot_t(queries, keys[free:])[:, :1] * scale
    top = jnp.maximum(top, one)
    weighs, one = jnp.exp(logits - top), jnp.exp(one - top) * extra
    total = jnp.sum(weighs, axis=-1, keepdims=True) + one
    return weighs / total, one / total


def self_kernel(tp, local, count, *refs):
    entries, masked_entries, gathered = refs[:tp], refs[tp], refs[tp + 1]
    partial = refs[tp + 2 : 2 * tp + 2]
    packed, mix_out, probs_out, weight, held, mixed, sems = refs[2 * tp + 2 :]
    free, rows, span = entries[0].shape[0], packed.shape[1], local * HDIM
    pairs = [(ref, held.at[i * free : (i + 1) * free]) for i, ref in enumerate(entries)]
    pairs += [(masked_entries, held.at[tp * free :]), (gathered, weight)]
    for copy in start_copies(pairs, sems):
        copy.wait()
    for k in range(3):
        cols = slice(k * span, (k + 1) * span)
        found = project(held[...], weight, cols).astype(BF)
        for i in range(tp):
            packed[i, :free, cols] = found[i * free : (i + 1) * free]
            packed[i, free:, cols] = found[tp * free :]
    probs_out[...] = jnp.zeros_like(probs_out)
    for i in range(tp):
        for h in range(local):
            cols = [slice(k * span + h * HDIM, k * span + (h + 1) * HDIM) for k in range(3)]
            queries, keys, values = (packed[i, :, c] for c in cols)
            probs, one = softmax_head(queries, keys, None, free, float(count))
            probs_out[i, h : h + 1, :free] = probs[free : free + 1]
            probs_out[i, h : h + 1, free:] = jnp.broadcast_to(one[free : free + 1], (1, TILE))
            mixture = dot(probs.astype(BF), values[:free])
            mixture = mixture + one.astype(BF).astype(F32) * values[free : free + 1].astype(F32)
            mixed[i * rows : (i + 1) * rows, cols[0]] = mixture.astype(BF)
        mix_out[i] = mixed[i * rows + free : (i + 1) * rows]
    write_out(tp, mixed, weight, partial)


def write_out(tp, mixed, weight, partial):
    rows, width = partial[0].shape
    span = width // tp
    for t in range(tp):
        added = dot(mixed[...], block(weight, t, slice(3 * span, 4 * span))).astype(BF)
        for i in range(tp):
            partial[i][:, t * span : (t + 1) * span] = added[i * rows : (i + 1) * rows]


def masked_row(last, i, one_entry, one_row):
    last = last.astype(F32)
    one_entry[i : i + 1] = last[:1]
    one_row[i : i + 1] = last[1:2] + last[2:3] + last[3:4]


def cross_kernel(tp, local, *refs):
    entries, text = refs[:tp], refs[tp : 2 * tp]
    bias, gathered = refs[2 * tp : 2 * tp + 2]
    partial = refs[2 * tp + 2 : 3 * tp + 2]
    pair, query_out, mix_out, probs_out, one_entry, one_row = refs[3 * tp + 2 : 3 * tp + 8]
    weight, held, held_text, queries, mixed, sems = refs[3 * tp + 8 :]
    rows, txt, span = entries[0].shape[0], text[0].shape[0], local * HDIM
    free = rows - PAD
    pairs = [(ref, held_text.at[i * txt : (i + 1) * txt]) for i, ref in enumerate(text)]
    pairs += [(ref, held.at[i * rows : (i + 1) * rows]) for i, ref in enumerate(entries)]
    pairs += [(gathered, weight)]
    for copy in start_copies(pairs, sems):
        copy.wait()
    for k in range(2):
        cols = slice(k * span, (k + 1) * span)
        found = project(held_text[...], weight, cols).astype(BF)
        for i in range(tp):
            pair[i, :, cols] = found[i * txt : (i + 1) * txt]
    queries[...] = project(held[...], weight, slice(2 * span, 3 * span)).astype(BF)
    probs_out[...] = jnp.zeros_like(probs_out)
    for i in range(tp):
        masked_row(held[i * rows + free : (i + 1) * rows], i, one_entry, one_row)
        query_out[i] = queries[i * rows + free : (i + 1) * rows]
        for h in range(local):
            cols = slice(h * HDIM, (h + 1) * HDIM)
            keys = pair[i, :, cols]
            values = pair[i, :, span + h * HDIM : span + (h + 1) * HDIM]
            some = queries[i * rows : (i + 1) * rows, cols]
            probs, _ = softmax_head(some, keys, bias[i : i + 1], txt, 0)
            probs_out[i, h : h + 1] = probs[free : free + 1]
            mixed[i * rows : (i + 1) * rows, cols] = dot(probs.astype(BF), values).astype(BF)
        mix_out[i] = mixed[i * rows + free : (i + 1) * rows]
    write_out(tp, mixed, weight, partial)


def gelu_parts(value):
    slope = 0.7978845608
    bent = jnp.tanh(slope * (value + 0.044715 * value * value * value))
    half = 0.5 * (1.0 + bent)
    steep = slope * (1.0 + 3.0 * 0.044715 * value * value)
    return value * half, half + 0.5 * value * (1.0 - bent * bent) * steep


def up_kernel(tp, *refs):
    entries, (weight, active, held, sems) = refs[:tp], refs[tp:]
    rows = entries[0].shape[0]

    @pl.when(pl.program_id(0) == 0)
    def _():
        pairs = [(ref, held.at[i * rows : (i + 1) * rows]) for i, ref in enumerate(entries)]
        for copy in start_copies(pairs, sems):
            copy.wait()

    active[...] = gelu_parts(project(held[...], weight, slice(None)))[0].astype(BF)


def mlp_back_kernel(tp, *refs):
    entries_all, grad_active, gathered = refs[:tp], refs[tp], refs[tp + 1]
    active, grad_pre, grad_entry, one_entry, one_row, weight, last, entries, sem = refs[tp + 2 :]
    step, free = entries.shape[1] // tp, entries_all[0].shape[0] - PAD
    ends = [
        pltpu.make_async_copy(ref.at[free:], last.at[i], sem.at[tp + i])
        for i, ref in enumerate(entries_all)
    ]
    for copy in ends:
        copy.start()
    copies = [
        pltpu.make_async_copy(gathered.at[:, t], weight.at[:, t], sem.at[t]) for t in range(tp)
    ]
    for copy in copies:
        copy.start()
    for i, copy in enumerate(ends):
        copy.wait()
        masked_row(last[i], i, one_entry, one_row)
    entries[...] = jnp.zeros_like(entries)
    entries[:tp] = one_entry[...]
    hidden = jnp.zeros(active.shape, F32)
    for t, copy in enumerate(copies):
        copy.wait()
        rows = entries[:, t * step : (t + 1) * step].astype(BF)
        hidden = hidden + dot(rows, block(weight, t, slice(None)))
    value, steep = gelu_parts(hidden)
    active[...] = value.astype(BF)
    grad_pre[...] = (steep * grad_active[...]).astype(BF)
    for t in range(tp):
        back = dot_t(grad_pre[...], block(weight, t, slice(None)))
        grad_entry[:, t * step : (t + 1) * step] = back[:tp]


def summed(parts, i):
    total = parts[0][i : i + 1]
    for j in range(1, len(parts)):
        total = total + parts[j][i ^ j : (i ^ j) + 1]
    return total


def out_back(rows, weights, columns):
    tp = weights.shape[1]
    step = rows.shape[1] // tp
    total = dot_t(rows[:, :step], block(weights, 0, columns))
    for t in range(1, tp):
        total = total + dot_t(rows[:, t * step : (t + 1) * step], block(weights, t, columns))
    return total.astype(BF).astype(F32)


def head_mask(span):
    heads = lax.broadcasted_iota(jnp.int32, (8, span), 0)
    return lax.broadcasted_iota(jnp.int32, (8, span), 1) // HDIM == heads


def row_back(parts, rows, gain, base, i, out, gain_row):
    grad = summed(parts, i)
    field, scale = normed(rows[i : i + 1])
    out[i : i + 1] = base[i : i + 1] + norm_back(grad * gain[...], field, scale)
    if i == 0:
        gain_row[...] = grad * field


def cross_back_kernel(
    tp, base, rows, gain, pair, probs, gathered, *refs,
):
    parts = refs[:tp]
    grad_mid, grad_cmix, scores, grad_cq, grad_entry, gain_row = refs[tp : tp + 6]
    weight, held, sems = refs[tp + 6 :]
    span = weight.shape[3] // 2
    copies = [
        pltpu.make_async_copy(gathered.at[:, :, :, 2 * span :], weight, sems.at[0]),
    ]
    for copy in copies:
        copy.start()
    held[...] = jnp.zeros_like(held)
    for i in range(tp):
        row_back(parts, rows, gain, base, i, held, gain_row)
    grad_mid[...] = held[:tp]
    copies[0].wait()
    mixed = out_back(held[...].astype(BF), weight, slice(span, 2 * span))
    grad_cmix[...] = mixed[:tp]
    mask = head_mask(span)
    held[...] = jnp.zeros_like(held)
    for i in range(tp):
        spread = jnp.where(mask, mixed[i : i + 1], 0.0).astype(BF)
        grad_probs = dot_t(spread, pair[i, :, span:])
        weighs = probs[i]
        grad = weighs * (grad_probs - jnp.sum(grad_probs * weighs, axis=-1, keepdims=True))
        grad = grad.astype(BF)
        scores[i] = grad.astype(F32)
        back = jnp.where(mask, dot(grad, pair[i, :, :span]), 0.0)
        held[i : i + 1, :span] = jnp.sum(back, axis=0, keepdims=True) * HDIM ** (-0.5)
    grad_cq[...] = held[:tp, :span]
    queries = held[:, :span].astype(BF)
    step = grad_entry.shape[1] // tp
    for t in range(tp):
        back = dot_t(queries, block(weight, t, slice(0, span)))
        grad_entry[:, t * step : (t + 1) * step] = back[:tp]


def spread_heads(rows, i, spreads, mask):
    spreads[8 * i : 8 * i + 8] = jnp.where(mask, rows, 0.0)


def text_back_kernel(tp, local, *refs):
    scores, probs, query_one, grad_cmix, kvq = refs[:5]
    cross_one_row, mlp_one, grad_pre, grad_cq, mixed, cross, active, grad_mid = refs[5:13]
    text = refs[13 : 13 + tp]
    sent = refs[13 + tp : 13 + 2 * tp]
    lefts, factors, weight, held, keys, values, sems = refs[13 + 2 * tp :]
    span, width, txt = grad_cmix.shape[1], lefts.shape[1], scores.shape[2]
    copy = pltpu.make_async_copy(kvq.at[:, :, :, : 2 * span], weight, sems.at[0])
    copy.start()
    mask = head_mask(span)
    ff = grad_pre.shape[1]
    places, at = [], 0
    for size in (ff, span, span, span, span, span, ff, width):
        places.append(slice(at, at + size))
        at += size
    for i in range(tp):
        spread_heads(query_one[i].astype(F32)[:1], i, keys, mask)
        spread_heads(grad_cmix[i : i + 1], i, values, mask)
        both = jnp.concatenate([scores[i], probs[i]], axis=0).astype(BF)
        found = dot(both, text[i][...])
        for kind in range(2):
            begin = (2 * i + kind) * local
            lefts[begin : begin + local] = found[8 * kind : 8 * kind + local]
        sent[i][:, width:] = both
        for k, rows in ((2, query_one), (4, mixed), (5, cross)):
            held[i : i + 1, places[k]] = rows[i].astype(F32)[:1]
    held[:tp, places[0]] = grad_pre[...].astype(F32)[:tp]
    held[:tp, places[1]] = grad_cq[...]
    held[:tp, places[3]] = grad_cmix[...]
    held[:tp, places[6]] = active[...].astype(F32)[:tp]
    held[:tp, places[7]] = grad_mid[...]
    factors[...] = held[:tp].astype(BF)
    begin = 2 * tp * local
    lefts[begin : begin + tp] = cross_one_row[...]
    lefts[begin + tp :] = mlp_one[...]
    copy.wait()
    step = width // tp
    key_spread, value_spread = keys[...].astype(BF), values[...].astype(BF)
    for t in range(tp):
        cols = slice(t * step, (t + 1) * step)
        key_rows = dot_t(key_spread, block(weight, t, slice(0, span))) * HDIM ** (-0.5)
        value_rows = dot_t(value_spread, block(weight, t, slice(span, 2 * span)))
        for i in range(tp):
            eight = slice(8 * i, 8 * i + 8)
            both = jnp.concatenate([key_rows[eight], value_rows[eight]], axis=0)
            sent[i][:, cols] = both.astype(BF)


def self_back_kernel(
    tp, local, base, rows, gain, packed, probs, masked_entries, text_lefts, text_factors,
    gain_a, embed, gain_m_row, gathered, *refs,
):
    parts, entries, text_sent = refs[:tp], refs[tp : 2 * tp], refs[2 * tp : 3 * tp]
    sent, refs = refs[3 * tp : 4 * tp], refs[4 * tp :]
    payload, factors, weight, held, spreads, lefts, small, sems = refs
    width = lefts.shape[1]
    span, free = weight.shape[3] // 4, entries[0].shape[0]
    copy = pltpu.make_async_copy(gathered, weight, sems.at[0])
    copy.start()
    ff = (text_factors.shape[1] - 5 * span - width) // 2
    cut = ff + 3 * span
    factors[:, :cut] = text_factors[:, :cut]
    factors[:, cut + 3 * span : -width] = text_factors[:, cut:]
    small[...] = jnp.zeros_like(small)
    small[3:4] = gain_m_row[...]
    held[...] = jnp.zeros_like(held)
    for i in range(tp):
        row_back(parts, rows, gain, base, i, held, small.at[2:3])
    small[0:1] = held[0:1]
    factors[:, -width:] = held[:tp].astype(BF)
    copy.wait()
    mixed = out_back(held[...].astype(BF), weight, slice(3 * span, 4 * span))
    factors[:, cut : cut + span] = mixed[:tp].astype(BF)
    mask = head_mask(span)
    held[...] = jnp.zeros_like(held)
    masked_row = masked_entries[:1].astype(F32)
    ones = []
    for i in range(tp):
        spread = jnp.where(mask, mixed[i : i + 1], 0.0)
        spreads[8 * i : 8 * i + 8] = spread
        spread = spread.astype(BF)
        values = packed[i, :, 2 * span :]
        grad_probs, grad_one = dot_t(spread, values[:free]), dot_t(spread, values[free:])[:, :1]
        weighs, one = probs[i, :, :free], probs[i, :, free : free + 1]
        mean = jnp.sum(grad_probs * weighs, axis=-1, keepdims=True) + grad_one * one
        grad = (weighs * (grad_probs - mean)).astype(BF)
        grad_one = (one * (grad_one - mean)).astype(BF).astype(F32)
        ones.append((grad_one, one))
        keys = packed[i, :, span : 2 * span]
        back = dot(grad, keys[:free]) + grad_one * keys[free : free + 1].astype(F32)
        back = jnp.sum(jnp.where(mask, back, 0.0), axis=0, keepdims=True)
        held[i : i + 1, :span] = back * HDIM ** (-0.5)
        both = jnp.concatenate([grad.astype(F32), weighs], axis=0).astype(BF)
        both_one = jnp.concatenate([grad_one, one], axis=0).astype(BF).astype(F32)
        found = dot(both, entries[i][...]) + both_one * masked_row
        for kind in range(2):
            begin = (2 * i + kind) * local
            lefts[begin : begin + local] = found[8 * kind : 8 * kind + local]
        sent[i][:PAD, width:] = both
        sent[i][PAD:] = text_sent[i][...]
    factors[:, cut + span : cut + 2 * span] = held[:tp, :span].astype(BF)
    queries = held[:, :span].astype(BF)
    zero_query = packed[0, free:, :span].astype(F32)[:1]
    factors[:, cut + 2 * span : cut + 3 * span] = jnp.broadcast_to(zero_query, (tp, span)).astype(BF)
    key_spread = jnp.where(mask, zero_query, 0.0).astype(BF)
    value_spread = spreads[...].astype(BF)
    step = width // tp
    field, scale = normed(embed[...])
    for t in range(tp):
        cols = slice(t * step, (t + 1) * step)
        keys = dot_t(key_spread, block(weight, t, slice(span, 2 * span))) * HDIM ** (-0.5)
        values = dot_t(value_spread, block(weight, t, slice(2 * span, 3 * span)))
        query_rows = dot_t(queries, block(weight, t, slice(0, span)))
        masked_grad, gain_grad = 0.0, 0.0
        for i in range(tp):
            mine = values[8 * i : 8 * i + 8]
            sent[i][:PAD, cols] = jnp.concatenate([keys, mine], axis=0).astype(BF)
            last = query_rows[i : i + 1]
            found = ones[i][0] * keys + ones[i][1] * mine
            masked_grad = masked_grad + last + jnp.sum(found, axis=0, keepdims=True)
            for kind, rows_back in enumerate((keys, mine)):
                begin = (2 * i + kind) * local
                found = lefts[begin : begin + local, cols] * rows_back[:local]
                gain_grad = gain_grad + jnp.sum(found, axis=0, keepdims=True)
        gain_grad = gain_grad / gain_a[:, cols]
        rows_sum = jnp.sum(query_rows[:tp], axis=0, keepdims=True)
        small[1:2, cols] = gain_grad + rows_sum * field[:, cols]
        held[0:1, cols] = masked_grad
    small[0:1] = small[0:1] + norm_back(held[0:1] * gain_a[...], field, scale)
    begin = 2 * tp * local
    lefts[begin : begin + text_lefts.shape[0]] = text_lefts[...]
    begin += text_lefts.shape[0]
    high = small[:4].astype(BF).astype(F32)
    lefts[begin : begin + 4] = high
    lefts[begin + 4 : begin + 8] = small[:4] - high
    half, own = lefts.shape[0] // 2, payload.shape[2] // 2
    for d in range(payload.shape[0]):
        cols = slice(d * own, (d + 1) * own)
        both = jnp.concatenate([lefts[:half, cols], lefts[half:, cols]], axis=1)
        payload[d] = both.astype(BF)


def tokens_back_kernel(tp, rows, gain, place, *refs):
    came, (tokens, text) = refs[:tp], refs[tp:]
    width, free = rows.shape[1], place.shape[1]
    grad, grad_text = 0.0, 0.0
    for part in came:
        grad = grad + dot_sum(part[:PAD, width:], part[:PAD, :width])
        grad_text = grad_text + dot_sum(part[PAD:, width:], part[PAD:, :width])
    text[...] = grad_text.astype(BF)
    field, scale = normed(rows[:free])
    start = norm_back(grad * gain[...], field, scale)
    tokens[...] = dot(place[...], start.astype(BF)).astype(BF)


def stack_kernel(*refs):
    for k, ref in enumerate(refs[:-1]):
        refs[-1][k] = ref[...]


def unpack_kernel(planes, others, right, group, held):
    count, tp = planes.shape[:2]
    for k in range(count):
        held[k * tp : (k + 1) * tp] = planes[k].astype(F32)
        held[(count + k) * tp : (count + k + 1) * tp] = others[k].astype(F32)
    right[...] = held[:, : right.shape[1]].astype(BF)
    group[...] = held[:, right.shape[1] :].astype(BF)


def aligned(right, corner, tp):
    count = right.shape[0]
    out = lax.broadcasted_iota(jnp.int32, (count, count), 0)
    into = lax.broadcasted_iota(jnp.int32, (count, count), 1)
    same = (out // tp == (corner ^ (into // tp))) & (out % tp == into % tp)
    return dot(same.astype(BF), right).astype(BF)


def columns_kernel(local, place, attn_left, text_left, one_left, entry, *refs):
    right, (grad_qkv, grad_kv, grad_cq, grad_up) = refs[:-4], refs[-4:]
    tp, span = len(right), local * HDIM
    ff = right[0].shape[1] - 6 * span
    ones = jnp.ones((right[0].shape[0], HDIM), BF)
    scale = HDIM ** (-0.5)

    def at_columns(begin, size):
        return pl.ds(pl.multiple_of(begin, HDIM), size)

    for j in range(tp):
        at = place[0] ^ j
        rows = aligned(right[j][...], place[1], tp)
        part = [rows[:, ff + k * span : ff + (k + 1) * span] for k in range(6)]
        grad_up[:, at_columns(at * ff, ff)] = dot_sum(one_left[at, 1], rows[:, :ff])
        grad_cq[:, at_columns(at * span, span)] = dot_sum(one_left[at, 0], part[0])
        total = jnp.sum(part[4].astype(F32), axis=0, keepdims=True)
        grad_qkv[:, at_columns(at * span, span)] = entry[...] * total
        queries = part[5].astype(F32)[:1] * scale
        for h in range(local):
            cols = slice(h * HDIM, (h + 1) * HDIM)
            begin = at * span + h * HDIM
            outer = dot_sum(text_left[at, 0, h], part[1][:, cols])
            grad_kv[:, at_columns(begin, HDIM)] = outer * scale
            outer = dot_sum(text_left[at, 1, h], part[2][:, cols])
            grad_kv[:, at_columns(tp * span + begin, HDIM)] = outer
            outer = dot_sum(attn_left[at, 0, h], ones) * queries[:, cols]
            grad_qkv[:, at_columns(tp * span + begin, HDIM)] = outer
            outer = dot_sum(attn_left[at, 1, h], part[3][:, cols])
            grad_qkv[:, at_columns(2 * tp * span + begin, HDIM)] = outer


def whole_spec():
    return pl.BlockSpec(memory_space=pl.ANY)


def in_vmem(kernel, name, operands, out_shape, scratch_shapes=(), held=()):
    spaces = dict(held)
    return pl.pallas_call(
        kernel,
        in_specs=[
            pl.BlockSpec(memory_space=spaces.get(k, pltpu.VMEM)) for k in range(len(operands))
        ],
        out_specs=[pl.BlockSpec(memory_space=pltpu.VMEM)] * len(out_shape),
        out_shape=[jax.ShapeDtypeStruct(shape, dtype) for shape, dtype in out_shape],
        scratch_shapes=scratch_shapes,
        compiler_params=pltpu.CompilerParams(vmem_limit_bytes=VMEM_BYTES),
        cost_estimate=COST,
        name=name,
    )(*operands)


def self_forward(local, count, entries, masked_entries, gathered):
    tp, (free, width) = len(entries), entries[0].shape
    span, rows = local * HDIM, free + PAD
    found = in_vmem(
        functools.partial(self_kernel, tp, local, count),
        "self_attention",
        [*entries, masked_entries, gathered],
        [((rows, width), BF)] * tp
        + [((tp, rows, 3 * span), BF), ((tp, PAD, span), BF), ((tp, 8, free + TILE), F32)],
        [
            pltpu.VMEM(gathered.shape, BF),
            pltpu.VMEM((tp * free + PAD, width), BF),
            pltpu.VMEM((tp * rows, span), BF),
            pltpu.SemaphoreType.DMA((tp + 2,)),
        ],
        [(k, pl.ANY) for k in range(tp + 2)],
    )
    return found[:tp], *found[tp:]


def cross_forward(local, entries, text, bias, gathered):
    tp, (rows, width) = len(entries), entries[0].shape
    txt, span = text[0].shape[0], local * HDIM
    found = in_vmem(
        functools.partial(cross_kernel, tp, local),
        "cross_attention",
        [*entries, *text, bias, gathered],
        [((rows, width), BF)] * tp
        + [
            ((tp, txt, 2 * span), BF),
            ((tp, PAD, span), BF),
            ((tp, PAD, span), BF),
            ((tp, 8, txt), F32),
            ((tp, width), F32),
            ((tp, width), F32),
        ],
        [
            pltpu.VMEM(gathered.shape, BF),
            pltpu.VMEM((tp * rows, width), BF),
            pltpu.VMEM((tp * txt, width), BF),
            pltpu.VMEM((tp * rows, span), BF),
            pltpu.VMEM((tp * rows, span), BF),
            pltpu.SemaphoreType.DMA((2 * tp + 1,)),
        ],
        [(k, pl.ANY) for k in range(2 * tp + 2) if k != 2 * tp],
    )
    return found[:tp], *found[tp:]


def down_kernel(tp, active, gathered, *refs):
    partial, (weight, sems) = refs[:tp], refs[tp:]
    rows, width = partial[0].shape
    step = min(512, width)
    parts = [slice(at, at + step) for at in range(0, width, step)]
    copies = start_copies([(gathered.at[:, :, cols], weight.at[:, :, cols]) for cols in parts], sems)
    for cols, copy in zip(parts, copies):
        copy.wait()
        part = weight[:, :, cols]
        added = dot(active[...], part.reshape(-1, step)).astype(BF)
        for i in range(tp):
            partial[i][:, cols] = added[i * rows : (i + 1) * rows]


def mlp_down(tp, active, gathered):
    rows, width = active.shape[0] // tp, gathered.shape[2]
    return in_vmem(
        functools.partial(down_kernel, tp),
        "mlp_down",
        [active, gathered],
        [((rows, width), BF)] * tp,
        [pltpu.VMEM(gathered.shape, BF), pltpu.SemaphoreType.DMA((width // min(512, width),))],
        ((1, pl.ANY),),
    )


def mlp_up(entries, gathered):
    tp, (rows, width) = len(entries), entries[0].shape
    blocks, _, own, ff = gathered.shape
    step = min(ff, 512)
    return pl.pallas_call(
        functools.partial(up_kernel, tp),
        grid=(ff // step,),
        in_specs=[whole_spec()] * tp
        + [pl.BlockSpec((blocks, tp, own, step), lambda i: (0, 0, 0, i))],
        out_specs=pl.BlockSpec((tp * rows, step), lambda i: (0, i)),
        out_shape=jax.ShapeDtypeStruct((tp * rows, ff), BF),
        scratch_shapes=[
            pltpu.VMEM((tp * rows, width), BF),
            pltpu.SemaphoreType.DMA((tp,)),
        ],
        compiler_params=pltpu.CompilerParams(vmem_limit_bytes=VMEM_BYTES),
        cost_estimate=COST,
        name="mlp_up",
    )(*entries, gathered)


def mlp_back(entries, grad_active, gathered):
    tp, width = len(entries), entries[0].shape[1]
    ff = gathered.shape[3]
    return in_vmem(
        functools.partial(mlp_back_kernel, tp),
        "mlp_back",
        [*entries, grad_active, gathered],
        [
            ((PAD, ff), BF),
            ((PAD, ff), BF),
            ((tp, width), F32),
            ((tp, width), F32),
            ((tp, width), F32),
        ],
        [
            pltpu.VMEM(gathered.shape, BF),
            pltpu.VMEM((tp, PAD, width), BF),
            pltpu.VMEM((PAD, width), F32),
            pltpu.SemaphoreType.DMA((2 * tp,)),
        ],
        [(k, pl.ANY) for k in range(tp + 2) if k != tp],
    )


def cross_back(base, rows, gain, pair, probs, gathered, parts):
    tp, width = base.shape
    blocks, _, own, columns = gathered.shape
    span = columns // 4
    return in_vmem(
        functools.partial(cross_back_kernel, tp),
        "cross_back",
        [base, rows, gain[None], pair, probs, gathered, *parts],
        [
            ((tp, width), F32),
            ((tp, span), F32),
            (probs.shape, F32),
            ((tp, span), F32),
            ((tp, width), F32),
            ((1, width), F32),
        ],
        [
            pltpu.VMEM((blocks, tp, own, 2 * span), BF),
            pltpu.VMEM((8, width), F32),
            pltpu.SemaphoreType.DMA((1,)),
        ],
        ((5, pl.ANY),),
    )


def text_back(local, scores, probs, query_one, grad_cmix, kvq, rest, text):
    tp, span = grad_cmix.shape
    blocks, _, own, _ = kvq.shape
    (txt, width), ff = text[0].shape, rest[2].shape[1]
    found = in_vmem(
        functools.partial(text_back_kernel, tp, local),
        "text_back",
        [scores, probs, query_one, grad_cmix, kvq, *rest, *text],
        [((PAD, width + txt), BF)] * tp
        + [((2 * tp * (local + 1), width), F32), ((tp, 2 * ff + 5 * span + width), BF)],
        [
            pltpu.VMEM((blocks, tp, own, 2 * span), BF),
            pltpu.VMEM((8, 2 * ff + 5 * span + width), F32),
            pltpu.VMEM((8 * tp, span), F32),
            pltpu.VMEM((8 * tp, span), F32),
            pltpu.SemaphoreType.DMA((1,)),
        ],
        ((4, pl.ANY),),
    )
    return found[:tp], *found[tp:]


def self_back(local, world, small_operands, gathered, parts, entries, text_sent):
    tp, width = small_operands[0].shape
    text_lefts, text_factors = small_operands[6], small_operands[7]
    _, _, own, columns = gathered.shape
    span, free = columns // 4, entries[0].shape[0]
    count = 2 * tp * local + text_lefts.shape[0] + 8
    operands = [*small_operands, gathered, *parts, *entries, *text_sent]
    found = in_vmem(
        functools.partial(self_back_kernel, tp, local),
        "self_back",
        operands,
        [((2 * PAD, width + free), BF)] * tp
        + [((world, count // 2, 2 * own), BF), ((tp, text_factors.shape[1] + 3 * span + width), BF)],
        [
            pltpu.VMEM(gathered.shape, BF),
            pltpu.VMEM((8, width), F32),
            pltpu.VMEM((8 * tp, span), F32),
            pltpu.VMEM((count, width), F32),
            pltpu.VMEM((8, width), F32),
            pltpu.SemaphoreType.DMA((1,)),
        ],
        ((len(small_operands), pl.ANY),),
    )
    return found[:tp], *found[tp:]


def stacked(pieces):
    shape = (len(pieces),) + pieces[0].shape
    return in_vmem(stack_kernel, "stack", pieces, [(shape, BF)])[0]


def unpack(planes, others, cut):
    count, tp, wide = planes.shape
    rows = 2 * count * tp
    return in_vmem(
        unpack_kernel,
        "unpack",
        [planes, others],
        [((rows, cut), BF), ((rows, wide - cut), BF)],
        [pltpu.VMEM((rows, wide), F32)],
    )


def join_kernel(free, base, gain, *refs):
    parts, (total, entries) = refs[:-2], refs[-2:]
    value = base[...]
    for part in parts:
        value = value + part[...].astype(F32)
    total[...] = value
    found = normed(value)[0] * gain[...]
    entries[...] = found.astype(BF)

    @pl.when(pl.program_id(0) == pl.num_programs(0) - 1)
    def _():
        at = value.shape[0] - PAD
        row = value[at : at + 1]
        spot = lax.broadcasted_iota(jnp.int32, (PAD, value.shape[1]), 0)
        last = found[at:]
        for k in range(3):
            part = row.astype(BF).astype(F32)
            last = jnp.where(spot == k + 1, part, last)
            row = row - part
        entries[at:] = last.astype(BF)


def join(base, parts, gain):
    rows, width = base.shape
    step = PAD * 3 if rows % (PAD * 3) == 0 else PAD
    block = pl.BlockSpec((step, width), lambda i: (i, 0))
    return pl.pallas_call(
        functools.partial(join_kernel, rows - PAD),
        grid=(rows // step,),
        in_specs=[block, pl.BlockSpec((1, width), lambda i: (0, 0))] + [block] * len(parts),
        out_specs=[block, block],
        out_shape=[
            jax.ShapeDtypeStruct((rows, width), F32),
            jax.ShapeDtypeStruct((rows, width), BF),
        ],
        compiler_params=pltpu.CompilerParams(vmem_limit_bytes=VMEM_BYTES),
        cost_estimate=COST,
        name="join",
    )(base, gain[None], *parts)


def shards(
    tp,
    planes,
    tokens,
    text,
    cotangent,
    positions,
    text_lengths,
    mask_embed,
    gain_attn,
    w_qkv,
    w_attn_out,
    gain_cross,
    w_cross_q,
    w_cross_kv,
    w_cross_out,
    gain_mlp,
    w_up,
    w_down,
):
    me = Layer(tp, planes)
    seq, width = tokens.shape
    masked_count = positions.shape[1]
    free = seq - masked_count
    txt = text.shape[1]
    local = HEADS // tp
    rows = free + PAD
    device = (me.t * 2 + me.c) * planes + me.z
    world = tp * 2 * planes
    own = width // world

    def after(value, earlier):
        return lax.optimization_barrier((value, earlier))[0]

    span = local * HDIM

    qkv_sent = me.shuffle([(w_qkv, 3)])
    attn_w = jnp.concatenate([qkv_sent, column_blocks(tp, [(w_attn_out, 1)])], axis=2)
    attn_w = me.gather_blocks(attn_w)

    def natural(value):
        split = value.reshape(value.shape[:-1] + (2 * planes, tp, own))
        return split.swapaxes(-3, -2).reshape(value.shape)

    cot_sum = jnp.sum(cotangent[0].astype(F32), axis=0)
    vectors = jnp.concatenate([mask_embed, gain_attn, gain_cross, gain_mlp]).astype(F32)
    fill = TILE - vectors.shape[0] % TILE
    length = jnp.broadcast_to(text_lengths.astype(F32), (fill,))
    gathered = me.tp_direct(me.gather_cz(jnp.concatenate([cot_sum, vectors, length])))
    others = after((w_cross_kv, w_cross_q, w_cross_out), (gathered, qkv_sent))
    kvq_sent = me.shuffle([(others[0], 2), (others[1], 1)])
    cross_sent = jnp.concatenate([kvq_sent, column_blocks(tp, [(others[2], 1)])], axis=2)
    vectors = gathered[:, :, width : width + 4 * own].reshape(world, 4, own)
    vectors = xor_order(vectors, device, world).transpose(1, 0, 2).reshape(4, width)
    embed, gain_a, gain_c, gain_m = vectors[0], vectors[1], vectors[2], vectors[3]
    lengths = gathered[:, 0, width + 4 * own :][:, :1]
    text_bias = jnp.where(
        lax.broadcasted_iota(jnp.int32, (tp, txt), 1).astype(F32) < lengths, 0.0, -1e30
    )
    cot_group = gathered[:, 0, :width]

    spots = lax.broadcasted_iota(jnp.int32, (masked_count, seq), 1)
    masked = jnp.sum((positions[0][:, None] == spots).astype(F32), axis=0)
    below = lax.broadcasted_iota(jnp.int32, (seq, seq), 0) <= lax.broadcasted_iota(
        jnp.int32, (seq, seq), 1
    )
    rank = dot((1.0 - masked).astype(BF)[None, :], below.astype(BF))[0]
    ranks = lax.broadcasted_iota(jnp.int32, (free, seq), 0).astype(F32) + 1.0
    pick = ((rank[None, :] == ranks) & (masked[None, :] == 0.0)).astype(BF)
    place = jnp.concatenate(
        [pick.T, masked[:, None].astype(BF), jnp.zeros((seq, PAD - 1), BF)], axis=1
    )
    start_free = dot(pick, tokens)
    start = jnp.concatenate([start_free, jnp.broadcast_to(embed[None], (PAD, width))])

    cot_rows = gathered[:, :, :width].reshape(world, width)
    high = cot_rows.astype(BF)
    low = (cot_rows - high.astype(F32)).astype(BF)
    through = dot_t(jnp.concatenate([high, low]), w_down)
    through = through[:world] + through[world:]
    through = through.reshape(tp, 2 * planes, -1).transpose(1, 0, 2)
    through = xor_order(through, me.c * planes + me.z, 2 * planes)
    through = lax.all_to_all(after(through, kvq_sent), ("core", "fsdp"), 0, 0, tiled=True)
    grad_active = through.transpose(1, 0, 2).reshape(tp, -1)

    field_a, scale_a = normed(start)
    entries = (field_a * gain_a[None]).astype(BF)
    masked_entries = entries[free:]
    entries_all = me.spread(entries[:free])
    text_rows = me.spread(after(text[0], entries_all))
    up_sent = me.shuffle([(after(w_up, (entries_all, kvq_sent)), 1)])
    cross_w = me.gather_blocks(after(cross_sent, (attn_w, entries_all, up_sent, place, masked_entries, text_bias)))
    partial, packed, mixed_one, probs_one = self_forward(
        local, masked_count, entries_all, masked_entries, attn_w
    )
    after_attn, cross_entries = join(after(start, (grad_active, place)), me.collect(after(tuple(partial), text_rows)), gain_c)

    cross_all = me.spread(cross_entries)
    up = me.gather_blocks(after(up_sent, (cross_w, cross_all)))
    partial, pair, query_one, cross_one, cross_probs_one, cross_entry, attn_stream = cross_forward(
        local, cross_all, text_rows, text_bias, cross_w
    )
    after_cross, mlp_entries = join(after_attn, me.collect(partial), gain_m)

    mlp_all = me.spread(mlp_entries)
    down = me.gather_blocks(after(w_down, (up, mlp_all)))

    active_one, grad_pre, grad_entry, mlp_one, cross_stream = mlp_back(
        mlp_all, jnp.pad(grad_active, ((0, PAD - tp), (0, 0))), up
    )
    grad_mid, grad_cmix, scores, grad_cq, grad_entry, grad_gain_m = cross_back(
        cot_group, cross_stream, gain_m, pair, cross_probs_one, cross_w, me.tp_parts(grad_entry)
    )
    text_sent, text_lefts, text_factors = text_back(
        local,
        scores,
        cross_probs_one,
        query_one,
        grad_cmix,
        cross_w,
        [
            cross_entry,
            mlp_one,
            grad_pre,
            grad_cq,
            mixed_one,
            cross_one,
            active_one,
            grad_mid,
        ],
        text_rows,
    )
    sent, payload, factors = self_back(
        local,
        world,
        [
            grad_mid,
            attn_stream,
            gain_c[None],
            packed,
            probs_one,
            masked_entries,
            text_lefts,
            text_factors,
            gain_a[None],
            embed[None],
            grad_gain_m,
        ],
        attn_w,
        me.tp_parts(grad_entry),
        entries_all,
        text_sent,
    )
    came = me.to_owner(sent)

    corner = me.c * planes + me.z
    ff = grad_pre.shape[1]
    active = mlp_up(after(tuple(mlp_all), payload), up)
    pieces = [factors] + [me.other_plane(factors, k) for k in range(1, planes)]
    planes_of = stacked(after(tuple(pieces), (active, came)))
    lefts = me.to_rows(after(payload, planes_of))
    right, group = unpack(planes_of, me.other_core(planes_of), ff + 6 * span)
    right = [right] + [me.hop(right, j) for j in range(1, tp)]

    def mine(stack):
        size = stack.shape[1] // (2 * planes)
        return lax.dynamic_slice_in_dim(stack, corner * size, size, axis=1)

    cuts = [span, 2 * span, 2 * span + ff, 2 * span + ff + width]
    mixed_f, cross_f, active_f, mid_f, attn_f = jnp.split(group, cuts, axis=1)
    cot_f = gathered[:, :, :width].astype(BF).swapaxes(0, 1).reshape(world, width)
    grad_w_out = dot_sum(mine(mixed_f), attn_f)
    grad_w_cout = dot_sum(mine(cross_f), mid_f)
    grad_w_down = dot_sum(mine(active_f), cot_f)
    active = after(active, (right[0], lefts, grad_w_out, grad_w_cout, grad_w_down))
    partial = mlp_down(tp, active, down)
    collected = me.collect(partial)

    grad_tokens, grad_text = in_vmem(
        functools.partial(tokens_back_kernel, tp),
        "tokens_back",
        [start, gain_a[None], pick.T, *after(tuple(came), partial)],
        [((seq, width), BF), ((txt, width), BF)],
    )

    heads = 2 * tp * local
    lefts = after(lefts, partial)
    lefts = jnp.concatenate([lefts[:, :, :own], lefts[:, :, own:]], axis=1)
    attn_left, text_left = (
        lefts[:, k * heads : (k + 1) * heads]
        .reshape(tp, 2 * planes, tp, 2, local, own)
        .transpose(0, 3, 4, 1, 2, 5)
        .reshape(tp, 2, local, world, own)
        for k in range(2)
    )
    one_left = lefts[:, 2 * heads : 2 * heads + 2 * tp].reshape(tp, 2 * planes, 2, tp, own)
    one_left = one_left.transpose(0, 2, 1, 3, 4).reshape(tp, 2, world, own)
    small = jnp.sum(lefts[:, 2 * heads + 2 * tp :].astype(F32), axis=0)
    small = small[:4] + small[4:]
    entry_own = lax.dynamic_slice_in_dim(entries[free], device * own, own).astype(F32)
    place_at = jnp.stack([me.t, corner]).astype(jnp.int32)
    grad_w_qkv, grad_w_kv, grad_w_cq, grad_w_up = in_vmem(
        functools.partial(columns_kernel, local),
        "columns",
        [place_at, attn_left, text_left, one_left, entry_own[:, None], *right],
        [((own, 3 * width), F32), ((own, 2 * width), F32), ((own, width), F32), ((own, tp * ff), F32)],
        held=((0, pltpu.SMEM),),
    )

    collected = after(tuple(collected), (grad_tokens, grad_w_qkv, small))
    output = sum(part.astype(F32) for part in collected)
    output = dot(place, (after_cross + output).astype(BF)).astype(BF)
    return (
        output,
        grad_tokens,
        grad_text[None],
        small[0],
        small[1],
        grad_w_qkv,
        grad_w_out,
        small[2],
        grad_w_cq,
        grad_w_kv,
        grad_w_cout,
        small[3],
        grad_w_up,
        grad_w_down,
    )


def solution(mesh):
    tp, planes = mesh.shape["dp"] // 2, mesh.shape["fsdp"]
    fine = Mesh(mesh.devices.reshape(tp, 2, planes), ("tp", "core", "fsdp"))
    every = ("tp", "core", "fsdp")
    one, two, three = P(every), P(every, None), P(every, None, None)

    def layer(*arguments):
        return shards(tp, planes, *arguments)

    return jax.shard_map(
        layer,
        mesh=fine,
        in_specs=(two, three, three, two, one, one, one, two, two, one, two, two, two, one, two, two),
        out_specs=(two, two, three, one, one, two, two, one, two, two, two, one, two, two),
        check_vma=False,
    )
```

```python
import functools

import jax
import jax.numpy as jnp
from jax import lax
from jax.experimental import pallas as pl
from jax.experimental.pallas import tpu as pltpu
from jax.sharding import Mesh, PartitionSpec as P

HEADS = 16
HDIM = 128
TILE = 128
PAD = 16
BF = jnp.bfloat16
F32 = jnp.float32
VMEM_BYTES = 60 << 20
COST = pl.CostEstimate(flops=1, bytes_accessed=1, transcendentals=0)


def dot(left, right):
    return jnp.dot(left, right, preferred_element_type=F32)


def dot_t(left, right):
    return lax.dot_general(left, right, (((1,), (1,)), ((), ())), preferred_element_type=F32)


def dot_sum(left, right):
    return lax.dot_general(left, right, (((0,), (0,)), ((), ())), preferred_element_type=F32)


def normed(rows):
    centered = rows - jnp.mean(rows, axis=-1, keepdims=True)
    scale = lax.rsqrt(jnp.mean(centered * centered, axis=-1, keepdims=True) + 1e-05)
    return centered * scale, scale


def norm_back(grad, field, scale):
    return scale * (
        grad
        - jnp.mean(grad, axis=-1, keepdims=True)
        - field * jnp.mean(grad * field, axis=-1, keepdims=True)
    )


def xor_order(stack, me, size):
    bit = 1
    while bit < size:
        split = stack.reshape((size // (2 * bit), 2, bit) + stack.shape[1:])
        turned = jnp.concatenate([split[:, 1:], split[:, :1]], axis=1)
        stack = jnp.where((me & bit) != 0, turned, split).reshape(stack.shape)
        bit *= 2
    return stack


def bits_of(size):
    return [1 << k for k in range(size.bit_length() - 1)]


class Layer:
    def __init__(self, tp, planes):
        self.tp, self.planes = tp, planes
        self.t, self.c, self.z = (lax.axis_index(a) for a in ("tp", "core", "fsdp"))


    def hop(self, value, j):
        return lax.ppermute(value, "tp", [(i, i ^ j) for i in range(self.tp)])

    def other_core(self, value):
        return lax.ppermute(value, "core", [(0, 1), (1, 0)])

    def other_plane(self, value, k):
        return lax.ppermute(value, "fsdp", [(i, i ^ k) for i in range(self.planes)])

    def spread(self, value):
        return [value] + [self.hop(value, j) for j in range(1, self.tp)]

    def collect(self, parts):
        return [parts[0]] + [self.hop(parts[j], j) for j in range(1, self.tp)]

    def tp_direct(self, value):
        return jnp.stack([value] + [self.hop(value, j) for j in range(1, self.tp)])

    def tp_parts(self, value):
        return [value] + [self.hop(value, j) for j in range(1, self.tp)]

    def to_owner(self, stack):
        return [stack[0]] + [self.hop(stack[j], j) for j in range(1, self.tp)]

    def to_rows(self, value):
        return lax.all_to_all(value, ("tp", "core", "fsdp"), 0, 0, tiled=True)

    def gather_cz(self, value):
        planes = jnp.stack([value] + [self.other_plane(value, k) for k in range(1, self.planes)])
        return jnp.concatenate([planes, self.other_core(planes)])


    def shuffle(self, shards):
        return lax.all_to_all(column_blocks(self.tp, shards), "tp", 0, 0, tiled=True)

    def gather_blocks(self, shard):
        return lax.all_gather(shard, ("core", "fsdp"), axis=0)


def blocks_kernel(moves, *refs):
    for source, begin, t, at, size in moves:
        refs[-1][t, :, at : at + size] = refs[source][:, begin : begin + size]


def column_blocks(tp, shards):
    moves, at = [], 0
    for source, (shard, kinds) in enumerate(shards):
        size = shard.shape[1] // (kinds * tp)
        for kind in range(kinds):
            moves += [(source, (kind * tp + t) * size, t, at, size) for t in range(tp)]
            at += size
    rows = shards[0][0].shape[0]
    return in_vmem(
        functools.partial(blocks_kernel, moves),
        "column_blocks",
        [shard for shard, _ in shards],
        [((tp, rows, at), BF)],
    )[0]


def parts_kernel(tp, kinds, place, shard, *parts):
    size = shard.shape[1] // (kinds * tp)
    for j in range(tp):
        for kind in range(kinds):
            begin = pl.multiple_of((kind * tp + (place[0] ^ j)) * size, HDIM)
            parts[j][:, kind * size : (kind + 1) * size] = shard[:, pl.ds(begin, size)]


def assemble_kernel(tp, place, *refs):
    parts, whole = refs[:tp], refs[tp]
    for j in range(tp):
        whole[place[0] ^ j] = parts[j][...]


def block(weights, t, columns):
    part = weights[:, t, :, columns]
    return part.reshape(part.shape[0] * part.shape[1], part.shape[2])


def project(rows, weights, columns):
    tp = weights.shape[1]
    step = rows.shape[1] // tp
    total = dot(rows[:, :step], block(weights, 0, columns))
    for t in range(1, tp):
        total = total + dot(rows[:, t * step : (t + 1) * step], block(weights, t, columns))
    return total


def start_copies(pairs, sems):
    copies = [pltpu.make_async_copy(a, b, sems.at[k]) for k, (a, b) in enumerate(pairs)]
    for copy in copies:
        copy.start()
    return copies


def softmax_head(queries, keys, bias, free, extra):
    scale = HDIM ** (-0.5)
    logits = dot_t(queries, keys[:free]) * scale
    if bias is not None:
        logits = logits + bias
    top = jnp.max(logits, axis=-1, keepdims=True)
    if not extra:
        weighs = jnp.exp(logits - top)
        return weighs / jnp.sum(weighs, axis=-1, keepdims=True), None
    one = dot_t(queries, keys[free:])[:, :1] * scale
    top = jnp.maximum(top, one)
    weighs, one = jnp.exp(logits - top), jnp.exp(one - top) * extra
    total = jnp.sum(weighs, axis=-1, keepdims=True) + one
    return weighs / total, one / total


def self_kernel(tp, local, count, *refs):
    entries, masked_entries, gathered, out_w = refs[:tp], refs[tp], refs[tp + 1], refs[tp + 2]
    partial = refs[tp + 3 : 2 * tp + 3]
    packed, mix_out, probs_out, weight, out_weight, held, mixed, sems = refs[2 * tp + 3 :]
    free, rows, span = entries[0].shape[0], packed.shape[1], local * HDIM
    pairs = [(ref, held.at[i * free : (i + 1) * free]) for i, ref in enumerate(entries)]
    pairs += [(masked_entries, held.at[tp * free :]), (gathered, weight), (out_w, out_weight)]
    copies = start_copies(pairs, sems)
    for copy in copies[:-1]:
        copy.wait()
    for k in range(3):
        cols = slice(k * span, (k + 1) * span)
        found = project(held[...], weight, cols).astype(BF)
        for i in range(tp):
            packed[i, :free, cols] = found[i * free : (i + 1) * free]
            packed[i, free:, cols] = found[tp * free :]
    probs_out[...] = jnp.zeros_like(probs_out)
    for i in range(tp):
        for h in range(local):
            cols = [slice(k * span + h * HDIM, k * span + (h + 1) * HDIM) for k in range(3)]
            queries, keys, values = (packed[i, :, c] for c in cols)
            probs, one = softmax_head(queries, keys, None, free, float(count))
            probs_out[i, h : h + 1, :free] = probs[free : free + 1]
            probs_out[i, h : h + 1, free:] = jnp.broadcast_to(one[free : free + 1], (1, TILE))
            mixture = dot(probs.astype(BF), values[:free])
            mixture = mixture + one.astype(BF).astype(F32) * values[free : free + 1].astype(F32)
            mixed[i * rows : (i + 1) * rows, cols[0]] = mixture.astype(BF)
        mix_out[i] = mixed[i * rows + free : (i + 1) * rows]
    copies[-1].wait()
    rows = packed.shape[1]
    for begin in range(0, partial[0].shape[1], 512):
        cols = slice(begin, begin + 512)
        part = out_weight[:, :, cols]
        added = dot(mixed[...], part.reshape(-1, 512)).astype(BF)
        for i in range(tp):
            partial[i][:, cols] = added[i * rows : (i + 1) * rows]


def write_out(tp, mixed, weight, partial):
    rows, width = partial[0].shape
    span = width // tp
    for t in range(tp):
        added = dot(mixed[...], block(weight, t, slice(3 * span, 4 * span))).astype(BF)
        for i in range(tp):
            partial[i][:, t * span : (t + 1) * span] = added[i * rows : (i + 1) * rows]


def masked_row(last, i, one_entry, one_row):
    last = last.astype(F32)
    one_entry[i : i + 1] = last[:1]
    one_row[i : i + 1] = last[1:2] + last[2:3] + last[3:4]


def cross_kernel(tp, local, *refs):
    entries, text = refs[:tp], refs[tp : 2 * tp]
    bias, gathered = refs[2 * tp : 2 * tp + 2]
    partial = refs[2 * tp + 2 : 3 * tp + 2]
    pair, query_out, mix_out, probs_out, one_entry, one_row = refs[3 * tp + 2 : 3 * tp + 8]
    weight, held, held_text, queries, mixed, sems = refs[3 * tp + 8 :]
    rows, txt, span = entries[0].shape[0], text[0].shape[0], local * HDIM
    free = rows - PAD
    pairs = [(ref, held_text.at[i * txt : (i + 1) * txt]) for i, ref in enumerate(text)]
    pairs += [(ref, held.at[i * rows : (i + 1) * rows]) for i, ref in enumerate(entries)]
    pairs += [(gathered, weight)]
    for copy in start_copies(pairs, sems):
        copy.wait()
    for k in range(2):
        cols = slice(k * span, (k + 1) * span)
        found = project(held_text[...], weight, cols).astype(BF)
        for i in range(tp):
            pair[i, :, cols] = found[i * txt : (i + 1) * txt]
    queries[...] = project(held[...], weight, slice(2 * span, 3 * span)).astype(BF)
    probs_out[...] = jnp.zeros_like(probs_out)
    for i in range(tp):
        masked_row(held[i * rows + free : (i + 1) * rows], i, one_entry, one_row)
        query_out[i] = queries[i * rows + free : (i + 1) * rows]
        for h in range(local):
            cols = slice(h * HDIM, (h + 1) * HDIM)
            keys = pair[i, :, cols]
            values = pair[i, :, span + h * HDIM : span + (h + 1) * HDIM]
            some = queries[i * rows : (i + 1) * rows, cols]
            probs, _ = softmax_head(some, keys, bias[i : i + 1], txt, 0)
            probs_out[i, h : h + 1] = probs[free : free + 1]
            mixed[i * rows : (i + 1) * rows, cols] = dot(probs.astype(BF), values).astype(BF)
        mix_out[i] = mixed[i * rows + free : (i + 1) * rows]
    write_out(tp, mixed, weight, partial)


def gelu_parts(value):
    slope = 0.7978845608
    bent = jnp.tanh(slope * (value + 0.044715 * value * value * value))
    half = 0.5 * (1.0 + bent)
    steep = slope * (1.0 + 3.0 * 0.044715 * value * value)
    return value * half, half + 0.5 * value * (1.0 - bent * bent) * steep


def up_kernel(tp, *refs):
    entries, (weight, active, held, sems) = refs[:tp], refs[tp:]
    rows = entries[0].shape[0]

    @pl.when(pl.program_id(0) == 0)
    def _():
        pairs = [(ref, held.at[i * rows : (i + 1) * rows]) for i, ref in enumerate(entries)]
        for copy in start_copies(pairs, sems):
            copy.wait()

    active[...] = gelu_parts(project(held[...], weight, slice(None)))[0].astype(BF)


def mlp_back_kernel(tp, *refs):
    entries_all, grad_active, gathered = refs[:tp], refs[tp], refs[tp + 1]
    active, grad_pre, grad_entry, one_entry, one_row, weight, last, entries, sem = refs[tp + 2 :]
    step, free = entries.shape[1] // tp, entries_all[0].shape[0] - PAD
    ends = [
        pltpu.make_async_copy(ref.at[free:], last.at[i], sem.at[tp + i])
        for i, ref in enumerate(entries_all)
    ]
    for copy in ends:
        copy.start()
    copies = [
        pltpu.make_async_copy(gathered.at[:, t], weight.at[:, t], sem.at[t]) for t in range(tp)
    ]
    for copy in copies:
        copy.start()
    for i, copy in enumerate(ends):
        copy.wait()
        masked_row(last[i], i, one_entry, one_row)
    entries[...] = jnp.zeros_like(entries)
    entries[:tp] = one_entry[...]
    hidden = jnp.zeros(active.shape, F32)
    for t, copy in enumerate(copies):
        copy.wait()
        rows = entries[:, t * step : (t + 1) * step].astype(BF)
        hidden = hidden + dot(rows, block(weight, t, slice(None)))
    value, steep = gelu_parts(hidden)
    active[...] = value.astype(BF)
    grad_pre[...] = (steep * grad_active[...]).astype(BF)
    for t in range(tp):
        back = dot_t(grad_pre[...], block(weight, t, slice(None)))
        grad_entry[:, t * step : (t + 1) * step] = back[:tp]


def summed(parts, i):
    total = parts[0][i : i + 1]
    for j in range(1, len(parts)):
        total = total + parts[j][i ^ j : (i ^ j) + 1]
    return total


def out_back(rows, weights, columns):
    tp = weights.shape[1]
    step = rows.shape[1] // tp
    total = dot_t(rows[:, :step], block(weights, 0, columns))
    for t in range(1, tp):
        total = total + dot_t(rows[:, t * step : (t + 1) * step], block(weights, t, columns))
    return total.astype(BF).astype(F32)


def head_mask(span):
    heads = lax.broadcasted_iota(jnp.int32, (8, span), 0)
    return lax.broadcasted_iota(jnp.int32, (8, span), 1) // HDIM == heads


def row_back(parts, rows, gain, base, i, out, gain_row):
    grad = summed(parts, i)
    field, scale = normed(rows[i : i + 1])
    out[i : i + 1] = base[i : i + 1] + norm_back(grad * gain[...], field, scale)
    if i == 0:
        gain_row[...] = grad * field


def cross_back_kernel(
    tp, base, rows, gain, pair, probs, gathered, *refs,
):
    parts = refs[:tp]
    grad_mid, grad_cmix, scores, grad_cq, grad_entry, gain_row = refs[tp : tp + 6]
    weight, held, sems = refs[tp + 6 :]
    span = weight.shape[3] // 2
    copies = [
        pltpu.make_async_copy(gathered.at[:, :, :, 2 * span :], weight, sems.at[0]),
    ]
    for copy in copies:
        copy.start()
    held[...] = jnp.zeros_like(held)
    for i in range(tp):
        row_back(parts, rows, gain, base, i, held, gain_row)
    grad_mid[...] = held[:tp]
    copies[0].wait()
    mixed = out_back(held[...].astype(BF), weight, slice(span, 2 * span))
    grad_cmix[...] = mixed[:tp]
    mask = head_mask(span)
    held[...] = jnp.zeros_like(held)
    for i in range(tp):
        spread = jnp.where(mask, mixed[i : i + 1], 0.0).astype(BF)
        grad_probs = dot_t(spread, pair[i, :, span:])
        weighs = probs[i]
        grad = weighs * (grad_probs - jnp.sum(grad_probs * weighs, axis=-1, keepdims=True))
        grad = grad.astype(BF)
        scores[i] = grad.astype(F32)
        back = jnp.where(mask, dot(grad, pair[i, :, :span]), 0.0)
        held[i : i + 1, :span] = jnp.sum(back, axis=0, keepdims=True) * HDIM ** (-0.5)
    grad_cq[...] = held[:tp, :span]
    queries = held[:, :span].astype(BF)
    step = grad_entry.shape[1] // tp
    for t in range(tp):
        back = dot_t(queries, block(weight, t, slice(0, span)))
        grad_entry[:, t * step : (t + 1) * step] = back[:tp]


def spread_heads(rows, i, spreads, mask):
    spreads[8 * i : 8 * i + 8] = jnp.where(mask, rows, 0.0)


def text_back_kernel(tp, local, *refs):
    scores, probs, query_one, grad_cmix, kvq = refs[:5]
    cross_one_row, mlp_one, grad_pre, grad_cq, mixed, cross, active, grad_mid = refs[5:13]
    text = refs[13 : 13 + tp]
    sent = refs[13 + tp : 13 + 2 * tp]
    lefts, factors, weight, held, keys, values, sems = refs[13 + 2 * tp :]
    span, width, txt = grad_cmix.shape[1], lefts.shape[1], scores.shape[2]
    copy = pltpu.make_async_copy(kvq.at[:, :, :, : 2 * span], weight, sems.at[0])
    copy.start()
    mask = head_mask(span)
    ff = grad_pre.shape[1]
    places, at = [], 0
    for size in (ff, span, span, span, span, span, ff, width):
        places.append(slice(at, at + size))
        at += size
    for i in range(tp):
        spread_heads(query_one[i].astype(F32)[:1], i, keys, mask)
        spread_heads(grad_cmix[i : i + 1], i, values, mask)
        both = jnp.concatenate([scores[i], probs[i]], axis=0).astype(BF)
        found = dot(both, text[i][...])
        for kind in range(2):
            begin = (2 * i + kind) * local
            lefts[begin : begin + local] = found[8 * kind : 8 * kind + local]
        sent[i][:, width:] = both
        for k, rows in ((2, query_one), (4, mixed), (5, cross)):
            held[i : i + 1, places[k]] = rows[i].astype(F32)[:1]
    held[:tp, places[0]] = grad_pre[...].astype(F32)[:tp]
    held[:tp, places[1]] = grad_cq[...]
    held[:tp, places[3]] = grad_cmix[...]
    held[:tp, places[6]] = active[...].astype(F32)[:tp]
    held[:tp, places[7]] = grad_mid[...]
    factors[...] = held[:tp].astype(BF)
    begin = 2 * tp * local
    lefts[begin : begin + tp] = cross_one_row[...]
    lefts[begin + tp :] = mlp_one[...]
    copy.wait()
    step = width // tp
    key_spread, value_spread = keys[...].astype(BF), values[...].astype(BF)
    for t in range(tp):
        cols = slice(t * step, (t + 1) * step)
        key_rows = dot_t(key_spread, block(weight, t, slice(0, span))) * HDIM ** (-0.5)
        value_rows = dot_t(value_spread, block(weight, t, slice(span, 2 * span)))
        for i in range(tp):
            eight = slice(8 * i, 8 * i + 8)
            both = jnp.concatenate([key_rows[eight], value_rows[eight]], axis=0)
            sent[i][:, cols] = both.astype(BF)


def self_back_kernel(
    tp, local, base, rows, gain, packed, probs, masked_entries, text_lefts, text_factors,
    gain_a, embed, gain_m_row, gathered, out_w, *refs,
):
    parts, entries, text_sent = refs[:tp], refs[tp : 2 * tp], refs[2 * tp : 3 * tp]
    sent, refs = refs[3 * tp : 4 * tp], refs[4 * tp :]
    payload, factors, weight, out_weight, held, spreads, lefts, small, sems = refs
    width = lefts.shape[1]
    span, free = weight.shape[3] // 3, entries[0].shape[0]
    copies = start_copies([(out_w, out_weight), (gathered, weight)], sems)
    ff = (text_factors.shape[1] - 5 * span - width) // 2
    cut = ff + 3 * span
    factors[:, :cut] = text_factors[:, :cut]
    factors[:, cut + 3 * span : -width] = text_factors[:, cut:]
    small[...] = jnp.zeros_like(small)
    small[3:4] = gain_m_row[...]
    held[...] = jnp.zeros_like(held)
    for i in range(tp):
        row_back(parts, rows, gain, base, i, held, small.at[2:3])
    small[0:1] = held[0:1]
    factors[:, -width:] = held[:tp].astype(BF)
    copies[0].wait()
    part = out_weight[...]
    mixed = dot_t(held[...].astype(BF), part.reshape(span, width)).astype(BF).astype(F32)
    factors[:, cut : cut + span] = mixed[:tp].astype(BF)
    mask = head_mask(span)
    held[...] = jnp.zeros_like(held)
    masked_row = masked_entries[:1].astype(F32)
    ones = []
    for i in range(tp):
        spread = jnp.where(mask, mixed[i : i + 1], 0.0)
        spreads[8 * i : 8 * i + 8] = spread
        spread = spread.astype(BF)
        values = packed[i, :, 2 * span :]
        grad_probs, grad_one = dot_t(spread, values[:free]), dot_t(spread, values[free:])[:, :1]
        weighs, one = probs[i, :, :free], probs[i, :, free : free + 1]
        mean = jnp.sum(grad_probs * weighs, axis=-1, keepdims=True) + grad_one * one
        grad = (weighs * (grad_probs - mean)).astype(BF)
        grad_one = (one * (grad_one - mean)).astype(BF).astype(F32)
        ones.append((grad_one, one))
        keys = packed[i, :, span : 2 * span]
        back = dot(grad, keys[:free]) + grad_one * keys[free : free + 1].astype(F32)
        back = jnp.sum(jnp.where(mask, back, 0.0), axis=0, keepdims=True)
        held[i : i + 1, :span] = back * HDIM ** (-0.5)
        both = jnp.concatenate([grad.astype(F32), weighs], axis=0).astype(BF)
        both_one = jnp.concatenate([grad_one, one], axis=0).astype(BF).astype(F32)
        found = dot(both, entries[i][...]) + both_one * masked_row
        for kind in range(2):
            begin = (2 * i + kind) * local
            lefts[begin : begin + local] = found[8 * kind : 8 * kind + local]
        sent[i][:PAD, width:] = both
        sent[i][PAD:] = text_sent[i][...]
    factors[:, cut + span : cut + 2 * span] = held[:tp, :span].astype(BF)
    queries = held[:, :span].astype(BF)
    zero_query = packed[0, free:, :span].astype(F32)[:1]
    factors[:, cut + 2 * span : cut + 3 * span] = jnp.broadcast_to(zero_query, (tp, span)).astype(BF)
    key_spread = jnp.where(mask, zero_query, 0.0).astype(BF)
    value_spread = spreads[...].astype(BF)
    step = width // tp
    field, scale = normed(embed[...])
    copies[1].wait()
    for t in range(tp):
        cols = slice(t * step, (t + 1) * step)
        keys = dot_t(key_spread, block(weight, t, slice(span, 2 * span))) * HDIM ** (-0.5)
        values = dot_t(value_spread, block(weight, t, slice(2 * span, 3 * span)))
        query_rows = dot_t(queries, block(weight, t, slice(0, span)))
        masked_grad, gain_grad = 0.0, 0.0
        for i in range(tp):
            mine = values[8 * i : 8 * i + 8]
            sent[i][:PAD, cols] = jnp.concatenate([keys, mine], axis=0).astype(BF)
            last = query_rows[i : i + 1]
            found = ones[i][0] * keys + ones[i][1] * mine
            masked_grad = masked_grad + last + jnp.sum(found, axis=0, keepdims=True)
            for kind, rows_back in enumerate((keys, mine)):
                begin = (2 * i + kind) * local
                found = lefts[begin : begin + local, cols] * rows_back[:local]
                gain_grad = gain_grad + jnp.sum(found, axis=0, keepdims=True)
        gain_grad = gain_grad / gain_a[:, cols]
        rows_sum = jnp.sum(query_rows[:tp], axis=0, keepdims=True)
        small[1:2, cols] = gain_grad + rows_sum * field[:, cols]
        held[0:1, cols] = masked_grad
    small[0:1] = small[0:1] + norm_back(held[0:1] * gain_a[...], field, scale)
    begin = 2 * tp * local
    lefts[begin : begin + text_lefts.shape[0]] = text_lefts[...]
    begin += text_lefts.shape[0]
    high = small[:4].astype(BF).astype(F32)
    lefts[begin : begin + 4] = high
    lefts[begin + 4 : begin + 8] = small[:4] - high
    half, own = lefts.shape[0] // 2, payload.shape[2] // 2
    for d in range(payload.shape[0]):
        cols = slice(d * own, (d + 1) * own)
        both = jnp.concatenate([lefts[:half, cols], lefts[half:, cols]], axis=1)
        payload[d] = both.astype(BF)


def tokens_back_kernel(tp, rows, gain, place, *refs):
    came, (tokens, text) = refs[:tp], refs[tp:]
    width, free = rows.shape[1], place.shape[1]
    grad, grad_text = 0.0, 0.0
    for part in came:
        grad = grad + dot_sum(part[:PAD, width:], part[:PAD, :width])
        grad_text = grad_text + dot_sum(part[PAD:, width:], part[PAD:, :width])
    text[...] = grad_text.astype(BF)
    field, scale = normed(rows[:free])
    start = norm_back(grad * gain[...], field, scale)
    tokens[...] = dot(place[...], start.astype(BF)).astype(BF)


def stack_kernel(*refs):
    for k, ref in enumerate(refs[:-1]):
        refs[-1][k] = ref[...]


def unpack_kernel(planes, others, right, group, held):
    count, tp = planes.shape[:2]
    for k in range(count):
        held[k * tp : (k + 1) * tp] = planes[k].astype(F32)
        held[(count + k) * tp : (count + k + 1) * tp] = others[k].astype(F32)
    right[...] = held[:, : right.shape[1]].astype(BF)
    group[...] = held[:, right.shape[1] :].astype(BF)


def aligned(right, corner, tp):
    count = right.shape[0]
    out = lax.broadcasted_iota(jnp.int32, (count, count), 0)
    into = lax.broadcasted_iota(jnp.int32, (count, count), 1)
    same = (out // tp == (corner ^ (into // tp))) & (out % tp == into % tp)
    return dot(same.astype(BF), right).astype(BF)


def columns_kernel(local, place, attn_left, text_left, one_left, entry, *refs):
    right, (grad_qkv, grad_kv, grad_cq, grad_up) = refs[:-4], refs[-4:]
    tp, span = len(right), local * HDIM
    ff = right[0].shape[1] - 6 * span
    ones = jnp.ones((right[0].shape[0], HDIM), BF)
    scale = HDIM ** (-0.5)

    def at_columns(begin, size):
        return pl.ds(pl.multiple_of(begin, HDIM), size)

    for j in range(tp):
        at = place[0] ^ j
        rows = aligned(right[j][...], place[1], tp)
        part = [rows[:, ff + k * span : ff + (k + 1) * span] for k in range(6)]
        grad_up[:, at_columns(at * ff, ff)] = dot_sum(one_left[at, 1], rows[:, :ff])
        grad_cq[:, at_columns(at * span, span)] = dot_sum(one_left[at, 0], part[0])
        total = jnp.sum(part[4].astype(F32), axis=0, keepdims=True)
        grad_qkv[:, at_columns(at * span, span)] = entry[...] * total
        queries = part[5].astype(F32)[:1] * scale
        for h in range(local):
            cols = slice(h * HDIM, (h + 1) * HDIM)
            begin = at * span + h * HDIM
            outer = dot_sum(text_left[at, 0, h], part[1][:, cols])
            grad_kv[:, at_columns(begin, HDIM)] = outer * scale
            outer = dot_sum(text_left[at, 1, h], part[2][:, cols])
            grad_kv[:, at_columns(tp * span + begin, HDIM)] = outer
            outer = dot_sum(attn_left[at, 0, h], ones) * queries[:, cols]
            grad_qkv[:, at_columns(tp * span + begin, HDIM)] = outer
            outer = dot_sum(attn_left[at, 1, h], part[3][:, cols])
            grad_qkv[:, at_columns(2 * tp * span + begin, HDIM)] = outer


def whole_spec():
    return pl.BlockSpec(memory_space=pl.ANY)


def in_vmem(kernel, name, operands, out_shape, scratch_shapes=(), held=()):
    spaces = dict(held)
    return pl.pallas_call(
        kernel,
        in_specs=[
            pl.BlockSpec(memory_space=spaces.get(k, pltpu.VMEM)) for k in range(len(operands))
        ],
        out_specs=[pl.BlockSpec(memory_space=pltpu.VMEM)] * len(out_shape),
        out_shape=[jax.ShapeDtypeStruct(shape, dtype) for shape, dtype in out_shape],
        scratch_shapes=scratch_shapes,
        compiler_params=pltpu.CompilerParams(vmem_limit_bytes=VMEM_BYTES),
        cost_estimate=COST,
        name=name,
    )(*operands)


def self_forward(local, count, entries, masked_entries, gathered, out_w):
    tp, (free, width) = len(entries), entries[0].shape
    span, rows = local * HDIM, free + PAD
    found = in_vmem(
        functools.partial(self_kernel, tp, local, count),
        "self_attention",
        [*entries, masked_entries, gathered, out_w],
        [((rows, width), BF)] * tp
        + [((tp, rows, 3 * span), BF), ((tp, PAD, span), BF), ((tp, 8, free + TILE), F32)],
        [
            pltpu.VMEM(gathered.shape, BF),
            pltpu.VMEM(out_w.shape, BF),
            pltpu.VMEM((tp * free + PAD, width), BF),
            pltpu.VMEM((tp * rows, span), BF),
            pltpu.SemaphoreType.DMA((tp + 3,)),
        ],
        [(k, pl.ANY) for k in range(tp + 3)],
    )
    return found[:tp], *found[tp:]


def cross_forward(local, entries, text, bias, gathered):
    tp, (rows, width) = len(entries), entries[0].shape
    txt, span = text[0].shape[0], local * HDIM
    found = in_vmem(
        functools.partial(cross_kernel, tp, local),
        "cross_attention",
        [*entries, *text, bias, gathered],
        [((rows, width), BF)] * tp
        + [
            ((tp, txt, 2 * span), BF),
            ((tp, PAD, span), BF),
            ((tp, PAD, span), BF),
            ((tp, 8, txt), F32),
            ((tp, width), F32),
            ((tp, width), F32),
        ],
        [
            pltpu.VMEM(gathered.shape, BF),
            pltpu.VMEM((tp * rows, width), BF),
            pltpu.VMEM((tp * txt, width), BF),
            pltpu.VMEM((tp * rows, span), BF),
            pltpu.VMEM((tp * rows, span), BF),
            pltpu.SemaphoreType.DMA((2 * tp + 1,)),
        ],
        [(k, pl.ANY) for k in range(2 * tp + 2) if k != 2 * tp],
    )
    return found[:tp], *found[tp:]


def down_kernel(tp, active, gathered, *refs):
    partial, (weight, sems) = refs[:tp], refs[tp:]
    rows, width = partial[0].shape
    step = min(512, width)
    parts = [slice(at, at + step) for at in range(0, width, step)]
    copies = start_copies([(gathered.at[:, :, cols], weight.at[:, :, cols]) for cols in parts], sems)
    for cols, copy in zip(parts, copies):
        copy.wait()
        part = weight[:, :, cols]
        added = dot(active[...], part.reshape(-1, step)).astype(BF)
        for i in range(tp):
            partial[i][:, cols] = added[i * rows : (i + 1) * rows]


def mlp_down(tp, active, gathered):
    rows, width = active.shape[0] // tp, gathered.shape[2]
    return in_vmem(
        functools.partial(down_kernel, tp),
        "mlp_down",
        [active, gathered],
        [((rows, width), BF)] * tp,
        [pltpu.VMEM(gathered.shape, BF), pltpu.SemaphoreType.DMA((width // min(512, width),))],
        ((1, pl.ANY),),
    )


def mlp_up(entries, gathered):
    tp, (rows, width) = len(entries), entries[0].shape
    blocks, _, own, ff = gathered.shape
    step = min(ff, 512)
    return pl.pallas_call(
        functools.partial(up_kernel, tp),
        grid=(ff // step,),
        in_specs=[whole_spec()] * tp
        + [pl.BlockSpec((blocks, tp, own, step), lambda i: (0, 0, 0, i))],
        out_specs=pl.BlockSpec((tp * rows, step), lambda i: (0, i)),
        out_shape=jax.ShapeDtypeStruct((tp * rows, ff), BF),
        scratch_shapes=[
            pltpu.VMEM((tp * rows, width), BF),
            pltpu.SemaphoreType.DMA((tp,)),
        ],
        compiler_params=pltpu.CompilerParams(vmem_limit_bytes=VMEM_BYTES),
        cost_estimate=COST,
        name="mlp_up",
    )(*entries, gathered)


def mlp_back(entries, grad_active, gathered):
    tp, width = len(entries), entries[0].shape[1]
    ff = gathered.shape[3]
    return in_vmem(
        functools.partial(mlp_back_kernel, tp),
        "mlp_back",
        [*entries, grad_active, gathered],
        [
            ((PAD, ff), BF),
            ((PAD, ff), BF),
            ((tp, width), F32),
            ((tp, width), F32),
            ((tp, width), F32),
        ],
        [
            pltpu.VMEM(gathered.shape, BF),
            pltpu.VMEM((tp, PAD, width), BF),
            pltpu.VMEM((PAD, width), F32),
            pltpu.SemaphoreType.DMA((2 * tp,)),
        ],
        [(k, pl.ANY) for k in range(tp + 2) if k != tp],
    )


def cross_back(base, rows, gain, pair, probs, gathered, parts):
    tp, width = base.shape
    blocks, _, own, columns = gathered.shape
    span = columns // 4
    return in_vmem(
        functools.partial(cross_back_kernel, tp),
        "cross_back",
        [base, rows, gain[None], pair, probs, gathered, *parts],
        [
            ((tp, width), F32),
            ((tp, span), F32),
            (probs.shape, F32),
            ((tp, span), F32),
            ((tp, width), F32),
            ((1, width), F32),
        ],
        [
            pltpu.VMEM((blocks, tp, own, 2 * span), BF),
            pltpu.VMEM((8, width), F32),
            pltpu.SemaphoreType.DMA((1,)),
        ],
        ((5, pl.ANY),),
    )


def text_back(local, scores, probs, query_one, grad_cmix, kvq, rest, text):
    tp, span = grad_cmix.shape
    blocks, _, own, _ = kvq.shape
    (txt, width), ff = text[0].shape, rest[2].shape[1]
    found = in_vmem(
        functools.partial(text_back_kernel, tp, local),
        "text_back",
        [scores, probs, query_one, grad_cmix, kvq, *rest, *text],
        [((PAD, width + txt), BF)] * tp
        + [((2 * tp * (local + 1), width), F32), ((tp, 2 * ff + 5 * span + width), BF)],
        [
            pltpu.VMEM((blocks, tp, own, 2 * span), BF),
            pltpu.VMEM((8, 2 * ff + 5 * span + width), F32),
            pltpu.VMEM((8 * tp, span), F32),
            pltpu.VMEM((8 * tp, span), F32),
            pltpu.SemaphoreType.DMA((1,)),
        ],
        ((4, pl.ANY),),
    )
    return found[:tp], *found[tp:]


def self_back(local, world, small_operands, gathered, out_w, parts, entries, text_sent):
    tp, width = small_operands[0].shape
    text_lefts, text_factors = small_operands[6], small_operands[7]
    _, _, own, columns = gathered.shape
    span, free = columns // 3, entries[0].shape[0]
    count = 2 * tp * local + text_lefts.shape[0] + 8
    operands = [*small_operands, gathered, out_w, *parts, *entries, *text_sent]
    found = in_vmem(
        functools.partial(self_back_kernel, tp, local),
        "self_back",
        operands,
        [((2 * PAD, width + free), BF)] * tp
        + [((world, count // 2, 2 * own), BF), ((tp, text_factors.shape[1] + 3 * span + width), BF)],
        [
            pltpu.VMEM(gathered.shape, BF),
            pltpu.VMEM(out_w.shape, BF),
            pltpu.VMEM((8, width), F32),
            pltpu.VMEM((8 * tp, span), F32),
            pltpu.VMEM((count, width), F32),
            pltpu.VMEM((8, width), F32),
            pltpu.SemaphoreType.DMA((2,)),
        ],
        [(len(small_operands) + k, pl.ANY) for k in range(2)],
    )
    return found[:tp], *found[tp:]


def stacked(pieces):
    shape = (len(pieces),) + pieces[0].shape
    return in_vmem(stack_kernel, "stack", pieces, [(shape, BF)])[0]


def unpack(planes, others, cut):
    count, tp, wide = planes.shape
    rows = 2 * count * tp
    return in_vmem(
        unpack_kernel,
        "unpack",
        [planes, others],
        [((rows, cut), BF), ((rows, wide - cut), BF)],
        [pltpu.VMEM((rows, wide), F32)],
    )


def join_kernel(free, base, gain, *refs):
    parts, (total, entries) = refs[:-2], refs[-2:]
    value = base[...]
    for part in parts:
        value = value + part[...].astype(F32)
    total[...] = value
    found = normed(value)[0] * gain[...]
    entries[...] = found.astype(BF)

    @pl.when(pl.program_id(0) == pl.num_programs(0) - 1)
    def _():
        at = value.shape[0] - PAD
        row = value[at : at + 1]
        spot = lax.broadcasted_iota(jnp.int32, (PAD, value.shape[1]), 0)
        last = found[at:]
        for k in range(3):
            part = row.astype(BF).astype(F32)
            last = jnp.where(spot == k + 1, part, last)
            row = row - part
        entries[at:] = last.astype(BF)


def join(base, parts, gain):
    rows, width = base.shape
    step = PAD * 3 if rows % (PAD * 3) == 0 else PAD
    block = pl.BlockSpec((step, width), lambda i: (i, 0))
    return pl.pallas_call(
        functools.partial(join_kernel, rows - PAD),
        grid=(rows // step,),
        in_specs=[block, pl.BlockSpec((1, width), lambda i: (0, 0))] + [block] * len(parts),
        out_specs=[block, block],
        out_shape=[
            jax.ShapeDtypeStruct((rows, width), F32),
            jax.ShapeDtypeStruct((rows, width), BF),
        ],
        compiler_params=pltpu.CompilerParams(vmem_limit_bytes=VMEM_BYTES),
        cost_estimate=COST,
        name="join",
    )(base, gain[None], *parts)


def shards(
    tp,
    planes,
    tokens,
    text,
    cotangent,
    positions,
    text_lengths,
    mask_embed,
    gain_attn,
    w_qkv,
    w_attn_out,
    gain_cross,
    w_cross_q,
    w_cross_kv,
    w_cross_out,
    gain_mlp,
    w_up,
    w_down,
):
    me = Layer(tp, planes)
    seq, width = tokens.shape
    masked_count = positions.shape[1]
    free = seq - masked_count
    txt = text.shape[1]
    local = HEADS // tp
    rows = free + PAD
    device = (me.t * 2 + me.c) * planes + me.z
    world = tp * 2 * planes
    own = width // world

    def after(value, earlier):
        return lax.optimization_barrier((value, earlier))[0]

    span = local * HDIM

    out_w = me.gather_blocks(w_attn_out)
    corner = me.c * planes + me.z
    place_at = jnp.stack([me.t, corner]).astype(jnp.int32)
    in_smem = ((0, pltpu.SMEM),)
    parts = in_vmem(
        functools.partial(parts_kernel, tp, 3),
        "parts",
        [place_at, w_qkv],
        [((own, 3 * span), BF)] * tp,
        held=in_smem,
    )
    attn_sent = in_vmem(
        functools.partial(assemble_kernel, tp),
        "assemble",
        [place_at, *me.to_owner(parts)],
        [((tp, own, 3 * span), BF)],
        held=in_smem,
    )[0]

    cot_sum = jnp.sum(cotangent[0].astype(F32), axis=0)
    vectors = jnp.concatenate([mask_embed, gain_attn, gain_cross, gain_mlp]).astype(F32)
    fill = TILE - vectors.shape[0] % TILE
    length = jnp.broadcast_to(text_lengths.astype(F32), (fill,))
    gathered = after(jnp.concatenate([cot_sum, vectors, length]), attn_sent)
    gathered = me.tp_direct(me.gather_cz(gathered))
    others = after((w_cross_kv, w_cross_q, w_cross_out), (gathered, attn_sent))
    kvq_sent = me.shuffle([(others[0], 2), (others[1], 1)])
    cross_sent = jnp.concatenate([kvq_sent, column_blocks(tp, [(others[2], 1)])], axis=2)
    attn_w = me.gather_blocks(after(attn_sent, (out_w, gathered)))
    vectors = gathered[:, :, width : width + 4 * own].reshape(world, 4, own)
    vectors = xor_order(vectors, device, world).transpose(1, 0, 2).reshape(4, width)
    embed, gain_a, gain_c, gain_m = vectors[0], vectors[1], vectors[2], vectors[3]
    lengths = gathered[:, 0, width + 4 * own :][:, :1]
    text_bias = jnp.where(
        lax.broadcasted_iota(jnp.int32, (tp, txt), 1).astype(F32) < lengths, 0.0, -1e30
    )
    cot_group = gathered[:, 0, :width]

    spots = lax.broadcasted_iota(jnp.int32, (masked_count, seq), 1)
    masked = jnp.sum((positions[0][:, None] == spots).astype(F32), axis=0)
    below = lax.broadcasted_iota(jnp.int32, (seq, seq), 0) <= lax.broadcasted_iota(
        jnp.int32, (seq, seq), 1
    )
    rank = dot((1.0 - masked).astype(BF)[None, :], below.astype(BF))[0]
    ranks = lax.broadcasted_iota(jnp.int32, (free, seq), 0).astype(F32) + 1.0
    pick = ((rank[None, :] == ranks) & (masked[None, :] == 0.0)).astype(BF)
    place = jnp.concatenate(
        [pick.T, masked[:, None].astype(BF), jnp.zeros((seq, PAD - 1), BF)], axis=1
    )
    start_free = dot(pick, tokens)
    start = jnp.concatenate([start_free, jnp.broadcast_to(embed[None], (PAD, width))])

    cot_rows = gathered[:, :, :width].reshape(world, width)
    high = cot_rows.astype(BF)
    low = (cot_rows - high.astype(F32)).astype(BF)
    through = dot_t(jnp.concatenate([high, low]), w_down)
    through = through[:world] + through[world:]
    through = through.reshape(tp, 2 * planes, -1).transpose(1, 0, 2)
    through = xor_order(through, me.c * planes + me.z, 2 * planes)
    through = lax.all_to_all(after(through, kvq_sent), ("core", "fsdp"), 0, 0, tiled=True)
    grad_active = through.transpose(1, 0, 2).reshape(tp, -1)

    field_a, scale_a = normed(start)
    entries = (field_a * gain_a[None]).astype(BF)
    masked_entries = entries[free:]
    entries_all = me.spread(entries[:free])
    text_rows = me.spread(after(text[0], entries_all))
    up_sent = me.shuffle([(after(w_up, (entries_all, kvq_sent)), 1)])
    cross_w = me.gather_blocks(after(cross_sent, (attn_w, entries_all, up_sent, place, masked_entries, text_bias)))
    partial, packed, mixed_one, probs_one = self_forward(
        local, masked_count, entries_all, masked_entries, attn_w, out_w
    )
    after_attn, cross_entries = join(after(start, (grad_active, place)), me.collect(after(tuple(partial), text_rows)), gain_c)

    cross_all = me.spread(cross_entries)
    up = me.gather_blocks(after(up_sent, (cross_w, cross_all)))
    partial, pair, query_one, cross_one, cross_probs_one, cross_entry, attn_stream = cross_forward(
        local, cross_all, text_rows, text_bias, cross_w
    )
    after_cross, mlp_entries = join(after_attn, me.collect(partial), gain_m)

    mlp_all = me.spread(mlp_entries)
    most = width * 3 // 4
    down = me.gather_blocks(after(w_down[:, :most], (up, mlp_all)))

    active_one, grad_pre, grad_entry, mlp_one, cross_stream = mlp_back(
        mlp_all, jnp.pad(grad_active, ((0, PAD - tp), (0, 0))), up
    )
    grad_mid, grad_cmix, scores, grad_cq, grad_entry, grad_gain_m = cross_back(
        cot_group, cross_stream, gain_m, pair, cross_probs_one, cross_w, me.tp_parts(grad_entry)
    )
    text_sent, text_lefts, text_factors = text_back(
        local,
        scores,
        cross_probs_one,
        query_one,
        grad_cmix,
        cross_w,
        [
            cross_entry,
            mlp_one,
            grad_pre,
            grad_cq,
            mixed_one,
            cross_one,
            active_one,
            grad_mid,
        ],
        text_rows,
    )
    sent, payload, factors = self_back(
        local,
        world,
        [
            grad_mid,
            attn_stream,
            gain_c[None],
            packed,
            probs_one,
            masked_entries,
            text_lefts,
            text_factors,
            gain_a[None],
            embed[None],
            grad_gain_m,
        ],
        attn_w,
        out_w,
        me.tp_parts(grad_entry),
        entries_all,
        text_sent,
    )
    came = me.to_owner(sent)

    ff = grad_pre.shape[1]
    active = mlp_up(after(tuple(mlp_all), payload), up)
    pieces = [factors] + [me.other_plane(factors, k) for k in range(1, planes)]
    planes_of = stacked(after(tuple(pieces), (active, came)))
    lefts = me.to_rows(after(payload, planes_of))
    right, group = unpack(planes_of, me.other_core(planes_of), ff + 6 * span)
    right = [right] + [me.hop(right, j) for j in range(1, tp)]

    active, _ = lax.optimization_barrier((active, right[0]))
    down_rest = me.gather_blocks(after(w_down[:, most:], (down, active)))
    partial = mlp_down(tp, active, down)
    collected = me.collect(partial)
    active = after(active, tuple(partial))

    grad_tokens, grad_text = in_vmem(
        functools.partial(tokens_back_kernel, tp),
        "tokens_back",
        [start, gain_a[None], pick.T, *after(tuple(came), partial)],
        [((seq, width), BF), ((txt, width), BF)],
    )

    partial = mlp_down(tp, after(active, grad_tokens), down_rest)
    collected_rest = me.collect(partial)

    heads = 2 * tp * local
    lefts = after(lefts, partial)
    lefts = jnp.concatenate([lefts[:, :, :own], lefts[:, :, own:]], axis=1)
    attn_left, text_left = (
        lefts[:, k * heads : (k + 1) * heads]
        .reshape(tp, 2 * planes, tp, 2, local, own)
        .transpose(0, 3, 4, 1, 2, 5)
        .reshape(tp, 2, local, world, own)
        for k in range(2)
    )
    one_left = lefts[:, 2 * heads : 2 * heads + 2 * tp].reshape(tp, 2 * planes, 2, tp, own)
    one_left = one_left.transpose(0, 2, 1, 3, 4).reshape(tp, 2, world, own)
    small = jnp.sum(lefts[:, 2 * heads + 2 * tp :].astype(F32), axis=0)
    small = small[:4] + small[4:]
    entry_own = lax.dynamic_slice_in_dim(entries[free], device * own, own).astype(F32)
    grad_w_qkv, grad_w_kv, grad_w_cq, grad_w_up = in_vmem(
        functools.partial(columns_kernel, local),
        "columns",
        [place_at, attn_left, text_left, one_left, entry_own[:, None], *right],
        [((own, 3 * width), F32), ((own, 2 * width), F32), ((own, width), F32), ((own, tp * ff), F32)],
        held=in_smem,
    )

    def mine(stack):
        size = stack.shape[1] // (2 * planes)
        return lax.dynamic_slice_in_dim(stack, corner * size, size, axis=1)

    group = after(group, partial)
    cuts = [span, 2 * span, 2 * span + ff, 2 * span + ff + width]
    mixed_f, cross_f, active_f, mid_f, attn_f = jnp.split(group, cuts, axis=1)
    cot_f = gathered[:, :, :width].astype(BF).swapaxes(0, 1).reshape(world, width)
    grad_w_out = dot_sum(mine(mixed_f), attn_f)
    grad_w_cout = dot_sum(mine(cross_f), mid_f)
    grad_w_down = dot_sum(mine(active_f), cot_f)
    collected_rest = after(tuple(collected_rest), (grad_w_qkv, grad_w_out, grad_w_cout, grad_w_down, small))
    output = [sum(p.astype(F32) for p in parts) for parts in (collected, collected_rest)]
    output = after_cross + jnp.concatenate(output, axis=1)
    output = dot(place, output.astype(BF)).astype(BF)
    return (
        output,
        grad_tokens,
        grad_text[None],
        small[0],
        small[1],
        grad_w_qkv,
        grad_w_out,
        small[2],
        grad_w_cq,
        grad_w_kv,
        grad_w_cout,
        small[3],
        grad_w_up,
        grad_w_down,
    )


def solution(mesh):
    tp, planes = mesh.shape["dp"] // 2, mesh.shape["fsdp"]
    fine = Mesh(mesh.devices.reshape(tp, 2, planes), ("tp", "core", "fsdp"))
    every = ("tp", "core", "fsdp")
    one, two, three = P(every), P(every, None), P(every, None, None)

    def layer(*arguments):
        return shards(tp, planes, *arguments)

    return jax.shard_map(
        layer,
        mesh=fine,
        in_specs=(two, three, three, two, one, one, one, two, two, one, two, two, two, one, two, two),
        out_specs=(two, two, three, one, one, two, two, one, two, two, two, one, two, two),
        check_vma=False,
    )
```

```python
import functools

import jax
import jax.numpy as jnp
from jax import lax
from jax.experimental import pallas as pl
from jax.experimental.pallas import tpu as pltpu
from jax.sharding import Mesh, PartitionSpec as P

HEADS = 16
HDIM = 128
TILE = 128
PAD = 16
BF = jnp.bfloat16
F32 = jnp.float32
VMEM_BYTES = 60 << 20
COST = pl.CostEstimate(flops=1, bytes_accessed=1, transcendentals=0)


def dot(left, right):
    return jnp.dot(left, right, preferred_element_type=F32)


def dot_t(left, right):
    return lax.dot_general(left, right, (((1,), (1,)), ((), ())), preferred_element_type=F32)


def dot_sum(left, right):
    return lax.dot_general(left, right, (((0,), (0,)), ((), ())), preferred_element_type=F32)


def normed(rows):
    centered = rows - jnp.mean(rows, axis=-1, keepdims=True)
    scale = lax.rsqrt(jnp.mean(centered * centered, axis=-1, keepdims=True) + 1e-05)
    return centered * scale, scale


def norm_back(grad, field, scale):
    return scale * (
        grad
        - jnp.mean(grad, axis=-1, keepdims=True)
        - field * jnp.mean(grad * field, axis=-1, keepdims=True)
    )


def xor_order(stack, me, size):
    bit = 1
    while bit < size:
        split = stack.reshape((size // (2 * bit), 2, bit) + stack.shape[1:])
        turned = jnp.concatenate([split[:, 1:], split[:, :1]], axis=1)
        stack = jnp.where((me & bit) != 0, turned, split).reshape(stack.shape)
        bit *= 2
    return stack


def bits_of(size):
    return [1 << k for k in range(size.bit_length() - 1)]


class Layer:
    def __init__(self, tp, planes):
        self.tp, self.planes = tp, planes
        self.t, self.c, self.z = (lax.axis_index(a) for a in ("tp", "core", "fsdp"))


    def hop(self, value, j):
        return lax.ppermute(value, "tp", [(i, i ^ j) for i in range(self.tp)])

    def other_core(self, value):
        return lax.ppermute(value, "core", [(0, 1), (1, 0)])

    def other_plane(self, value, k):
        return lax.ppermute(value, "fsdp", [(i, i ^ k) for i in range(self.planes)])

    def spread(self, value):
        return [value] + [self.hop(value, j) for j in range(1, self.tp)]

    def collect(self, parts):
        return [parts[0]] + [self.hop(parts[j], j) for j in range(1, self.tp)]

    def tp_direct(self, value):
        return jnp.stack([value] + [self.hop(value, j) for j in range(1, self.tp)])

    def tp_parts(self, value):
        return [value] + [self.hop(value, j) for j in range(1, self.tp)]

    def to_owner(self, stack):
        return [stack[0]] + [self.hop(stack[j], j) for j in range(1, self.tp)]

    def to_rows(self, value):
        return lax.all_to_all(value, ("tp", "core", "fsdp"), 0, 0, tiled=True)

    def gather_cz(self, value):
        planes = jnp.stack([value] + [self.other_plane(value, k) for k in range(1, self.planes)])
        return jnp.concatenate([planes, self.other_core(planes)])


    def shuffle(self, shards):
        return lax.all_to_all(column_blocks(self.tp, shards), "tp", 0, 0, tiled=True)

    def gather_blocks(self, shard):
        return lax.all_gather(shard, ("core", "fsdp"), axis=0)


def blocks_kernel(moves, *refs):
    for source, begin, t, at, size in moves:
        refs[-1][t, :, at : at + size] = refs[source][:, begin : begin + size]


def column_blocks(tp, shards):
    moves, at = [], 0
    for source, (shard, kinds) in enumerate(shards):
        size = shard.shape[1] // (kinds * tp)
        for kind in range(kinds):
            moves += [(source, (kind * tp + t) * size, t, at, size) for t in range(tp)]
            at += size
    rows = shards[0][0].shape[0]
    return in_vmem(
        functools.partial(blocks_kernel, moves),
        "column_blocks",
        [shard for shard, _ in shards],
        [((tp, rows, at), BF)],
    )[0]


def parts_kernel(tp, kinds, place, shard, *parts):
    size = shard.shape[1] // (kinds * tp)
    for j in range(tp):
        for kind in range(kinds):
            begin = pl.multiple_of((kind * tp + (place[0] ^ j)) * size, HDIM)
            parts[j][:, kind * size : (kind + 1) * size] = shard[:, pl.ds(begin, size)]


def assemble_kernel(tp, place, *refs):
    parts, whole = refs[:tp], refs[tp]
    for j in range(tp):
        whole[place[0] ^ j] = parts[j][...]


def block(weights, t, columns):
    part = weights[:, t, :, columns]
    return part.reshape(part.shape[0] * part.shape[1], part.shape[2])


def project(rows, weights, columns):
    tp = weights.shape[1]
    step = rows.shape[1] // tp
    total = dot(rows[:, :step], block(weights, 0, columns))
    for t in range(1, tp):
        total = total + dot(rows[:, t * step : (t + 1) * step], block(weights, t, columns))
    return total


def start_copies(pairs, sems):
    copies = [pltpu.make_async_copy(a, b, sems.at[k]) for k, (a, b) in enumerate(pairs)]
    for copy in copies:
        copy.start()
    return copies


def softmax_head(queries, keys, bias, free, extra):
    scale = HDIM ** (-0.5)
    logits = dot_t(queries, keys[:free]) * scale
    if bias is not None:
        logits = logits + bias
    top = jnp.max(logits, axis=-1, keepdims=True)
    if not extra:
        weighs = jnp.exp(logits - top)
        return weighs / jnp.sum(weighs, axis=-1, keepdims=True), None
    one = dot_t(queries, keys[free:])[:, :1] * scale
    top = jnp.maximum(top, one)
    weighs, one = jnp.exp(logits - top), jnp.exp(one - top) * extra
    total = jnp.sum(weighs, axis=-1, keepdims=True) + one
    return weighs / total, one / total


def self_kernel(tp, local, count, *refs):
    entries, masked_entries, gathered, out_w = refs[:tp], refs[tp], refs[tp + 1], refs[tp + 2]
    partial = refs[tp + 3 : 2 * tp + 3]
    packed, mix_out, probs_out, weight, out_weight, held, mixed, sems = refs[2 * tp + 3 :]
    free, rows, span = entries[0].shape[0], packed.shape[1], local * HDIM
    pairs = [(ref, held.at[i * free : (i + 1) * free]) for i, ref in enumerate(entries)]
    pairs += [(masked_entries, held.at[tp * free :]), (gathered, weight), (out_w, out_weight)]
    copies = start_copies(pairs, sems)
    for copy in copies[:-1]:
        copy.wait()
    for k in range(3):
        cols = slice(k * span, (k + 1) * span)
        found = project(held[...], weight, cols).astype(BF)
        for i in range(tp):
            packed[i, :free, cols] = found[i * free : (i + 1) * free]
            packed[i, free:, cols] = found[tp * free :]
    probs_out[...] = jnp.zeros_like(probs_out)
    for i in range(tp):
        for h in range(local):
            cols = [slice(k * span + h * HDIM, k * span + (h + 1) * HDIM) for k in range(3)]
            queries, keys, values = (packed[i, :, c] for c in cols)
            probs, one = softmax_head(queries, keys, None, free, float(count))
            probs_out[i, h : h + 1, :free] = probs[free : free + 1]
            probs_out[i, h : h + 1, free:] = jnp.broadcast_to(one[free : free + 1], (1, TILE))
            mixture = dot(probs.astype(BF), values[:free])
            mixture = mixture + one.astype(BF).astype(F32) * values[free : free + 1].astype(F32)
            mixed[i * rows : (i + 1) * rows, cols[0]] = mixture.astype(BF)
        mix_out[i] = mixed[i * rows + free : (i + 1) * rows]
    copies[-1].wait()
    rows = packed.shape[1]
    for begin in range(0, partial[0].shape[1], 512):
        cols = slice(begin, begin + 512)
        part = out_weight[:, :, cols]
        added = dot(mixed[...], part.reshape(-1, 512)).astype(BF)
        for i in range(tp):
            partial[i][:, cols] = added[i * rows : (i + 1) * rows]


def write_out(tp, mixed, weight, partial):
    rows, width = partial[0].shape
    span = width // tp
    for t in range(tp):
        added = dot(mixed[...], block(weight, t, slice(3 * span, 4 * span))).astype(BF)
        for i in range(tp):
            partial[i][:, t * span : (t + 1) * span] = added[i * rows : (i + 1) * rows]


def masked_row(last, i, one_entry, one_row):
    last = last.astype(F32)
    one_entry[i : i + 1] = last[:1]
    one_row[i : i + 1] = last[1:2] + last[2:3] + last[3:4]


def cross_kernel(tp, local, *refs):
    entries, text = refs[:tp], refs[tp : 2 * tp]
    bias, gathered = refs[2 * tp : 2 * tp + 2]
    partial = refs[2 * tp + 2 : 3 * tp + 2]
    pair, query_out, mix_out, probs_out, one_entry, one_row = refs[3 * tp + 2 : 3 * tp + 8]
    weight, held, held_text, queries, mixed, sems = refs[3 * tp + 8 :]
    rows, txt, span = entries[0].shape[0], text[0].shape[0], local * HDIM
    free = rows - PAD
    pairs = [(ref, held_text.at[i * txt : (i + 1) * txt]) for i, ref in enumerate(text)]
    pairs += [(ref, held.at[i * rows : (i + 1) * rows]) for i, ref in enumerate(entries)]
    pairs += [(gathered, weight)]
    for copy in start_copies(pairs, sems):
        copy.wait()
    for k in range(2):
        cols = slice(k * span, (k + 1) * span)
        found = project(held_text[...], weight, cols).astype(BF)
        for i in range(tp):
            pair[i, :, cols] = found[i * txt : (i + 1) * txt]
    queries[...] = project(held[...], weight, slice(2 * span, 3 * span)).astype(BF)
    probs_out[...] = jnp.zeros_like(probs_out)
    for i in range(tp):
        masked_row(held[i * rows + free : (i + 1) * rows], i, one_entry, one_row)
        query_out[i] = queries[i * rows + free : (i + 1) * rows]
        for h in range(local):
            cols = slice(h * HDIM, (h + 1) * HDIM)
            keys = pair[i, :, cols]
            values = pair[i, :, span + h * HDIM : span + (h + 1) * HDIM]
            some = queries[i * rows : (i + 1) * rows, cols]
            probs, _ = softmax_head(some, keys, bias[i : i + 1], txt, 0)
            probs_out[i, h : h + 1] = probs[free : free + 1]
            mixed[i * rows : (i + 1) * rows, cols] = dot(probs.astype(BF), values).astype(BF)
        mix_out[i] = mixed[i * rows + free : (i + 1) * rows]
    write_out(tp, mixed, weight, partial)


def gelu_parts(value):
    slope = 0.7978845608
    bent = jnp.tanh(slope * (value + 0.044715 * value * value * value))
    half = 0.5 * (1.0 + bent)
    steep = slope * (1.0 + 3.0 * 0.044715 * value * value)
    return value * half, half + 0.5 * value * (1.0 - bent * bent) * steep


def up_kernel(tp, *refs):
    entries, (weight, active, held, sems) = refs[:tp], refs[tp:]
    rows = entries[0].shape[0]

    @pl.when(pl.program_id(0) == 0)
    def _():
        pairs = [(ref, held.at[i * rows : (i + 1) * rows]) for i, ref in enumerate(entries)]
        for copy in start_copies(pairs, sems):
            copy.wait()

    active[...] = gelu_parts(project(held[...], weight, slice(None)))[0].astype(BF)


def mlp_back_kernel(tp, *refs):
    entries_all, grad_active, gathered = refs[:tp], refs[tp], refs[tp + 1]
    active, grad_pre, grad_entry, one_entry, one_row, weight, last, entries, sem = refs[tp + 2 :]
    step, free = entries.shape[1] // tp, entries_all[0].shape[0] - PAD
    ends = [
        pltpu.make_async_copy(ref.at[free:], last.at[i], sem.at[tp + i])
        for i, ref in enumerate(entries_all)
    ]
    for copy in ends:
        copy.start()
    copies = [
        pltpu.make_async_copy(gathered.at[:, t], weight.at[:, t], sem.at[t]) for t in range(tp)
    ]
    for copy in copies:
        copy.start()
    for i, copy in enumerate(ends):
        copy.wait()
        masked_row(last[i], i, one_entry, one_row)
    entries[...] = jnp.zeros_like(entries)
    entries[:tp] = one_entry[...]
    hidden = jnp.zeros(active.shape, F32)
    for t, copy in enumerate(copies):
        copy.wait()
        rows = entries[:, t * step : (t + 1) * step].astype(BF)
        hidden = hidden + dot(rows, block(weight, t, slice(None)))
    value, steep = gelu_parts(hidden)
    active[...] = value.astype(BF)
    grad_pre[...] = (steep * grad_active[...]).astype(BF)
    for t in range(tp):
        back = dot_t(grad_pre[...], block(weight, t, slice(None)))
        grad_entry[:, t * step : (t + 1) * step] = back[:tp]


def summed(parts, i):
    total = parts[0][i : i + 1]
    for j in range(1, len(parts)):
        total = total + parts[j][i ^ j : (i ^ j) + 1]
    return total


def out_back(rows, weights, columns):
    tp = weights.shape[1]
    step = rows.shape[1] // tp
    total = dot_t(rows[:, :step], block(weights, 0, columns))
    for t in range(1, tp):
        total = total + dot_t(rows[:, t * step : (t + 1) * step], block(weights, t, columns))
    return total.astype(BF).astype(F32)


def head_mask(span):
    heads = lax.broadcasted_iota(jnp.int32, (8, span), 0)
    return lax.broadcasted_iota(jnp.int32, (8, span), 1) // HDIM == heads


def row_back(parts, rows, gain, base, i, out, gain_row):
    grad = summed(parts, i)
    field, scale = normed(rows[i : i + 1])
    out[i : i + 1] = base[i : i + 1] + norm_back(grad * gain[...], field, scale)
    if i == 0:
        gain_row[...] = grad * field


def cross_back_kernel(
    tp, base, rows, gain, pair, probs, gathered, *refs,
):
    parts = refs[:tp]
    grad_mid, grad_cmix, scores, grad_cq, grad_entry, gain_row = refs[tp : tp + 6]
    weight, held, sems = refs[tp + 6 :]
    span = weight.shape[3] // 2
    copies = [
        pltpu.make_async_copy(gathered.at[:, :, :, 2 * span :], weight, sems.at[0]),
    ]
    for copy in copies:
        copy.start()
    held[...] = jnp.zeros_like(held)
    for i in range(tp):
        row_back(parts, rows, gain, base, i, held, gain_row)
    grad_mid[...] = held[:tp]
    copies[0].wait()
    mixed = out_back(held[...].astype(BF), weight, slice(span, 2 * span))
    grad_cmix[...] = mixed[:tp]
    mask = head_mask(span)
    held[...] = jnp.zeros_like(held)
    for i in range(tp):
        spread = jnp.where(mask, mixed[i : i + 1], 0.0).astype(BF)
        grad_probs = dot_t(spread, pair[i, :, span:])
        weighs = probs[i]
        grad = weighs * (grad_probs - jnp.sum(grad_probs * weighs, axis=-1, keepdims=True))
        grad = grad.astype(BF)
        scores[i] = grad.astype(F32)
        back = jnp.where(mask, dot(grad, pair[i, :, :span]), 0.0)
        held[i : i + 1, :span] = jnp.sum(back, axis=0, keepdims=True) * HDIM ** (-0.5)
    grad_cq[...] = held[:tp, :span]
    queries = held[:, :span].astype(BF)
    step = grad_entry.shape[1] // tp
    for t in range(tp):
        back = dot_t(queries, block(weight, t, slice(0, span)))
        grad_entry[:, t * step : (t + 1) * step] = back[:tp]


def spread_heads(rows, i, spreads, mask):
    spreads[8 * i : 8 * i + 8] = jnp.where(mask, rows, 0.0)


def text_back_kernel(tp, local, *refs):
    scores, probs, query_one, grad_cmix, kvq = refs[:5]
    cross_one_row, mlp_one, grad_pre, grad_cq, mixed, cross, active, grad_mid = refs[5:13]
    text = refs[13 : 13 + tp]
    sent = refs[13 + tp : 13 + 2 * tp]
    lefts, factors, weight, held, keys, values, sems = refs[13 + 2 * tp :]
    span, width, txt = grad_cmix.shape[1], lefts.shape[1], scores.shape[2]
    copy = pltpu.make_async_copy(kvq.at[:, :, :, : 2 * span], weight, sems.at[0])
    copy.start()
    mask = head_mask(span)
    ff = grad_pre.shape[1]
    places, at = [], 0
    for size in (ff, span, span, span, span, span, ff, width):
        places.append(slice(at, at + size))
        at += size
    for i in range(tp):
        spread_heads(query_one[i].astype(F32)[:1], i, keys, mask)
        spread_heads(grad_cmix[i : i + 1], i, values, mask)
        both = jnp.concatenate([scores[i], probs[i]], axis=0).astype(BF)
        found = dot(both, text[i][...])
        for kind in range(2):
            begin = (2 * i + kind) * local
            lefts[begin : begin + local] = found[8 * kind : 8 * kind + local]
        sent[i][:, width:] = both
        for k, rows in ((2, query_one), (4, mixed), (5, cross)):
            held[i : i + 1, places[k]] = rows[i].astype(F32)[:1]
    held[:tp, places[0]] = grad_pre[...].astype(F32)[:tp]
    held[:tp, places[1]] = grad_cq[...]
    held[:tp, places[3]] = grad_cmix[...]
    held[:tp, places[6]] = active[...].astype(F32)[:tp]
    held[:tp, places[7]] = grad_mid[...]
    factors[...] = held[:tp].astype(BF)
    begin = 2 * tp * local
    lefts[begin : begin + tp] = cross_one_row[...]
    lefts[begin + tp :] = mlp_one[...]
    copy.wait()
    step = width // tp
    key_spread, value_spread = keys[...].astype(BF), values[...].astype(BF)
    for t in range(tp):
        cols = slice(t * step, (t + 1) * step)
        key_rows = dot_t(key_spread, block(weight, t, slice(0, span))) * HDIM ** (-0.5)
        value_rows = dot_t(value_spread, block(weight, t, slice(span, 2 * span)))
        for i in range(tp):
            eight = slice(8 * i, 8 * i + 8)
            both = jnp.concatenate([key_rows[eight], value_rows[eight]], axis=0)
            sent[i][:, cols] = both.astype(BF)


def self_back_kernel(
    tp, local, base, rows, gain, packed, probs, masked_entries, text_lefts, text_factors,
    gain_a, embed, gain_m_row, gathered, out_w, *refs,
):
    parts, entries, text_sent = refs[:tp], refs[tp : 2 * tp], refs[2 * tp : 3 * tp]
    sent, refs = refs[3 * tp : 4 * tp], refs[4 * tp :]
    payload, factors, weight, out_weight, held, spreads, lefts, small, sems = refs
    width = lefts.shape[1]
    span, free = weight.shape[3] // 3, entries[0].shape[0]
    copies = start_copies([(out_w, out_weight), (gathered, weight)], sems)
    ff = (text_factors.shape[1] - 5 * span - width) // 2
    cut = ff + 3 * span
    factors[:, :cut] = text_factors[:, :cut]
    factors[:, cut + 3 * span : -width] = text_factors[:, cut:]
    small[...] = jnp.zeros_like(small)
    small[3:4] = gain_m_row[...]
    held[...] = jnp.zeros_like(held)
    for i in range(tp):
        row_back(parts, rows, gain, base, i, held, small.at[2:3])
    small[0:1] = held[0:1]
    factors[:, -width:] = held[:tp].astype(BF)
    copies[0].wait()
    part = out_weight[...]
    mixed = dot_t(held[...].astype(BF), part.reshape(span, width)).astype(BF).astype(F32)
    factors[:, cut : cut + span] = mixed[:tp].astype(BF)
    mask = head_mask(span)
    held[...] = jnp.zeros_like(held)
    masked_row = masked_entries[:1].astype(F32)
    ones = []
    for i in range(tp):
        spread = jnp.where(mask, mixed[i : i + 1], 0.0)
        spreads[8 * i : 8 * i + 8] = spread
        spread = spread.astype(BF)
        values = packed[i, :, 2 * span :]
        grad_probs, grad_one = dot_t(spread, values[:free]), dot_t(spread, values[free:])[:, :1]
        weighs, one = probs[i, :, :free], probs[i, :, free : free + 1]
        mean = jnp.sum(grad_probs * weighs, axis=-1, keepdims=True) + grad_one * one
        grad = (weighs * (grad_probs - mean)).astype(BF)
        grad_one = (one * (grad_one - mean)).astype(BF).astype(F32)
        ones.append((grad_one, one))
        keys = packed[i, :, span : 2 * span]
        back = dot(grad, keys[:free]) + grad_one * keys[free : free + 1].astype(F32)
        back = jnp.sum(jnp.where(mask, back, 0.0), axis=0, keepdims=True)
        held[i : i + 1, :span] = back * HDIM ** (-0.5)
        both = jnp.concatenate([grad.astype(F32), weighs], axis=0).astype(BF)
        both_one = jnp.concatenate([grad_one, one], axis=0).astype(BF).astype(F32)
        found = dot(both, entries[i][...]) + both_one * masked_row
        for kind in range(2):
            begin = (2 * i + kind) * local
            lefts[begin : begin + local] = found[8 * kind : 8 * kind + local]
        sent[i][:PAD, width:] = both
        sent[i][PAD:] = text_sent[i][...]
    factors[:, cut + span : cut + 2 * span] = held[:tp, :span].astype(BF)
    queries = held[:, :span].astype(BF)
    zero_query = packed[0, free:, :span].astype(F32)[:1]
    factors[:, cut + 2 * span : cut + 3 * span] = jnp.broadcast_to(zero_query, (tp, span)).astype(BF)
    key_spread = jnp.where(mask, zero_query, 0.0).astype(BF)
    value_spread = spreads[...].astype(BF)
    step = width // tp
    field, scale = normed(embed[...])
    copies[1].wait()
    for t in range(tp):
        cols = slice(t * step, (t + 1) * step)
        keys = dot_t(key_spread, block(weight, t, slice(span, 2 * span))) * HDIM ** (-0.5)
        values = dot_t(value_spread, block(weight, t, slice(2 * span, 3 * span)))
        query_rows = dot_t(queries, block(weight, t, slice(0, span)))
        masked_grad, gain_grad = 0.0, 0.0
        for i in range(tp):
            mine = values[8 * i : 8 * i + 8]
            sent[i][:PAD, cols] = jnp.concatenate([keys, mine], axis=0).astype(BF)
            last = query_rows[i : i + 1]
            found = ones[i][0] * keys + ones[i][1] * mine
            masked_grad = masked_grad + last + jnp.sum(found, axis=0, keepdims=True)
            for kind, rows_back in enumerate((keys, mine)):
                begin = (2 * i + kind) * local
                found = lefts[begin : begin + local, cols] * rows_back[:local]
                gain_grad = gain_grad + jnp.sum(found, axis=0, keepdims=True)
        gain_grad = gain_grad / gain_a[:, cols]
        rows_sum = jnp.sum(query_rows[:tp], axis=0, keepdims=True)
        small[1:2, cols] = gain_grad + rows_sum * field[:, cols]
        held[0:1, cols] = masked_grad
    small[0:1] = small[0:1] + norm_back(held[0:1] * gain_a[...], field, scale)
    begin = 2 * tp * local
    lefts[begin : begin + text_lefts.shape[0]] = text_lefts[...]
    begin += text_lefts.shape[0]
    high = small[:4].astype(BF).astype(F32)
    lefts[begin : begin + 4] = high
    lefts[begin + 4 : begin + 8] = small[:4] - high
    half, own = lefts.shape[0] // 2, payload.shape[2] // 2
    for d in range(payload.shape[0]):
        cols = slice(d * own, (d + 1) * own)
        both = jnp.concatenate([lefts[:half, cols], lefts[half:, cols]], axis=1)
        payload[d] = both.astype(BF)


def tokens_back_kernel(tp, rows, gain, place, *refs):
    came, (tokens, text) = refs[:tp], refs[tp:]
    width, free = rows.shape[1], place.shape[1]
    grad, grad_text = 0.0, 0.0
    for part in came:
        grad = grad + dot_sum(part[:PAD, width:], part[:PAD, :width])
        grad_text = grad_text + dot_sum(part[PAD:, width:], part[PAD:, :width])
    text[...] = grad_text.astype(BF)
    field, scale = normed(rows[:free])
    start = norm_back(grad * gain[...], field, scale)
    tokens[...] = dot(place[...], start.astype(BF)).astype(BF)


def stack_kernel(*refs):
    for k, ref in enumerate(refs[:-1]):
        refs[-1][k] = ref[...]


def unpack_kernel(planes, others, right, group, held):
    count, tp = planes.shape[:2]
    for k in range(count):
        held[k * tp : (k + 1) * tp] = planes[k].astype(F32)
        held[(count + k) * tp : (count + k + 1) * tp] = others[k].astype(F32)
    right[...] = held[:, : right.shape[1]].astype(BF)
    group[...] = held[:, right.shape[1] :].astype(BF)


def aligned(right, corner, tp):
    count = right.shape[0]
    out = lax.broadcasted_iota(jnp.int32, (count, count), 0)
    into = lax.broadcasted_iota(jnp.int32, (count, count), 1)
    same = (out // tp == (corner ^ (into // tp))) & (out % tp == into % tp)
    return dot(same.astype(BF), right).astype(BF)


def columns_kernel(local, place, attn_left, text_left, one_left, entry, *refs):
    right, (grad_qkv, grad_kv, grad_cq, grad_up) = refs[:-4], refs[-4:]
    tp, span = len(right), local * HDIM
    ff = right[0].shape[1] - 6 * span
    ones = jnp.ones((right[0].shape[0], HDIM), BF)
    scale = HDIM ** (-0.5)

    def at_columns(begin, size):
        return pl.ds(pl.multiple_of(begin, HDIM), size)

    for j in range(tp):
        at = place[0] ^ j
        rows = aligned(right[j][...], place[1], tp)
        part = [rows[:, ff + k * span : ff + (k + 1) * span] for k in range(6)]
        grad_up[:, at_columns(at * ff, ff)] = dot_sum(one_left[at, 1], rows[:, :ff])
        grad_cq[:, at_columns(at * span, span)] = dot_sum(one_left[at, 0], part[0])
        total = jnp.sum(part[4].astype(F32), axis=0, keepdims=True)
        grad_qkv[:, at_columns(at * span, span)] = entry[...] * total
        queries = part[5].astype(F32)[:1] * scale
        for h in range(local):
            cols = slice(h * HDIM, (h + 1) * HDIM)
            begin = at * span + h * HDIM
            outer = dot_sum(text_left[at, 0, h], part[1][:, cols])
            grad_kv[:, at_columns(begin, HDIM)] = outer * scale
            outer = dot_sum(text_left[at, 1, h], part[2][:, cols])
            grad_kv[:, at_columns(tp * span + begin, HDIM)] = outer
            outer = dot_sum(attn_left[at, 0, h], ones) * queries[:, cols]
            grad_qkv[:, at_columns(tp * span + begin, HDIM)] = outer
            outer = dot_sum(attn_left[at, 1, h], part[3][:, cols])
            grad_qkv[:, at_columns(2 * tp * span + begin, HDIM)] = outer


def whole_spec():
    return pl.BlockSpec(memory_space=pl.ANY)


def in_vmem(kernel, name, operands, out_shape, scratch_shapes=(), held=()):
    spaces = dict(held)
    return pl.pallas_call(
        kernel,
        in_specs=[
            pl.BlockSpec(memory_space=spaces.get(k, pltpu.VMEM)) for k in range(len(operands))
        ],
        out_specs=[pl.BlockSpec(memory_space=pltpu.VMEM)] * len(out_shape),
        out_shape=[jax.ShapeDtypeStruct(shape, dtype) for shape, dtype in out_shape],
        scratch_shapes=scratch_shapes,
        compiler_params=pltpu.CompilerParams(vmem_limit_bytes=VMEM_BYTES),
        cost_estimate=COST,
        name=name,
    )(*operands)


def self_forward(local, count, entries, masked_entries, gathered, out_w):
    tp, (free, width) = len(entries), entries[0].shape
    span, rows = local * HDIM, free + PAD
    found = in_vmem(
        functools.partial(self_kernel, tp, local, count),
        "self_attention",
        [*entries, masked_entries, gathered, out_w],
        [((rows, width), BF)] * tp
        + [((tp, rows, 3 * span), BF), ((tp, PAD, span), BF), ((tp, 8, free + TILE), F32)],
        [
            pltpu.VMEM(gathered.shape, BF),
            pltpu.VMEM(out_w.shape, BF),
            pltpu.VMEM((tp * free + PAD, width), BF),
            pltpu.VMEM((tp * rows, span), BF),
            pltpu.SemaphoreType.DMA((tp + 3,)),
        ],
        [(k, pl.ANY) for k in range(tp + 3)],
    )
    return found[:tp], *found[tp:]


def cross_forward(local, entries, text, bias, gathered):
    tp, (rows, width) = len(entries), entries[0].shape
    txt, span = text[0].shape[0], local * HDIM
    found = in_vmem(
        functools.partial(cross_kernel, tp, local),
        "cross_attention",
        [*entries, *text, bias, gathered],
        [((rows, width), BF)] * tp
        + [
            ((tp, txt, 2 * span), BF),
            ((tp, PAD, span), BF),
            ((tp, PAD, span), BF),
            ((tp, 8, txt), F32),
            ((tp, width), F32),
            ((tp, width), F32),
        ],
        [
            pltpu.VMEM(gathered.shape, BF),
            pltpu.VMEM((tp * rows, width), BF),
            pltpu.VMEM((tp * txt, width), BF),
            pltpu.VMEM((tp * rows, span), BF),
            pltpu.VMEM((tp * rows, span), BF),
            pltpu.SemaphoreType.DMA((2 * tp + 1,)),
        ],
        [(k, pl.ANY) for k in range(2 * tp + 2) if k != 2 * tp],
    )
    return found[:tp], *found[tp:]


def down_kernel(tp, active, gathered, *refs):
    partial, (weight, sems) = refs[:tp], refs[tp:]
    rows, width = partial[0].shape
    step = min(512, width)
    parts = [slice(at, at + step) for at in range(0, width, step)]
    copies = start_copies([(gathered.at[:, :, cols], weight.at[:, :, cols]) for cols in parts], sems)
    for cols, copy in zip(parts, copies):
        copy.wait()
        part = weight[:, :, cols]
        added = dot(active[...], part.reshape(-1, step)).astype(BF)
        for i in range(tp):
            partial[i][:, cols] = added[i * rows : (i + 1) * rows]


def mlp_down(tp, active, gathered):
    rows, width = active.shape[0] // tp, gathered.shape[2]
    return in_vmem(
        functools.partial(down_kernel, tp),
        "mlp_down",
        [active, gathered],
        [((rows, width), BF)] * tp,
        [pltpu.VMEM(gathered.shape, BF), pltpu.SemaphoreType.DMA((width // min(512, width),))],
        ((1, pl.ANY),),
    )


def mlp_up(entries, gathered):
    tp, (rows, width) = len(entries), entries[0].shape
    blocks, _, own, ff = gathered.shape
    step = min(ff, 512)
    return pl.pallas_call(
        functools.partial(up_kernel, tp),
        grid=(ff // step,),
        in_specs=[whole_spec()] * tp
        + [pl.BlockSpec((blocks, tp, own, step), lambda i: (0, 0, 0, i))],
        out_specs=pl.BlockSpec((tp * rows, step), lambda i: (0, i)),
        out_shape=jax.ShapeDtypeStruct((tp * rows, ff), BF),
        scratch_shapes=[
            pltpu.VMEM((tp * rows, width), BF),
            pltpu.SemaphoreType.DMA((tp,)),
        ],
        compiler_params=pltpu.CompilerParams(vmem_limit_bytes=VMEM_BYTES),
        cost_estimate=COST,
        name="mlp_up",
    )(*entries, gathered)


def mlp_back(entries, grad_active, gathered):
    tp, width = len(entries), entries[0].shape[1]
    ff = gathered.shape[3]
    return in_vmem(
        functools.partial(mlp_back_kernel, tp),
        "mlp_back",
        [*entries, grad_active, gathered],
        [
            ((PAD, ff), BF),
            ((PAD, ff), BF),
            ((tp, width), F32),
            ((tp, width), F32),
            ((tp, width), F32),
        ],
        [
            pltpu.VMEM(gathered.shape, BF),
            pltpu.VMEM((tp, PAD, width), BF),
            pltpu.VMEM((PAD, width), F32),
            pltpu.SemaphoreType.DMA((2 * tp,)),
        ],
        [(k, pl.ANY) for k in range(tp + 2) if k != tp],
    )


def cross_back(base, rows, gain, pair, probs, gathered, parts):
    tp, width = base.shape
    blocks, _, own, columns = gathered.shape
    span = columns // 4
    return in_vmem(
        functools.partial(cross_back_kernel, tp),
        "cross_back",
        [base, rows, gain[None], pair, probs, gathered, *parts],
        [
            ((tp, width), F32),
            ((tp, span), F32),
            (probs.shape, F32),
            ((tp, span), F32),
            ((tp, width), F32),
            ((1, width), F32),
        ],
        [
            pltpu.VMEM((blocks, tp, own, 2 * span), BF),
            pltpu.VMEM((8, width), F32),
            pltpu.SemaphoreType.DMA((1,)),
        ],
        ((5, pl.ANY),),
    )


def text_back(local, scores, probs, query_one, grad_cmix, kvq, rest, text):
    tp, span = grad_cmix.shape
    blocks, _, own, _ = kvq.shape
    (txt, width), ff = text[0].shape, rest[2].shape[1]
    found = in_vmem(
        functools.partial(text_back_kernel, tp, local),
        "text_back",
        [scores, probs, query_one, grad_cmix, kvq, *rest, *text],
        [((PAD, width + txt), BF)] * tp
        + [((2 * tp * (local + 1), width), F32), ((tp, 2 * ff + 5 * span + width), BF)],
        [
            pltpu.VMEM((blocks, tp, own, 2 * span), BF),
            pltpu.VMEM((8, 2 * ff + 5 * span + width), F32),
            pltpu.VMEM((8 * tp, span), F32),
            pltpu.VMEM((8 * tp, span), F32),
            pltpu.SemaphoreType.DMA((1,)),
        ],
        ((4, pl.ANY),),
    )
    return found[:tp], *found[tp:]


def self_back(local, world, small_operands, gathered, out_w, parts, entries, text_sent):
    tp, width = small_operands[0].shape
    text_lefts, text_factors = small_operands[6], small_operands[7]
    _, _, own, columns = gathered.shape
    span, free = columns // 3, entries[0].shape[0]
    count = 2 * tp * local + text_lefts.shape[0] + 8
    operands = [*small_operands, gathered, out_w, *parts, *entries, *text_sent]
    found = in_vmem(
        functools.partial(self_back_kernel, tp, local),
        "self_back",
        operands,
        [((2 * PAD, width + free), BF)] * tp
        + [((world, count // 2, 2 * own), BF), ((tp, text_factors.shape[1] + 3 * span + width), BF)],
        [
            pltpu.VMEM(gathered.shape, BF),
            pltpu.VMEM(out_w.shape, BF),
            pltpu.VMEM((8, width), F32),
            pltpu.VMEM((8 * tp, span), F32),
            pltpu.VMEM((count, width), F32),
            pltpu.VMEM((8, width), F32),
            pltpu.SemaphoreType.DMA((2,)),
        ],
        [(len(small_operands) + k, pl.ANY) for k in range(2)],
    )
    return found[:tp], *found[tp:]


def stacked(pieces):
    shape = (len(pieces),) + pieces[0].shape
    return in_vmem(stack_kernel, "stack", pieces, [(shape, BF)])[0]


def unpack(planes, others, cut):
    count, tp, wide = planes.shape
    rows = 2 * count * tp
    return in_vmem(
        unpack_kernel,
        "unpack",
        [planes, others],
        [((rows, cut), BF), ((rows, wide - cut), BF)],
        [pltpu.VMEM((rows, wide), F32)],
    )


def join_kernel(free, base, gain, *refs):
    parts, (total, entries) = refs[:-2], refs[-2:]
    value = base[...]
    for part in parts:
        value = value + part[...].astype(F32)
    total[...] = value
    found = normed(value)[0] * gain[...]
    entries[...] = found.astype(BF)

    @pl.when(pl.program_id(0) == pl.num_programs(0) - 1)
    def _():
        at = value.shape[0] - PAD
        row = value[at : at + 1]
        spot = lax.broadcasted_iota(jnp.int32, (PAD, value.shape[1]), 0)
        last = found[at:]
        for k in range(3):
            part = row.astype(BF).astype(F32)
            last = jnp.where(spot == k + 1, part, last)
            row = row - part
        entries[at:] = last.astype(BF)


def join(base, parts, gain):
    rows, width = base.shape
    step = PAD * 3 if rows % (PAD * 3) == 0 else PAD
    block = pl.BlockSpec((step, width), lambda i: (i, 0))
    return pl.pallas_call(
        functools.partial(join_kernel, rows - PAD),
        grid=(rows // step,),
        in_specs=[block, pl.BlockSpec((1, width), lambda i: (0, 0))] + [block] * len(parts),
        out_specs=[block, block],
        out_shape=[
            jax.ShapeDtypeStruct((rows, width), F32),
            jax.ShapeDtypeStruct((rows, width), BF),
        ],
        compiler_params=pltpu.CompilerParams(vmem_limit_bytes=VMEM_BYTES),
        cost_estimate=COST,
        name="join",
    )(base, gain[None], *parts)


def shards(
    tp,
    planes,
    tokens,
    text,
    cotangent,
    positions,
    text_lengths,
    mask_embed,
    gain_attn,
    w_qkv,
    w_attn_out,
    gain_cross,
    w_cross_q,
    w_cross_kv,
    w_cross_out,
    gain_mlp,
    w_up,
    w_down,
):
    me = Layer(tp, planes)
    seq, width = tokens.shape
    masked_count = positions.shape[1]
    free = seq - masked_count
    txt = text.shape[1]
    local = HEADS // tp
    rows = free + PAD
    device = (me.t * 2 + me.c) * planes + me.z
    world = tp * 2 * planes
    own = width // world

    def after(value, earlier):
        return lax.optimization_barrier((value, earlier))[0]

    span = local * HDIM

    out_w = me.gather_blocks(w_attn_out)
    corner = me.c * planes + me.z
    place_at = jnp.stack([me.t, corner]).astype(jnp.int32)
    in_smem = ((0, pltpu.SMEM),)
    parts = in_vmem(
        functools.partial(parts_kernel, tp, 3),
        "parts",
        [place_at, w_qkv],
        [((own, 3 * span), BF)] * tp,
        held=in_smem,
    )
    attn_sent = in_vmem(
        functools.partial(assemble_kernel, tp),
        "assemble",
        [place_at, *me.to_owner(parts)],
        [((tp, own, 3 * span), BF)],
        held=in_smem,
    )[0]

    cot_sum = jnp.sum(cotangent[0].astype(F32), axis=0)
    vectors = jnp.concatenate([mask_embed, gain_attn, gain_cross, gain_mlp]).astype(F32)
    fill = TILE - vectors.shape[0] % TILE
    length = jnp.broadcast_to(text_lengths.astype(F32), (fill,))
    gathered = after(jnp.concatenate([cot_sum, vectors, length]), attn_sent)
    by_plane = me.gather_cz(gathered)
    gathered = me.tp_direct(by_plane)
    others = after((w_cross_kv, w_cross_q, w_cross_out), (gathered, attn_sent))
    kvq_sent = me.shuffle([(others[0], 2), (others[1], 1)])
    cross_sent = jnp.concatenate([kvq_sent, column_blocks(tp, [(others[2], 1)])], axis=2)
    attn_w = me.gather_blocks(after(attn_sent, (out_w, by_plane)))
    vectors = gathered[:, :, width : width + 4 * own].reshape(world, 4, own)
    vectors = xor_order(vectors, device, world).transpose(1, 0, 2).reshape(4, width)
    embed, gain_a, gain_c, gain_m = vectors[0], vectors[1], vectors[2], vectors[3]
    lengths = gathered[:, 0, width + 4 * own :][:, :1]
    text_bias = jnp.where(
        lax.broadcasted_iota(jnp.int32, (tp, txt), 1).astype(F32) < lengths, 0.0, -1e30
    )
    cot_group = gathered[:, 0, :width]

    spots = lax.broadcasted_iota(jnp.int32, (masked_count, seq), 1)
    masked = jnp.sum((positions[0][:, None] == spots).astype(F32), axis=0)
    below = lax.broadcasted_iota(jnp.int32, (seq, seq), 0) <= lax.broadcasted_iota(
        jnp.int32, (seq, seq), 1
    )
    rank = dot((1.0 - masked).astype(BF)[None, :], below.astype(BF))[0]
    ranks = lax.broadcasted_iota(jnp.int32, (free, seq), 0).astype(F32) + 1.0
    pick = ((rank[None, :] == ranks) & (masked[None, :] == 0.0)).astype(BF)
    place = jnp.concatenate(
        [pick.T, masked[:, None].astype(BF), jnp.zeros((seq, PAD - 1), BF)], axis=1
    )
    start_free = dot(pick, tokens)
    start = jnp.concatenate([start_free, jnp.broadcast_to(embed[None], (PAD, width))])

    cot_rows = gathered[:, :, :width].reshape(world, width)
    high = cot_rows.astype(BF)
    low = (cot_rows - high.astype(F32)).astype(BF)
    through = dot_t(jnp.concatenate([high, low]), w_down)
    through = through[:world] + through[world:]
    through = through.reshape(tp, 2 * planes, -1).transpose(1, 0, 2)
    through = xor_order(through, me.c * planes + me.z, 2 * planes)
    through = lax.all_to_all(after(through, kvq_sent), ("core", "fsdp"), 0, 0, tiled=True)
    grad_active = through.transpose(1, 0, 2).reshape(tp, -1)

    field_a, scale_a = normed(start)
    entries = (field_a * gain_a[None]).astype(BF)
    masked_entries = entries[free:]
    entries_all = me.spread(entries[:free])
    text_rows = me.spread(after(text[0], entries_all))
    up_sent = me.shuffle([(after(w_up, (entries_all, kvq_sent)), 1)])
    cross_w = me.gather_blocks(after(cross_sent, (attn_w, entries_all, up_sent, place, masked_entries, text_bias)))
    partial, packed, mixed_one, probs_one = self_forward(
        local, masked_count, entries_all, masked_entries, attn_w, out_w
    )
    after_attn, cross_entries = join(after(start, (grad_active, place)), me.collect(after(tuple(partial), text_rows)), gain_c)

    cross_all = me.spread(cross_entries)
    up = me.gather_blocks(after(up_sent, (cross_w, cross_all)))
    partial, pair, query_one, cross_one, cross_probs_one, cross_entry, attn_stream = cross_forward(
        local, cross_all, text_rows, text_bias, cross_w
    )
    after_cross, mlp_entries = join(after_attn, me.collect(partial), gain_m)

    mlp_all = me.spread(mlp_entries)
    most = width * 3 // 4
    down = me.gather_blocks(after(w_down[:, :most], (up, mlp_all)))

    active_one, grad_pre, grad_entry, mlp_one, cross_stream = mlp_back(
        mlp_all, jnp.pad(grad_active, ((0, PAD - tp), (0, 0))), up
    )
    grad_mid, grad_cmix, scores, grad_cq, grad_entry, grad_gain_m = cross_back(
        cot_group, cross_stream, gain_m, pair, cross_probs_one, cross_w, me.tp_parts(grad_entry)
    )
    text_sent, text_lefts, text_factors = text_back(
        local,
        scores,
        cross_probs_one,
        query_one,
        grad_cmix,
        cross_w,
        [
            cross_entry,
            mlp_one,
            grad_pre,
            grad_cq,
            mixed_one,
            cross_one,
            active_one,
            grad_mid,
        ],
        text_rows,
    )
    sent, payload, factors = self_back(
        local,
        world,
        [
            grad_mid,
            attn_stream,
            gain_c[None],
            packed,
            probs_one,
            masked_entries,
            text_lefts,
            text_factors,
            gain_a[None],
            embed[None],
            grad_gain_m,
        ],
        attn_w,
        out_w,
        me.tp_parts(grad_entry),
        entries_all,
        text_sent,
    )
    came = me.to_owner(sent)

    ff = grad_pre.shape[1]
    active = mlp_up(after(tuple(mlp_all), payload), up)
    pieces = [factors] + [me.other_plane(factors, k) for k in range(1, planes)]
    planes_of = stacked(after(tuple(pieces), (active, came)))
    lefts = me.to_rows(after(payload, planes_of))
    right, group = unpack(planes_of, me.other_core(planes_of), ff + 6 * span)
    right = [right] + [me.hop(right, j) for j in range(1, tp)]

    active, _ = lax.optimization_barrier((active, right[0]))
    down_rest = me.gather_blocks(after(w_down[:, most:], (down, active)))
    partial = mlp_down(tp, active, down)
    collected = me.collect(partial)
    active = after(active, tuple(partial))

    grad_tokens, grad_text = in_vmem(
        functools.partial(tokens_back_kernel, tp),
        "tokens_back",
        [start, gain_a[None], pick.T, *after(tuple(came), partial)],
        [((seq, width), BF), ((txt, width), BF)],
    )

    partial = mlp_down(tp, after(active, grad_tokens), down_rest)
    collected_rest = me.collect(partial)

    heads = 2 * tp * local
    lefts = after(lefts, partial)
    lefts = jnp.concatenate([lefts[:, :, :own], lefts[:, :, own:]], axis=1)
    attn_left, text_left = (
        lefts[:, k * heads : (k + 1) * heads]
        .reshape(tp, 2 * planes, tp, 2, local, own)
        .transpose(0, 3, 4, 1, 2, 5)
        .reshape(tp, 2, local, world, own)
        for k in range(2)
    )
    one_left = lefts[:, 2 * heads : 2 * heads + 2 * tp].reshape(tp, 2 * planes, 2, tp, own)
    one_left = one_left.transpose(0, 2, 1, 3, 4).reshape(tp, 2, world, own)
    small = jnp.sum(lefts[:, 2 * heads + 2 * tp :].astype(F32), axis=0)
    small = small[:4] + small[4:]
    entry_own = lax.dynamic_slice_in_dim(entries[free], device * own, own).astype(F32)
    grad_w_qkv, grad_w_kv, grad_w_cq, grad_w_up = in_vmem(
        functools.partial(columns_kernel, local),
        "columns",
        [place_at, attn_left, text_left, one_left, entry_own[:, None], *right],
        [((own, 3 * width), F32), ((own, 2 * width), F32), ((own, width), F32), ((own, tp * ff), F32)],
        held=in_smem,
    )

    def mine(stack):
        size = stack.shape[1] // (2 * planes)
        return lax.dynamic_slice_in_dim(stack, corner * size, size, axis=1)

    group = after(group, partial)
    cuts = [span, 2 * span, 2 * span + ff, 2 * span + ff + width]
    mixed_f, cross_f, active_f, mid_f, attn_f = jnp.split(group, cuts, axis=1)
    cot_f = gathered[:, :, :width].astype(BF).swapaxes(0, 1).reshape(world, width)
    grad_w_out = dot_sum(mine(mixed_f), attn_f)
    grad_w_cout = dot_sum(mine(cross_f), mid_f)
    grad_w_down = dot_sum(mine(active_f), cot_f)
    collected_rest = after(tuple(collected_rest), (grad_w_qkv, grad_w_out, grad_w_cout, grad_w_down, small))
    output = [sum(p.astype(F32) for p in parts) for parts in (collected, collected_rest)]
    output = after_cross + jnp.concatenate(output, axis=1)
    output = dot(place, output.astype(BF)).astype(BF)
    return (
        output,
        grad_tokens,
        grad_text[None],
        small[0],
        small[1],
        grad_w_qkv,
        grad_w_out,
        small[2],
        grad_w_cq,
        grad_w_kv,
        grad_w_cout,
        small[3],
        grad_w_up,
        grad_w_down,
    )


def solution(mesh):
    tp, planes = mesh.shape["dp"] // 2, mesh.shape["fsdp"]
    fine = Mesh(mesh.devices.reshape(tp, 2, planes), ("tp", "core", "fsdp"))
    every = ("tp", "core", "fsdp")
    one, two, three = P(every), P(every, None), P(every, None, None)

    def layer(*arguments):
        return shards(tp, planes, *arguments)

    return jax.shard_map(
        layer,
        mesh=fine,
        in_specs=(two, three, three, two, one, one, one, two, two, one, two, two, two, one, two, two),
        out_specs=(two, two, three, one, one, two, two, one, two, two, two, one, two, two),
        check_vma=False,
    )
```

```python
import functools

import jax
import jax.numpy as jnp
from jax import lax
from jax.experimental import pallas as pl
from jax.experimental.pallas import tpu as pltpu
from jax.sharding import Mesh, PartitionSpec as P

HEADS = 16
HDIM = 128
TILE = 128
PAD = 16
BF = jnp.bfloat16
F32 = jnp.float32
VMEM_BYTES = 60 << 20
COST = pl.CostEstimate(flops=1, bytes_accessed=1, transcendentals=0)


def dot(left, right):
    return jnp.dot(left, right, preferred_element_type=F32)


def dot_t(left, right):
    return lax.dot_general(left, right, (((1,), (1,)), ((), ())), preferred_element_type=F32)


def dot_sum(left, right):
    return lax.dot_general(left, right, (((0,), (0,)), ((), ())), preferred_element_type=F32)


def normed(rows):
    centered = rows - jnp.mean(rows, axis=-1, keepdims=True)
    scale = lax.rsqrt(jnp.mean(centered * centered, axis=-1, keepdims=True) + 1e-05)
    return centered * scale, scale


def norm_back(grad, field, scale):
    return scale * (
        grad
        - jnp.mean(grad, axis=-1, keepdims=True)
        - field * jnp.mean(grad * field, axis=-1, keepdims=True)
    )


def xor_order(stack, me, size):
    bit = 1
    while bit < size:
        split = stack.reshape((size // (2 * bit), 2, bit) + stack.shape[1:])
        turned = jnp.concatenate([split[:, 1:], split[:, :1]], axis=1)
        stack = jnp.where((me & bit) != 0, turned, split).reshape(stack.shape)
        bit *= 2
    return stack


def bits_of(size):
    return [1 << k for k in range(size.bit_length() - 1)]


class Layer:
    def __init__(self, tp, planes):
        self.tp, self.planes = tp, planes
        self.t, self.c, self.z = (lax.axis_index(a) for a in ("tp", "core", "fsdp"))


    def hop(self, value, j):
        return lax.ppermute(value, "tp", [(i, i ^ j) for i in range(self.tp)])

    def other_core(self, value):
        return lax.ppermute(value, "core", [(0, 1), (1, 0)])

    def other_plane(self, value, k):
        return lax.ppermute(value, "fsdp", [(i, i ^ k) for i in range(self.planes)])

    def spread(self, value):
        return [value] + [self.hop(value, j) for j in range(1, self.tp)]

    def collect(self, parts):
        return [parts[0]] + [self.hop(parts[j], j) for j in range(1, self.tp)]

    def tp_direct(self, value):
        return jnp.stack([value] + [self.hop(value, j) for j in range(1, self.tp)])

    def tp_parts(self, value):
        return [value] + [self.hop(value, j) for j in range(1, self.tp)]

    def to_owner(self, stack):
        return [stack[0]] + [self.hop(stack[j], j) for j in range(1, self.tp)]

    def to_rows(self, value):
        return lax.all_to_all(value, ("tp", "core", "fsdp"), 0, 0, tiled=True)

    def gather_cz(self, value):
        planes = jnp.stack([value] + [self.other_plane(value, k) for k in range(1, self.planes)])
        return jnp.concatenate([planes, self.other_core(planes)])


    def shuffle(self, shards):
        return lax.all_to_all(column_blocks(self.tp, shards), "tp", 0, 0, tiled=True)

    def gather_blocks(self, shard):
        return lax.all_gather(shard, ("core", "fsdp"), axis=0)


def blocks_kernel(moves, *refs):
    for source, begin, t, at, size in moves:
        refs[-1][t, :, at : at + size] = refs[source][:, begin : begin + size]


def column_blocks(tp, shards):
    moves, at = [], 0
    for source, (shard, kinds) in enumerate(shards):
        size = shard.shape[1] // (kinds * tp)
        for kind in range(kinds):
            moves += [(source, (kind * tp + t) * size, t, at, size) for t in range(tp)]
            at += size
    rows = shards[0][0].shape[0]
    return in_vmem(
        functools.partial(blocks_kernel, moves),
        "column_blocks",
        [shard for shard, _ in shards],
        [((tp, rows, at), BF)],
    )[0]


def parts_kernel(tp, kinds, place, shard, *parts):
    size = shard.shape[1] // (kinds * tp)
    for j in range(tp):
        for kind in range(kinds):
            begin = pl.multiple_of((kind * tp + (place[0] ^ j)) * size, HDIM)
            parts[j][:, kind * size : (kind + 1) * size] = shard[:, pl.ds(begin, size)]


def assemble_kernel(tp, place, *refs):
    parts, whole = refs[:tp], refs[tp]
    for j in range(tp):
        whole[place[0] ^ j] = parts[j][...]


def block(weights, t, columns):
    part = weights[:, t, :, columns]
    return part.reshape(part.shape[0] * part.shape[1], part.shape[2])


def project(rows, weights, columns):
    tp = weights.shape[1]
    step = rows.shape[1] // tp
    total = dot(rows[:, :step], block(weights, 0, columns))
    for t in range(1, tp):
        total = total + dot(rows[:, t * step : (t + 1) * step], block(weights, t, columns))
    return total


def start_copies(pairs, sems):
    copies = [pltpu.make_async_copy(a, b, sems.at[k]) for k, (a, b) in enumerate(pairs)]
    for copy in copies:
        copy.start()
    return copies


def softmax_head(queries, keys, bias, free, extra):
    scale = HDIM ** (-0.5)
    logits = dot_t(queries, keys[:free]) * scale
    if bias is not None:
        logits = logits + bias
    top = jnp.max(logits, axis=-1, keepdims=True)
    if not extra:
        weighs = jnp.exp(logits - top)
        return weighs / jnp.sum(weighs, axis=-1, keepdims=True), None
    one = dot_t(queries, keys[free:])[:, :1] * scale
    top = jnp.maximum(top, one)
    weighs, one = jnp.exp(logits - top), jnp.exp(one - top) * extra
    total = jnp.sum(weighs, axis=-1, keepdims=True) + one
    return weighs / total, one / total


def self_kernel(tp, local, count, *refs):
    entries, masked_entries, gathered, out_w = refs[:tp], refs[tp], refs[tp + 1], refs[tp + 2]
    partial = refs[tp + 3 : 2 * tp + 3]
    packed, mix_out, probs_out, weight, out_weight, held, mixed, sems = refs[2 * tp + 3 :]
    free, rows, span = entries[0].shape[0], packed.shape[1], local * HDIM
    pairs = [(ref, held.at[i * free : (i + 1) * free]) for i, ref in enumerate(entries)]
    pairs += [(masked_entries, held.at[tp * free :]), (gathered, weight), (out_w, out_weight)]
    copies = start_copies(pairs, sems)
    for copy in copies[:-1]:
        copy.wait()
    for k in range(3):
        cols = slice(k * span, (k + 1) * span)
        found = project(held[...], weight, cols).astype(BF)
        for i in range(tp):
            packed[i, :free, cols] = found[i * free : (i + 1) * free]
            packed[i, free:, cols] = found[tp * free :]
    probs_out[...] = jnp.zeros_like(probs_out)
    for i in range(tp):
        for h in range(local):
            cols = [slice(k * span + h * HDIM, k * span + (h + 1) * HDIM) for k in range(3)]
            queries, keys, values = (packed[i, :, c] for c in cols)
            probs, one = softmax_head(queries, keys, None, free, float(count))
            probs_out[i, h : h + 1, :free] = probs[free : free + 1]
            probs_out[i, h : h + 1, free:] = jnp.broadcast_to(one[free : free + 1], (1, TILE))
            mixture = dot(probs.astype(BF), values[:free])
            mixture = mixture + one.astype(BF).astype(F32) * values[free : free + 1].astype(F32)
            mixed[i * rows : (i + 1) * rows, cols[0]] = mixture.astype(BF)
        mix_out[i] = mixed[i * rows + free : (i + 1) * rows]
    copies[-1].wait()
    rows = packed.shape[1]
    for begin in range(0, partial[0].shape[1], 512):
        cols = slice(begin, begin + 512)
        part = out_weight[:, :, cols]
        added = dot(mixed[...], part.reshape(-1, 512)).astype(BF)
        for i in range(tp):
            partial[i][:, cols] = added[i * rows : (i + 1) * rows]


def write_out(tp, mixed, weight, partial):
    rows, width = partial[0].shape
    span = width // tp
    for t in range(tp):
        added = dot(mixed[...], block(weight, t, slice(3 * span, 4 * span))).astype(BF)
        for i in range(tp):
            partial[i][:, t * span : (t + 1) * span] = added[i * rows : (i + 1) * rows]


def masked_row(last, i, one_entry, one_row):
    last = last.astype(F32)
    one_entry[i : i + 1] = last[:1]
    one_row[i : i + 1] = last[1:2] + last[2:3] + last[3:4]


def cross_kernel(tp, local, *refs):
    entries, text = refs[:tp], refs[tp : 2 * tp]
    bias, gathered = refs[2 * tp : 2 * tp + 2]
    partial = refs[2 * tp + 2 : 3 * tp + 2]
    pair, query_out, mix_out, probs_out, one_entry, one_row = refs[3 * tp + 2 : 3 * tp + 8]
    weight, held, held_text, queries, mixed, sems = refs[3 * tp + 8 :]
    rows, txt, span = entries[0].shape[0], text[0].shape[0], local * HDIM
    free = rows - PAD
    pairs = [(ref, held_text.at[i * txt : (i + 1) * txt]) for i, ref in enumerate(text)]
    pairs += [(ref, held.at[i * rows : (i + 1) * rows]) for i, ref in enumerate(entries)]
    pairs += [(gathered, weight)]
    for copy in start_copies(pairs, sems):
        copy.wait()
    for k in range(2):
        cols = slice(k * span, (k + 1) * span)
        found = project(held_text[...], weight, cols).astype(BF)
        for i in range(tp):
            pair[i, :, cols] = found[i * txt : (i + 1) * txt]
    queries[...] = project(held[...], weight, slice(2 * span, 3 * span)).astype(BF)
    probs_out[...] = jnp.zeros_like(probs_out)
    for i in range(tp):
        masked_row(held[i * rows + free : (i + 1) * rows], i, one_entry, one_row)
        query_out[i] = queries[i * rows + free : (i + 1) * rows]
        for h in range(local):
            cols = slice(h * HDIM, (h + 1) * HDIM)
            keys = pair[i, :, cols]
            values = pair[i, :, span + h * HDIM : span + (h + 1) * HDIM]
            some = queries[i * rows : (i + 1) * rows, cols]
            probs, _ = softmax_head(some, keys, bias[i : i + 1], txt, 0)
            probs_out[i, h : h + 1] = probs[free : free + 1]
            mixed[i * rows : (i + 1) * rows, cols] = dot(probs.astype(BF), values).astype(BF)
        mix_out[i] = mixed[i * rows + free : (i + 1) * rows]
    write_out(tp, mixed, weight, partial)


def gelu_parts(value):
    slope = 0.7978845608
    bent = jnp.tanh(slope * (value + 0.044715 * value * value * value))
    half = 0.5 * (1.0 + bent)
    steep = slope * (1.0 + 3.0 * 0.044715 * value * value)
    return value * half, half + 0.5 * value * (1.0 - bent * bent) * steep


def up_kernel(tp, *refs):
    entries, (weight, active, held, sems) = refs[:tp], refs[tp:]
    rows = entries[0].shape[0]

    @pl.when(pl.program_id(0) == 0)
    def _():
        pairs = [(ref, held.at[i * rows : (i + 1) * rows]) for i, ref in enumerate(entries)]
        for copy in start_copies(pairs, sems):
            copy.wait()

    active[...] = gelu_parts(project(held[...], weight, slice(None)))[0].astype(BF)


def mlp_back_kernel(tp, *refs):
    entries_all, grad_active, gathered = refs[:tp], refs[tp], refs[tp + 1]
    active, grad_pre, grad_entry, one_entry, one_row, weight, last, entries, sem = refs[tp + 2 :]
    step, free = entries.shape[1] // tp, entries_all[0].shape[0] - PAD
    ends = [
        pltpu.make_async_copy(ref.at[free:], last.at[i], sem.at[tp + i])
        for i, ref in enumerate(entries_all)
    ]
    for copy in ends:
        copy.start()
    copies = [
        pltpu.make_async_copy(gathered.at[:, t], weight.at[:, t], sem.at[t]) for t in range(tp)
    ]
    for copy in copies:
        copy.start()
    for i, copy in enumerate(ends):
        copy.wait()
        masked_row(last[i], i, one_entry, one_row)
    entries[...] = jnp.zeros_like(entries)
    entries[:tp] = one_entry[...]
    hidden = jnp.zeros(active.shape, F32)
    for t, copy in enumerate(copies):
        copy.wait()
        rows = entries[:, t * step : (t + 1) * step].astype(BF)
        hidden = hidden + dot(rows, block(weight, t, slice(None)))
    value, steep = gelu_parts(hidden)
    active[...] = value.astype(BF)
    grad_pre[...] = (steep * grad_active[...]).astype(BF)
    for t in range(tp):
        back = dot_t(grad_pre[...], block(weight, t, slice(None)))
        grad_entry[:, t * step : (t + 1) * step] = back[:tp]


def summed(parts, i):
    total = parts[0][i : i + 1]
    for j in range(1, len(parts)):
        total = total + parts[j][i ^ j : (i ^ j) + 1]
    return total


def out_back(rows, weights, columns):
    tp = weights.shape[1]
    step = rows.shape[1] // tp
    total = dot_t(rows[:, :step], block(weights, 0, columns))
    for t in range(1, tp):
        total = total + dot_t(rows[:, t * step : (t + 1) * step], block(weights, t, columns))
    return total.astype(BF).astype(F32)


def head_mask(span):
    heads = lax.broadcasted_iota(jnp.int32, (8, span), 0)
    return lax.broadcasted_iota(jnp.int32, (8, span), 1) // HDIM == heads


def row_back(parts, rows, gain, base, i, out, gain_row):
    grad = summed(parts, i)
    field, scale = normed(rows[i : i + 1])
    out[i : i + 1] = base[i : i + 1] + norm_back(grad * gain[...], field, scale)
    if i == 0:
        gain_row[...] = grad * field


def cross_back_kernel(
    tp, base, rows, gain, pair, probs, gathered, *refs,
):
    parts = refs[:tp]
    grad_mid, grad_cmix, scores, grad_cq, grad_entry, gain_row = refs[tp : tp + 6]
    weight, held, sems = refs[tp + 6 :]
    span = weight.shape[3] // 2
    copies = [
        pltpu.make_async_copy(gathered.at[:, :, :, 2 * span :], weight, sems.at[0]),
    ]
    for copy in copies:
        copy.start()
    held[...] = jnp.zeros_like(held)
    for i in range(tp):
        row_back(parts, rows, gain, base, i, held, gain_row)
    grad_mid[...] = held[:tp]
    copies[0].wait()
    mixed = out_back(held[...].astype(BF), weight, slice(span, 2 * span))
    grad_cmix[...] = mixed[:tp]
    mask = head_mask(span)
    held[...] = jnp.zeros_like(held)
    for i in range(tp):
        spread = jnp.where(mask, mixed[i : i + 1], 0.0).astype(BF)
        grad_probs = dot_t(spread, pair[i, :, span:])
        weighs = probs[i]
        grad = weighs * (grad_probs - jnp.sum(grad_probs * weighs, axis=-1, keepdims=True))
        grad = grad.astype(BF)
        scores[i] = grad.astype(F32)
        back = jnp.where(mask, dot(grad, pair[i, :, :span]), 0.0)
        held[i : i + 1, :span] = jnp.sum(back, axis=0, keepdims=True) * HDIM ** (-0.5)
    grad_cq[...] = held[:tp, :span]
    queries = held[:, :span].astype(BF)
    step = grad_entry.shape[1] // tp
    for t in range(tp):
        back = dot_t(queries, block(weight, t, slice(0, span)))
        grad_entry[:, t * step : (t + 1) * step] = back[:tp]


def spread_heads(rows, i, spreads, mask):
    spreads[8 * i : 8 * i + 8] = jnp.where(mask, rows, 0.0)


def text_back_kernel(tp, local, *refs):
    scores, probs, query_one, grad_cmix, kvq = refs[:5]
    cross_one_row, mlp_one, grad_pre, grad_cq, mixed, cross, active, grad_mid = refs[5:13]
    text = refs[13 : 13 + tp]
    sent = refs[13 + tp : 13 + 2 * tp]
    lefts, factors, weight, held, keys, values, sems = refs[13 + 2 * tp :]
    span, width, txt = grad_cmix.shape[1], lefts.shape[1], scores.shape[2]
    copy = pltpu.make_async_copy(kvq.at[:, :, :, : 2 * span], weight, sems.at[0])
    copy.start()
    mask = head_mask(span)
    ff = grad_pre.shape[1]
    places, at = [], 0
    for size in (ff, span, span, span, span, span, ff, width):
        places.append(slice(at, at + size))
        at += size
    for i in range(tp):
        spread_heads(query_one[i].astype(F32)[:1], i, keys, mask)
        spread_heads(grad_cmix[i : i + 1], i, values, mask)
        both = jnp.concatenate([scores[i], probs[i]], axis=0).astype(BF)
        found = dot(both, text[i][...])
        for kind in range(2):
            begin = (2 * i + kind) * local
            lefts[begin : begin + local] = found[8 * kind : 8 * kind + local]
        sent[i][:, width:] = both
        for k, rows in ((2, query_one), (4, mixed), (5, cross)):
            held[i : i + 1, places[k]] = rows[i].astype(F32)[:1]
    held[:tp, places[0]] = grad_pre[...].astype(F32)[:tp]
    held[:tp, places[1]] = grad_cq[...]
    held[:tp, places[3]] = grad_cmix[...]
    held[:tp, places[6]] = active[...].astype(F32)[:tp]
    held[:tp, places[7]] = grad_mid[...]
    factors[...] = held[:tp].astype(BF)
    begin = 2 * tp * local
    lefts[begin : begin + tp] = cross_one_row[...]
    lefts[begin + tp :] = mlp_one[...]
    copy.wait()
    step = width // tp
    key_spread, value_spread = keys[...].astype(BF), values[...].astype(BF)
    for t in range(tp):
        cols = slice(t * step, (t + 1) * step)
        key_rows = dot_t(key_spread, block(weight, t, slice(0, span))) * HDIM ** (-0.5)
        value_rows = dot_t(value_spread, block(weight, t, slice(span, 2 * span)))
        for i in range(tp):
            eight = slice(8 * i, 8 * i + 8)
            both = jnp.concatenate([key_rows[eight], value_rows[eight]], axis=0)
            sent[i][:, cols] = both.astype(BF)


def self_back_kernel(
    tp, local, base, rows, gain, packed, probs, masked_entries, text_lefts, text_factors,
    gain_a, embed, gain_m_row, gathered, out_w, *refs,
):
    parts, entries, text_sent = refs[:tp], refs[tp : 2 * tp], refs[2 * tp : 3 * tp]
    sent, refs = refs[3 * tp : 4 * tp], refs[4 * tp :]
    payload, factors, weight, out_weight, held, spreads, lefts, small, sems = refs
    width = lefts.shape[1]
    span, free = weight.shape[3] // 3, entries[0].shape[0]
    copies = start_copies([(out_w, out_weight), (gathered, weight)], sems)
    ff = (text_factors.shape[1] - 5 * span - width) // 2
    cut = ff + 3 * span
    factors[:, :cut] = text_factors[:, :cut]
    factors[:, cut + 2 * span : -width] = text_factors[:, cut:]
    small[...] = jnp.zeros_like(small)
    small[3:4] = gain_m_row[...]
    held[...] = jnp.zeros_like(held)
    for i in range(tp):
        row_back(parts, rows, gain, base, i, held, small.at[2:3])
    small[0:1] = held[0:1]
    factors[:, -width:] = held[:tp].astype(BF)
    copies[0].wait()
    part = out_weight[...]
    mixed = dot_t(held[...].astype(BF), part.reshape(span, width)).astype(BF).astype(F32)
    factors[:, cut : cut + span] = mixed[:tp].astype(BF)
    mask = head_mask(span)
    held[...] = jnp.zeros_like(held)
    masked_row = masked_entries[:1].astype(F32)
    ones = []
    for i in range(tp):
        spread = jnp.where(mask, mixed[i : i + 1], 0.0)
        spreads[8 * i : 8 * i + 8] = spread
        spread = spread.astype(BF)
        values = packed[i, :, 2 * span :]
        grad_probs, grad_one = dot_t(spread, values[:free]), dot_t(spread, values[free:])[:, :1]
        weighs, one = probs[i, :, :free], probs[i, :, free : free + 1]
        mean = jnp.sum(grad_probs * weighs, axis=-1, keepdims=True) + grad_one * one
        grad = (weighs * (grad_probs - mean)).astype(BF)
        grad_one = (one * (grad_one - mean)).astype(BF).astype(F32)
        ones.append((grad_one, one))
        keys = packed[i, :, span : 2 * span]
        back = dot(grad, keys[:free]) + grad_one * keys[free : free + 1].astype(F32)
        back = jnp.sum(jnp.where(mask, back, 0.0), axis=0, keepdims=True)
        held[i : i + 1, :span] = back * HDIM ** (-0.5)
        both = jnp.concatenate([grad.astype(F32), weighs], axis=0).astype(BF)
        both_one = jnp.concatenate([grad_one, one], axis=0).astype(BF).astype(F32)
        found = dot(both, entries[i][...]) + both_one * masked_row
        for kind in range(2):
            begin = (2 * i + kind) * local
            lefts[begin : begin + local] = found[8 * kind : 8 * kind + local]
        sent[i][:PAD, width:] = both
        sent[i][PAD:] = text_sent[i][...]
    factors[:, cut + span : cut + 2 * span] = held[:tp, :span].astype(BF)
    queries = held[:, :span].astype(BF)
    zero_query = packed[0, free:, :span].astype(F32)[:1]
    key_spread = jnp.where(mask, zero_query, 0.0).astype(BF)
    value_spread = spreads[...].astype(BF)
    step = width // tp
    field, scale = normed(embed[...])
    copies[1].wait()
    for t in range(tp):
        cols = slice(t * step, (t + 1) * step)
        keys = dot_t(key_spread, block(weight, t, slice(span, 2 * span))) * HDIM ** (-0.5)
        values = dot_t(value_spread, block(weight, t, slice(2 * span, 3 * span)))
        query_rows = dot_t(queries, block(weight, t, slice(0, span)))
        masked_grad, gain_grad = 0.0, 0.0
        for i in range(tp):
            mine = values[8 * i : 8 * i + 8]
            sent[i][:PAD, cols] = jnp.concatenate([keys, mine], axis=0).astype(BF)
            last = query_rows[i : i + 1]
            found = ones[i][0] * keys + ones[i][1] * mine
            masked_grad = masked_grad + last + jnp.sum(found, axis=0, keepdims=True)
            for kind, rows_back in enumerate((keys, mine)):
                begin = (2 * i + kind) * local
                found = lefts[begin : begin + local, cols] * rows_back[:local]
                gain_grad = gain_grad + jnp.sum(found, axis=0, keepdims=True)
        gain_grad = gain_grad / gain_a[:, cols]
        rows_sum = jnp.sum(query_rows[:tp], axis=0, keepdims=True)
        small[1:2, cols] = gain_grad + rows_sum * field[:, cols]
        held[0:1, cols] = masked_grad
    small[0:1] = small[0:1] + norm_back(held[0:1] * gain_a[...], field, scale)
    begin = 2 * tp * local
    lefts[begin : begin + text_lefts.shape[0]] = text_lefts[...]
    begin += text_lefts.shape[0]
    high = small[:4].astype(BF).astype(F32)
    lefts[begin : begin + 4] = high
    lefts[begin + 4 : begin + 8] = small[:4] - high
    half, own = lefts.shape[0] // 2, payload.shape[2] // 2
    for d in range(payload.shape[0]):
        cols = slice(d * own, (d + 1) * own)
        both = jnp.concatenate([lefts[:half, cols], lefts[half:, cols]], axis=1)
        payload[d] = both.astype(BF)


def tokens_back_kernel(tp, rows, gain, place, *refs):
    came, (tokens, text) = refs[:tp], refs[tp:]
    width, free = rows.shape[1], place.shape[1]
    grad, grad_text = 0.0, 0.0
    for part in came:
        grad = grad + dot_sum(part[:PAD, width:], part[:PAD, :width])
        grad_text = grad_text + dot_sum(part[PAD:, width:], part[PAD:, :width])
    text[...] = grad_text.astype(BF)
    field, scale = normed(rows[:free])
    start = norm_back(grad * gain[...], field, scale)
    tokens[...] = dot(place[...], start.astype(BF)).astype(BF)


def stack_kernel(*refs):
    for k, ref in enumerate(refs[:-1]):
        refs[-1][k] = ref[...]


def unpack_kernel(local, planes, others, query, right, group, held):
    count, tp = planes.shape[:2]
    for k in range(count):
        held[k * tp : (k + 1) * tp] = planes[k].astype(F32)
        held[(count + k) * tp : (count + k + 1) * tp] = others[k].astype(F32)
    cut, span = right.shape[1] - TILE, local * HDIM
    right[:, :cut] = held[:, :cut].astype(BF)
    total = jnp.sum(held[:, cut : cut + span], axis=0, keepdims=True)
    group[...] = held[:, cut + span :].astype(BF)
    held[:, :TILE] = jnp.zeros((held.shape[0], TILE), F32)
    for h in range(local):
        cols = slice(h * HDIM, (h + 1) * HDIM)
        held[h : h + 1, :TILE] = total[:, cols]
        held[local + h : local + h + 1, :TILE] = query[:1, cols].astype(F32)
    right[:, cut:] = held[:, :TILE].astype(BF)


def aligned(right, corner, tp):
    count = right.shape[0]
    out = lax.broadcasted_iota(jnp.int32, (count, count), 0)
    into = lax.broadcasted_iota(jnp.int32, (count, count), 1)
    same = (out // tp == (corner ^ (into // tp))) & (out % tp == into % tp)
    return dot(same.astype(BF), right).astype(BF)


def columns_kernel(local, place, attn_left, text_left, one_left, entry, *refs):
    right, (grad_qkv, grad_kv, grad_cq, grad_up) = refs[:-4], refs[-4:]
    tp, span = len(right), local * HDIM
    ff = right[0].shape[1] - 4 * span - TILE
    ones = jnp.ones((right[0].shape[0], HDIM), BF)
    scale = HDIM ** (-0.5)

    def at_columns(begin, size):
        return pl.ds(pl.multiple_of(begin, HDIM), size)

    for j in range(tp):
        at = place[0] ^ j
        rows = aligned(right[j][:, : ff + 4 * span], place[1], tp)
        part = [rows[:, ff + k * span : ff + (k + 1) * span] for k in range(4)]
        extra = right[j][:, ff + 4 * span :].astype(F32)
        grad_up[:, at_columns(at * ff, ff)] = dot_sum(one_left[at, 1], rows[:, :ff])
        grad_cq[:, at_columns(at * span, span)] = dot_sum(one_left[at, 0], part[0])
        for h in range(local):
            cols = slice(h * HDIM, (h + 1) * HDIM)
            begin = at * span + h * HDIM
            outer = dot_sum(text_left[at, 0, h], part[1][:, cols])
            grad_kv[:, at_columns(begin, HDIM)] = outer * scale
            outer = dot_sum(text_left[at, 1, h], part[2][:, cols])
            grad_kv[:, at_columns(tp * span + begin, HDIM)] = outer
            grad_qkv[:, at_columns(begin, HDIM)] = entry[...] * extra[h : h + 1]
            outer = dot_sum(attn_left[at, 0, h], ones) * (extra[local + h : local + h + 1] * scale)
            grad_qkv[:, at_columns(tp * span + begin, HDIM)] = outer
            outer = dot_sum(attn_left[at, 1, h], part[3][:, cols])
            grad_qkv[:, at_columns(2 * tp * span + begin, HDIM)] = outer


def whole_spec():
    return pl.BlockSpec(memory_space=pl.ANY)


def in_vmem(kernel, name, operands, out_shape, scratch_shapes=(), held=()):
    spaces = dict(held)
    return pl.pallas_call(
        kernel,
        in_specs=[
            pl.BlockSpec(memory_space=spaces.get(k, pltpu.VMEM)) for k in range(len(operands))
        ],
        out_specs=[pl.BlockSpec(memory_space=pltpu.VMEM)] * len(out_shape),
        out_shape=[jax.ShapeDtypeStruct(shape, dtype) for shape, dtype in out_shape],
        scratch_shapes=scratch_shapes,
        compiler_params=pltpu.CompilerParams(vmem_limit_bytes=VMEM_BYTES),
        cost_estimate=COST,
        name=name,
    )(*operands)


def self_forward(local, count, entries, masked_entries, gathered, out_w):
    tp, (free, width) = len(entries), entries[0].shape
    span, rows = local * HDIM, free + PAD
    found = in_vmem(
        functools.partial(self_kernel, tp, local, count),
        "self_attention",
        [*entries, masked_entries, gathered, out_w],
        [((rows, width), BF)] * tp
        + [((tp, rows, 3 * span), BF), ((tp, PAD, span), BF), ((tp, 8, free + TILE), F32)],
        [
            pltpu.VMEM(gathered.shape, BF),
            pltpu.VMEM(out_w.shape, BF),
            pltpu.VMEM((tp * free + PAD, width), BF),
            pltpu.VMEM((tp * rows, span), BF),
            pltpu.SemaphoreType.DMA((tp + 3,)),
        ],
        [(k, pl.ANY) for k in range(tp + 3)],
    )
    return found[:tp], *found[tp:]


def cross_forward(local, entries, text, bias, gathered):
    tp, (rows, width) = len(entries), entries[0].shape
    txt, span = text[0].shape[0], local * HDIM
    found = in_vmem(
        functools.partial(cross_kernel, tp, local),
        "cross_attention",
        [*entries, *text, bias, gathered],
        [((rows, width), BF)] * tp
        + [
            ((tp, txt, 2 * span), BF),
            ((tp, PAD, span), BF),
            ((tp, PAD, span), BF),
            ((tp, 8, txt), F32),
            ((tp, width), F32),
            ((tp, width), F32),
        ],
        [
            pltpu.VMEM(gathered.shape, BF),
            pltpu.VMEM((tp * rows, width), BF),
            pltpu.VMEM((tp * txt, width), BF),
            pltpu.VMEM((tp * rows, span), BF),
            pltpu.VMEM((tp * rows, span), BF),
            pltpu.SemaphoreType.DMA((2 * tp + 1,)),
        ],
        [(k, pl.ANY) for k in range(2 * tp + 2) if k != 2 * tp],
    )
    return found[:tp], *found[tp:]


def down_kernel(tp, active, gathered, *refs):
    partial, (weight, sems) = refs[:tp], refs[tp:]
    rows, width = partial[0].shape
    step = min(512, width)
    parts = [slice(at, at + step) for at in range(0, width, step)]
    copies = start_copies([(gathered.at[:, :, cols], weight.at[:, :, cols]) for cols in parts], sems)
    for cols, copy in zip(parts, copies):
        copy.wait()
        part = weight[:, :, cols]
        added = dot(active[...], part.reshape(-1, step)).astype(BF)
        for i in range(tp):
            partial[i][:, cols] = added[i * rows : (i + 1) * rows]


def mlp_down(tp, active, gathered):
    rows, width = active.shape[0] // tp, gathered.shape[2]
    return in_vmem(
        functools.partial(down_kernel, tp),
        "mlp_down",
        [active, gathered],
        [((rows, width), BF)] * tp,
        [pltpu.VMEM(gathered.shape, BF), pltpu.SemaphoreType.DMA((width // min(512, width),))],
        ((1, pl.ANY),),
    )


def mlp_up(entries, gathered):
    tp, (rows, width) = len(entries), entries[0].shape
    blocks, _, own, ff = gathered.shape
    step = min(ff, 512)
    return pl.pallas_call(
        functools.partial(up_kernel, tp),
        grid=(ff // step,),
        in_specs=[whole_spec()] * tp
        + [pl.BlockSpec((blocks, tp, own, step), lambda i: (0, 0, 0, i))],
        out_specs=pl.BlockSpec((tp * rows, step), lambda i: (0, i)),
        out_shape=jax.ShapeDtypeStruct((tp * rows, ff), BF),
        scratch_shapes=[
            pltpu.VMEM((tp * rows, width), BF),
            pltpu.SemaphoreType.DMA((tp,)),
        ],
        compiler_params=pltpu.CompilerParams(vmem_limit_bytes=VMEM_BYTES),
        cost_estimate=COST,
        name="mlp_up",
    )(*entries, gathered)


def mlp_back(entries, grad_active, gathered):
    tp, width = len(entries), entries[0].shape[1]
    ff = gathered.shape[3]
    return in_vmem(
        functools.partial(mlp_back_kernel, tp),
        "mlp_back",
        [*entries, grad_active, gathered],
        [
            ((PAD, ff), BF),
            ((PAD, ff), BF),
            ((tp, width), F32),
            ((tp, width), F32),
            ((tp, width), F32),
        ],
        [
            pltpu.VMEM(gathered.shape, BF),
            pltpu.VMEM((tp, PAD, width), BF),
            pltpu.VMEM((PAD, width), F32),
            pltpu.SemaphoreType.DMA((2 * tp,)),
        ],
        [(k, pl.ANY) for k in range(tp + 2) if k != tp],
    )


def cross_back(base, rows, gain, pair, probs, gathered, parts):
    tp, width = base.shape
    blocks, _, own, columns = gathered.shape
    span = columns // 4
    return in_vmem(
        functools.partial(cross_back_kernel, tp),
        "cross_back",
        [base, rows, gain[None], pair, probs, gathered, *parts],
        [
            ((tp, width), F32),
            ((tp, span), F32),
            (probs.shape, F32),
            ((tp, span), F32),
            ((tp, width), F32),
            ((1, width), F32),
        ],
        [
            pltpu.VMEM((blocks, tp, own, 2 * span), BF),
            pltpu.VMEM((8, width), F32),
            pltpu.SemaphoreType.DMA((1,)),
        ],
        ((5, pl.ANY),),
    )


def text_back(local, scores, probs, query_one, grad_cmix, kvq, rest, text):
    tp, span = grad_cmix.shape
    blocks, _, own, _ = kvq.shape
    (txt, width), ff = text[0].shape, rest[2].shape[1]
    found = in_vmem(
        functools.partial(text_back_kernel, tp, local),
        "text_back",
        [scores, probs, query_one, grad_cmix, kvq, *rest, *text],
        [((PAD, width + txt), BF)] * tp
        + [((2 * tp * (local + 1), width), F32), ((tp, 2 * ff + 5 * span + width), BF)],
        [
            pltpu.VMEM((blocks, tp, own, 2 * span), BF),
            pltpu.VMEM((8, 2 * ff + 5 * span + width), F32),
            pltpu.VMEM((8 * tp, span), F32),
            pltpu.VMEM((8 * tp, span), F32),
            pltpu.SemaphoreType.DMA((1,)),
        ],
        ((4, pl.ANY),),
    )
    return found[:tp], *found[tp:]


def self_back(local, world, small_operands, gathered, out_w, parts, entries, text_sent):
    tp, width = small_operands[0].shape
    text_lefts, text_factors = small_operands[6], small_operands[7]
    _, _, own, columns = gathered.shape
    span, free = columns // 3, entries[0].shape[0]
    count = 2 * tp * local + text_lefts.shape[0] + 8
    operands = [*small_operands, gathered, out_w, *parts, *entries, *text_sent]
    found = in_vmem(
        functools.partial(self_back_kernel, tp, local),
        "self_back",
        operands,
        [((2 * PAD, width + free), BF)] * tp
        + [((world, count // 2, 2 * own), BF), ((tp, text_factors.shape[1] + 2 * span + width), BF)],
        [
            pltpu.VMEM(gathered.shape, BF),
            pltpu.VMEM(out_w.shape, BF),
            pltpu.VMEM((8, width), F32),
            pltpu.VMEM((8 * tp, span), F32),
            pltpu.VMEM((count, width), F32),
            pltpu.VMEM((8, width), F32),
            pltpu.SemaphoreType.DMA((2,)),
        ],
        [(len(small_operands) + k, pl.ANY) for k in range(2)],
    )
    return found[:tp], *found[tp:]


def stacked(pieces):
    shape = (len(pieces),) + pieces[0].shape
    return in_vmem(stack_kernel, "stack", pieces, [(shape, BF)])[0]


def unpack(local, planes, others, query, cut):
    count, tp, wide = planes.shape
    span = local * HDIM
    rows = 2 * count * tp
    return in_vmem(
        functools.partial(unpack_kernel, local),
        "unpack",
        [planes, others, query],
        [((rows, cut + TILE), BF), ((rows, wide - cut - span), BF)],
        [pltpu.VMEM((rows, wide), F32)],
    )


def join_kernel(free, base, gain, *refs):
    parts, (total, entries) = refs[:-2], refs[-2:]
    value = base[...]
    for part in parts:
        value = value + part[...].astype(F32)
    total[...] = value
    found = normed(value)[0] * gain[...]
    entries[...] = found.astype(BF)

    @pl.when(pl.program_id(0) == pl.num_programs(0) - 1)
    def _():
        at = value.shape[0] - PAD
        row = value[at : at + 1]
        spot = lax.broadcasted_iota(jnp.int32, (PAD, value.shape[1]), 0)
        last = found[at:]
        for k in range(3):
            part = row.astype(BF).astype(F32)
            last = jnp.where(spot == k + 1, part, last)
            row = row - part
        entries[at:] = last.astype(BF)


def join(base, parts, gain):
    rows, width = base.shape
    step = PAD * 3 if rows % (PAD * 3) == 0 else PAD
    block = pl.BlockSpec((step, width), lambda i: (i, 0))
    return pl.pallas_call(
        functools.partial(join_kernel, rows - PAD),
        grid=(rows // step,),
        in_specs=[block, pl.BlockSpec((1, width), lambda i: (0, 0))] + [block] * len(parts),
        out_specs=[block, block],
        out_shape=[
            jax.ShapeDtypeStruct((rows, width), F32),
            jax.ShapeDtypeStruct((rows, width), BF),
        ],
        compiler_params=pltpu.CompilerParams(vmem_limit_bytes=VMEM_BYTES),
        cost_estimate=COST,
        name="join",
    )(base, gain[None], *parts)


def shards(
    tp,
    planes,
    tokens,
    text,
    cotangent,
    positions,
    text_lengths,
    mask_embed,
    gain_attn,
    w_qkv,
    w_attn_out,
    gain_cross,
    w_cross_q,
    w_cross_kv,
    w_cross_out,
    gain_mlp,
    w_up,
    w_down,
):
    me = Layer(tp, planes)
    seq, width = tokens.shape
    masked_count = positions.shape[1]
    free = seq - masked_count
    txt = text.shape[1]
    local = HEADS // tp
    rows = free + PAD
    device = (me.t * 2 + me.c) * planes + me.z
    world = tp * 2 * planes
    own = width // world

    def after(value, earlier):
        return lax.optimization_barrier((value, earlier))[0]

    span = local * HDIM

    out_w = me.gather_blocks(w_attn_out)
    corner = me.c * planes + me.z
    place_at = jnp.stack([me.t, corner]).astype(jnp.int32)
    in_smem = ((0, pltpu.SMEM),)
    parts = in_vmem(
        functools.partial(parts_kernel, tp, 3),
        "parts",
        [place_at, w_qkv],
        [((own, 3 * span), BF)] * tp,
        held=in_smem,
    )
    attn_sent = in_vmem(
        functools.partial(assemble_kernel, tp),
        "assemble",
        [place_at, *me.to_owner(parts)],
        [((tp, own, 3 * span), BF)],
        held=in_smem,
    )[0]

    cot_sum = jnp.sum(cotangent[0].astype(F32), axis=0)
    vectors = jnp.concatenate([mask_embed, gain_attn, gain_cross, gain_mlp]).astype(F32)
    fill = TILE - vectors.shape[0] % TILE
    length = jnp.broadcast_to(text_lengths.astype(F32), (fill,))
    gathered = after(jnp.concatenate([cot_sum, vectors, length]), attn_sent)
    by_plane = me.gather_cz(gathered)
    gathered = me.tp_direct(by_plane)
    others = after((w_cross_kv, w_cross_q, w_cross_out), (gathered, attn_sent))
    kvq_sent = me.shuffle([(others[0], 2), (others[1], 1)])
    cross_sent = jnp.concatenate([kvq_sent, column_blocks(tp, [(others[2], 1)])], axis=2)
    attn_w = me.gather_blocks(after(attn_sent, (out_w, by_plane)))
    vectors = gathered[:, :, width : width + 4 * own].reshape(world, 4, own)
    vectors = xor_order(vectors, device, world).transpose(1, 0, 2).reshape(4, width)
    embed, gain_a, gain_c, gain_m = vectors[0], vectors[1], vectors[2], vectors[3]
    lengths = gathered[:, 0, width + 4 * own :][:, :1]
    text_bias = jnp.where(
        lax.broadcasted_iota(jnp.int32, (tp, txt), 1).astype(F32) < lengths, 0.0, -1e30
    )
    cot_group = gathered[:, 0, :width]

    spots = lax.broadcasted_iota(jnp.int32, (masked_count, seq), 1)
    masked = jnp.sum((positions[0][:, None] == spots).astype(F32), axis=0)
    below = lax.broadcasted_iota(jnp.int32, (seq, seq), 0) <= lax.broadcasted_iota(
        jnp.int32, (seq, seq), 1
    )
    rank = dot((1.0 - masked).astype(BF)[None, :], below.astype(BF))[0]
    ranks = lax.broadcasted_iota(jnp.int32, (free, seq), 0).astype(F32) + 1.0
    pick = ((rank[None, :] == ranks) & (masked[None, :] == 0.0)).astype(BF)
    place = jnp.concatenate(
        [pick.T, masked[:, None].astype(BF), jnp.zeros((seq, PAD - 1), BF)], axis=1
    )
    start_free = dot(pick, tokens)
    start = jnp.concatenate([start_free, jnp.broadcast_to(embed[None], (PAD, width))])

    cot_rows = gathered[:, :, :width].reshape(world, width)
    high = cot_rows.astype(BF)
    low = (cot_rows - high.astype(F32)).astype(BF)
    through = dot_t(jnp.concatenate([high, low]), w_down)
    through = through[:world] + through[world:]
    through = through.reshape(tp, 2 * planes, -1).transpose(1, 0, 2)
    through = xor_order(through, me.c * planes + me.z, 2 * planes)
    through = lax.all_to_all(after(through, kvq_sent), ("core", "fsdp"), 0, 0, tiled=True)
    grad_active = through.transpose(1, 0, 2).reshape(tp, -1)

    field_a, scale_a = normed(start)
    entries = (field_a * gain_a[None]).astype(BF)
    masked_entries = entries[free:]
    entries_all = me.spread(entries[:free])
    text_rows = me.spread(after(text[0], entries_all))
    up_sent = me.shuffle([(after(w_up, (entries_all, kvq_sent)), 1)])
    cross_w = me.gather_blocks(after(cross_sent, (attn_w, entries_all, up_sent, place, masked_entries, text_bias)))
    partial, packed, mixed_one, probs_one = self_forward(
        local, masked_count, entries_all, masked_entries, attn_w, out_w
    )
    after_attn, cross_entries = join(after(start, (grad_active, place)), me.collect(after(tuple(partial), text_rows)), gain_c)

    cross_all = me.spread(cross_entries)
    up = me.gather_blocks(after(up_sent, (cross_w, cross_all)))
    partial, pair, query_one, cross_one, cross_probs_one, cross_entry, attn_stream = cross_forward(
        local, cross_all, text_rows, text_bias, cross_w
    )
    after_cross, mlp_entries = join(after_attn, me.collect(partial), gain_m)

    mlp_all = me.spread(mlp_entries)
    most = width * 3 // 4
    down = me.gather_blocks(after(w_down[:, :most], (up, mlp_all)))

    active_one, grad_pre, grad_entry, mlp_one, cross_stream = mlp_back(
        mlp_all, jnp.pad(grad_active, ((0, PAD - tp), (0, 0))), up
    )
    grad_mid, grad_cmix, scores, grad_cq, grad_entry, grad_gain_m = cross_back(
        cot_group, cross_stream, gain_m, pair, cross_probs_one, cross_w, me.tp_parts(grad_entry)
    )
    text_sent, text_lefts, text_factors = text_back(
        local,
        scores,
        cross_probs_one,
        query_one,
        grad_cmix,
        cross_w,
        [
            cross_entry,
            mlp_one,
            grad_pre,
            grad_cq,
            mixed_one,
            cross_one,
            active_one,
            grad_mid,
        ],
        text_rows,
    )
    sent, payload, factors = self_back(
        local,
        world,
        [
            grad_mid,
            attn_stream,
            gain_c[None],
            packed,
            probs_one,
            masked_entries,
            text_lefts,
            text_factors,
            gain_a[None],
            embed[None],
            grad_gain_m,
        ],
        attn_w,
        out_w,
        me.tp_parts(grad_entry),
        entries_all,
        text_sent,
    )
    came = me.to_owner(sent)

    ff = grad_pre.shape[1]
    active = mlp_up(after(tuple(mlp_all), payload), up)
    pieces = [factors] + [me.other_plane(factors, k) for k in range(1, planes)]
    planes_of = stacked(after(tuple(pieces), (active, came)))
    lefts = me.to_rows(after(payload, planes_of))
    right, group = unpack(
        local, planes_of, me.other_core(planes_of), packed[0, free:, :span], ff + 4 * span
    )
    right = [right] + [me.hop(right, j) for j in range(1, tp)]

    active, _ = lax.optimization_barrier((active, right[0]))
    down_rest = me.gather_blocks(after(w_down[:, most:], (down, active)))
    partial = mlp_down(tp, active, down)
    collected = me.collect(partial)
    active = after(active, tuple(partial))

    grad_tokens, grad_text = in_vmem(
        functools.partial(tokens_back_kernel, tp),
        "tokens_back",
        [start, gain_a[None], pick.T, *after(tuple(came), partial)],
        [((seq, width), BF), ((txt, width), BF)],
    )

    partial = mlp_down(tp, after(active, grad_tokens), down_rest)
    collected_rest = me.collect(partial)

    heads = 2 * tp * local
    lefts = after(lefts, partial)
    lefts = jnp.concatenate([lefts[:, :, :own], lefts[:, :, own:]], axis=1)
    attn_left, text_left = (
        lefts[:, k * heads : (k + 1) * heads]
        .reshape(tp, 2 * planes, tp, 2, local, own)
        .transpose(0, 3, 4, 1, 2, 5)
        .reshape(tp, 2, local, world, own)
        for k in range(2)
    )
    one_left = lefts[:, 2 * heads : 2 * heads + 2 * tp].reshape(tp, 2 * planes, 2, tp, own)
    one_left = one_left.transpose(0, 2, 1, 3, 4).reshape(tp, 2, world, own)
    small = jnp.sum(lefts[:, 2 * heads + 2 * tp :].astype(F32), axis=0)
    small = small[:4] + small[4:]
    entry_own = lax.dynamic_slice_in_dim(entries[free], device * own, own).astype(F32)
    grad_w_qkv, grad_w_kv, grad_w_cq, grad_w_up = in_vmem(
        functools.partial(columns_kernel, local),
        "columns",
        [place_at, attn_left, text_left, one_left, entry_own[:, None], *right],
        [((own, 3 * width), F32), ((own, 2 * width), F32), ((own, width), F32), ((own, tp * ff), F32)],
        held=in_smem,
    )

    def mine(stack):
        size = stack.shape[1] // (2 * planes)
        return lax.dynamic_slice_in_dim(stack, corner * size, size, axis=1)

    group = after(group, partial)
    cuts = [span, 2 * span, 2 * span + ff, 2 * span + ff + width]
    mixed_f, cross_f, active_f, mid_f, attn_f = jnp.split(group, cuts, axis=1)
    cot_f = gathered[:, :, :width].astype(BF).swapaxes(0, 1).reshape(world, width)
    grad_w_out = dot_sum(mine(mixed_f), attn_f)
    grad_w_cout = dot_sum(mine(cross_f), mid_f)
    grad_w_down = dot_sum(mine(active_f), cot_f)
    collected_rest = after(tuple(collected_rest), (grad_w_qkv, grad_w_out, grad_w_cout, grad_w_down, small))
    output = [sum(p.astype(F32) for p in parts) for parts in (collected, collected_rest)]
    output = after_cross + jnp.concatenate(output, axis=1)
    output = dot(place, output.astype(BF)).astype(BF)
    return (
        output,
        grad_tokens,
        grad_text[None],
        small[0],
        small[1],
        grad_w_qkv,
        grad_w_out,
        small[2],
        grad_w_cq,
        grad_w_kv,
        grad_w_cout,
        small[3],
        grad_w_up,
        grad_w_down,
    )


def solution(mesh):
    tp, planes = mesh.shape["dp"] // 2, mesh.shape["fsdp"]
    fine = Mesh(mesh.devices.reshape(tp, 2, planes), ("tp", "core", "fsdp"))
    every = ("tp", "core", "fsdp")
    one, two, three = P(every), P(every, None), P(every, None, None)

    def layer(*arguments):
        return shards(tp, planes, *arguments)

    return jax.shard_map(
        layer,
        mesh=fine,
        in_specs=(two, three, three, two, one, one, one, two, two, one, two, two, two, one, two, two),
        out_specs=(two, two, three, one, one, two, two, one, two, two, two, one, two, two),
        check_vma=False,
    )
```
